128 devices in a mesh: row: 16 (over z, y_hi, core), col: 8 (over y_lo, x).
Axes of the slice: x: 4, y: 4 (y_hi: 2, y_lo: 2; y = y_hi * 2 + y_lo), z: 4, core: 2. Of those that a mesh axis runs over, the one named last changes fastest.
Arguments:
- tokens: bfloat16 [16384, 2048], P('row', 'col')
- segment_ids: int32 [16384], replicated, may hold values from 0 to 23, as said below
- norm_one: bfloat16 [2048], replicated, may hold values from 0.5 to 1.5
- w_query: bfloat16 [2048, 2048], P('row', 'col'), may hold values from -0.125 to 0.125
- w_key: bfloat16 [2048, 256], replicated, may hold values from -0.125 to 0.125
- w_value: bfloat16 [2048, 256], replicated, may hold values from -0.125 to 0.125
- w_out: bfloat16 [2048, 2048], P('col', 'row'), may hold values from -0.75 to 0.75
- norm_two: bfloat16 [2048], replicated, may hold values from 0.5 to 1.5
- w_gate: bfloat16 [2048, 5632], P('row', 'col'), may hold values from -0.125 to 0.125
- w_up: bfloat16 [2048, 5632], P('row', 'col'), may hold values from -0.125 to 0.125
- w_down: bfloat16 [5632, 2048], P('col', 'row'), may hold values from -0.15625 to 0.15625
- cotangent: bfloat16 [16384, 2048], P('row', 'col'), may hold values from -6 to 6
Outputs:
- mixed: bfloat16 [16384, 2048], P('row', 'col')
- input_grad: float32 [16384, 2048], P('row', 'col')
- query_grad: float32 [2048, 2048], P('row', 'col')
- key_grad: float32 [2048, 256], replicated
- value_grad: float32 [2048, 256], replicated
- out_grad: float32 [2048, 2048], P('col', 'row')
- gate_grad: float32 [2048, 5632], P('row', 'col')
- up_grad: float32 [2048, 5632], P('row', 'col')
- down_grad: float32 [5632, 2048], P('col', 'row')
- norm_one_grad: float32 [2048], replicated
- norm_two_grad: float32 [2048], replicated
- stream_rms: float32 [3], replicated
The draws below stay inside these ranges and needn't reach their ends.
Inputs may be any that keep to these rules, and one draw needn't show every extreme that they name: `segment_ids`: Non-decreasing, rising by at most one from a token to the next; every sequence of 2048 tokens holds exactly three documents, numbered 3 s, 3 s + 1 and 3 s + 2 for sequence s; the middle one covers its positions 768 to 1279.
All inputs are finite; a program needn't handle non-finite values.
Results may differ from the reference program's by a relative error of at most 0.02.
Values may be sent and summed in bfloat16 or wider, within the bound.
A program may use at most 256 MiB of HBM per device.

```python
import math
import jax
import jax.numpy as jnp
from jax import lax

D = 2048
HEADS = 32
KV_HEADS = 4
HEAD = 64
FF = 5632
TOK_ROW = 1024
SEQ = 2048
TOKENS = 16384
HQ = 2048
KV = 256
N_COL = 8


def draw_tokens(key, part):
    key = jax.random.fold_in(key, 11)
    place = jnp.arange(TOKENS, dtype=jnp.float32)[:, None] / TOKENS
    return (jax.random.normal(key, (TOKENS, D), jnp.float32) * (0.6 + 1.2 * place)).astype(jnp.bfloat16)


def draw_segment_ids(key, part):
    key = jax.random.fold_in(key, 23)
    first, second = jax.random.split(key)
    seqs = TOKENS // (2 * TOK_ROW)
    early = jax.random.randint(first, (seqs, 1), 1, TOK_ROW - TOK_ROW // 4)
    late = jax.random.randint(second, (seqs, 1), TOK_ROW + TOK_ROW // 4, 2 * TOK_ROW)
    where = jnp.arange(2 * TOK_ROW, dtype=jnp.int32)[None, :]
    number = jnp.arange(seqs, dtype=jnp.int32)[:, None] * 3
    ids = number + (where >= early).astype(jnp.int32) + (where >= late).astype(jnp.int32)
    return ids.reshape(-1).astype(jnp.int32)


def shard_levels(own_key, shape, shards, least, high):
    loudness, own = 1.0, jax.random.fold_in(own_key, 6)
    for position, blocks in shards:
        draws = jnp.exp(jax.random.uniform(jax.random.fold_in(own, position), (blocks,), jnp.float32, least / len(shards), high / len(shards)))
        loudness = loudness * jnp.repeat(draws, shape[position] // blocks).reshape([-1 if axis == position else 1 for axis in range(len(shape))])
    return loudness


def centred(key, extent, spread, limit, cuts=(), held_as=jnp.bfloat16):
    loudness = shard_levels(key, extent, cuts, -0.22, 0.18) if cuts else 1.0
    values = jax.random.normal(key, extent, jnp.float32) * spread * loudness
    return jnp.minimum(jnp.maximum(values, -limit), limit).astype(held_as)


def setup_inputs(seed: int = 0) -> dict:
    seeds = jax.random.split(jax.random.key(seed), 13)
    return {
        "tokens": draw_tokens(jax.random.fold_in(seeds[12], 71), 0),
        "segment_ids": draw_segment_ids(jax.random.fold_in(seeds[12], 71), 0),
        "norm_one": jnp.clip(1.0 + 0.1 * jax.random.normal(seeds[2], (D,), jnp.float32), 0.5, 1.5).astype(jnp.bfloat16),
        "w_query": centred(seeds[3], (D, HQ), D ** -0.5, 0.125, ((0, 16), (1, 8))),
        "w_key": centred(seeds[4], (D, KV), D ** -0.5, 0.125),
        "w_value": centred(seeds[5], (D, KV), D ** -0.5, 0.125),
        "w_out": centred(seeds[6], (HQ, D), (HQ // 32) ** -0.5, 0.75, ((0, 8), (1, 16))),
        "norm_two": jnp.clip(1.0 + 0.1 * jax.random.normal(seeds[7], (D,), jnp.float32), 0.5, 1.5).astype(jnp.bfloat16),
        "w_gate": centred(seeds[8], (D, FF), D ** -0.5, 0.125, ((0, 16), (1, 8))),
        "w_up": centred(seeds[9], (D, FF), D ** -0.5, 0.125, ((0, 16), (1, 8))),
        "w_down": centred(seeds[10], (FF, D), (FF // 4) ** -0.5, 0.15625, ((0, 8), (1, 16))),
        "cotangent": centred(seeds[11], (TOKENS, D), 1.0, 6.0, ((0, 16), (1, 8))),
    }


@jax.custom_vjp
def low(v):
    return lax.optimization_barrier(v.astype(jnp.bfloat16)).astype(jnp.float32)

@jax.custom_vjp
def low_back(v):
    return v

def low_keep(v):
    return (low(v), None)

def low_pass(kept, grad):
    return (grad,)

def back_keep(v):
    return (v, None)

def back_low(kept, grad):
    return (low(grad),)
low.defvjp(low_keep, low_pass)
low_back.defvjp(back_keep, back_low)
eps = 1e-05

def matmul(left, right):
    return jnp.dot(left, right, precision=lax.Precision.HIGHEST, preferred_element_type=jnp.float32)

def angles(positions, half):
    freq = jnp.exp(-math.log(10000.0) * jnp.arange(half, dtype=jnp.float32) / half)
    turned = positions.astype(jnp.float32)[:, None] * freq[None, :]
    return (jnp.cos(turned), jnp.sin(turned))

def rotate(values, cosine, sine, sign):
    count = values.shape[0]
    parts = values.reshape(count, -1, 2, cosine.shape[1])
    first = parts[:, :, 0]
    second = parts[:, :, 1]
    cos_b = cosine[:, None, :]
    sin_b = sine[:, None, :] * sign
    return jnp.stack([first * cos_b - second * sin_b, second * cos_b + first * sin_b], 2).reshape(values.shape)

def attend_sequence(query_seq, key_seq, value_seq, ids):
    length = ids.shape[0]
    order = jnp.arange(length, dtype=jnp.int32)
    allowed = (ids[:, None] == ids[None, :]) & (order[None, :] <= order[:, None])
    per = HEADS // N_COL
    outputs = []
    for group_at in range(N_COL):
        query_block = query_seq[:, group_at * per * HEAD:(group_at + 1) * per * HEAD].reshape(length, per, HEAD)
        raw = low_back(jnp.einsum('qhd,kd->hqk', query_block, key_seq[group_at], precision=lax.Precision.HIGHEST))
        scores = jnp.where(allowed[None], raw * 0.125, -1e+30)
        top = lax.optimization_barrier(jnp.max(scores, -1, keepdims=True))
        weights = jnp.where(allowed[None], jnp.exp(scores - top), 0.0)
        probs = weights / lax.optimization_barrier(jnp.sum(weights, -1, keepdims=True))
        attended = jnp.einsum('hqk,kd->qhd', low(probs), value_seq[group_at], precision=lax.Precision.HIGHEST)
        outputs.append(attended.reshape(length, per * HEAD))
    return jnp.concatenate(outputs, 1)

def reference(tokens, segment_ids, norm_one, w_query, w_key, w_value, w_out, norm_two, w_gate, w_up, w_down, cotangent):
    count = tokens.shape[0]
    seqs = count // SEQ
    ids_seq = segment_ids.reshape(seqs, SEQ)
    before = lax.optimization_barrier(jnp.sum((ids_seq[:, None, :] < ids_seq[:, :, None]).astype(jnp.int32), -1))
    positions = (jnp.arange(SEQ, dtype=jnp.int32)[None, :] - before).reshape(-1)
    cosine, sine = angles(positions, HEAD // 2)
    per = HEADS // N_COL
    group = HEADS // KV_HEADS
    step = jax.checkpoint(lambda items: attend_sequence(items[0], items[1], items[2], items[3]))

    def layer(x, gain_one, wq, wk, wv, wo, gain_two, wg, wu, wd):
        rstd_one = lax.rsqrt(lax.optimization_barrier(jnp.mean(x * x, -1, keepdims=True)) + eps)
        normed_one = low(x * rstd_one * gain_one)
        query_pre = low_back(matmul(normed_one, wq))
        queries = low(rotate(query_pre, cosine, sine, 1.0))
        key_pre = matmul(normed_one, wk)
        value_pre = matmul(normed_one, wv)
        key_groups = []
        value_groups = []
        for group_at in range(N_COL):
            slot = group_at * per // group
            key_groups.append(low(rotate(low_back(key_pre[:, slot * HEAD:(slot + 1) * HEAD]), cosine, sine, 1.0)))
            value_groups.append(low(low_back(value_pre[:, slot * HEAD:(slot + 1) * HEAD])))
        key_all = jnp.stack(key_groups).reshape(N_COL, seqs, SEQ, HEAD).transpose(1, 0, 2, 3)
        value_all = jnp.stack(value_groups).reshape(N_COL, seqs, SEQ, HEAD).transpose(1, 0, 2, 3)
        attended = lax.map(step, (queries.reshape(seqs, SEQ, -1), key_all, value_all, ids_seq))
        attended = low(low_back(attended.reshape(count, -1)))
        stream = x + low_back(matmul(attended, wo))
        stream_low = low(stream)
        rstd_two = lax.rsqrt(lax.optimization_barrier(jnp.mean(stream_low * stream_low, -1, keepdims=True)) + eps)
        normed_two = low(stream_low * rstd_two * gain_two)
        gate = low_back(matmul(normed_two, wg))
        up = low_back(matmul(normed_two, wu))
        hidden = low(jax.nn.silu(gate) * up)
        result = stream + low_back(matmul(hidden, wd))
        return (result, stream)
    inputs = (tokens.astype(jnp.float32), norm_one.astype(jnp.float32), w_query.astype(jnp.float32), w_key.astype(jnp.float32), w_value.astype(jnp.float32), w_out.astype(jnp.float32), norm_two.astype(jnp.float32), w_gate.astype(jnp.float32), w_up.astype(jnp.float32), w_down.astype(jnp.float32))
    result, pull, stream = jax.vjp(layer, *inputs, has_aux=True)
    grads = pull(cotangent.astype(jnp.float32))
    x = inputs[0]
    stats = jnp.stack([jnp.sqrt(jnp.mean(x * x)), jnp.sqrt(jnp.mean(stream * stream)), jnp.sqrt(jnp.mean(result * result))])
    return (result.astype(jnp.bfloat16), grads[0], grads[2], grads[3], grads[4], grads[5], grads[7], grads[8], grads[9], grads[1], grads[6], stats)
```

```python
import functools
import math

import jax
import jax.numpy as jnp
from jax import lax
from jax.experimental import pallas as pl
from jax.experimental.pallas import tpu as pltpu
from jax.sharding import PartitionSpec as P

BF16 = jnp.bfloat16
F32 = jnp.float32
HEAD = 64
eps = 1e-05
MESH = pl.DeviceIdType.MESH
ANY = pl.BlockSpec(memory_space=pl.ANY)
CHUNK = 256
T = 512


class Place:
    def __init__(self):
        row = lax.axis_index("row")
        col = lax.axis_index("col")
        self.z = row // 4
        self.yh = (row // 2) % 2
        self.core = row % 2
        self.yl = col // 4
        self.x = col % 4
        self.y = self.yh * 2 + self.yl
        self.quarter = self.core * 2 + self.yl

    def at(self, z, y, core, x):
        return {"row": z * 4 + (y // 2) * 2 + core, "col": (y % 2) * 4 + x}

    def by_x(self, d):
        return self.at(self.z, self.y, self.core, (self.x + d) % 4)

    def by_z(self, d):
        return self.at((self.z + d) % 4, self.y, self.core, self.x)

    def by_y(self, d):
        return self.at(self.z, (self.y + d) % 4, self.core, self.x)

    def partner(self):
        return self.at(self.z, self.y, 1 - self.core, self.x)

    def by_quarter(self, d):
        q = (self.quarter + d) % 4
        return self.at(self.z, self.yh * 2 + q % 2, q // 2, self.x)


def greet(peers):
    barrier = pltpu.get_barrier_semaphore()
    for peer in peers:
        pl.semaphore_signal(barrier, inc=1, device_id=peer, device_id_type=MESH)
    pl.semaphore_wait(barrier, len(peers))


def send(src, dst, sems, k, peer):
    return pltpu.make_async_remote_copy(
        src_ref=src, dst_ref=dst, send_sem=sems[0].at[k], recv_sem=sems[1].at[k],
        device_id=peer, device_id_type=MESH,
    )


def each(count, act):
    def step(i, carry):
        act(i)
        return carry

    lax.fori_loop(0, count, step, 0)


def perm_row(z, y, core):
    yh = y // 2
    return ((z % 2) * 2 + yh) * 512 + (z // 2) * 256 + core * 128


def reshard_in(me, src, full, sems, lsem):
    def chunk(q):
        return src.at[pl.ds(pl.multiple_of(jnp.where(me.core == 0, q, 3 - q) * CHUNK, CHUNK), CHUNK)]

    half = pl.multiple_of(me.core * CHUNK, CHUNK)
    place = full.at[me.x, pl.ds(half, CHUNK), pl.ds(pl.multiple_of(me.yl * 256, 256), 256)]
    copies = []
    for d in (1, 2, 3):
        copies.append(send(chunk((me.quarter + d) % 4), place, sems, d, me.by_quarter(d)))
    local = pltpu.make_async_copy(chunk(me.quarter), place, lsem)
    return copies, local


def ring_gather(me, full, sems):
    x = me.x
    right, left = me.by_x(1), me.by_x(3)
    xl, xr = (x + 3) % 4, (x + 1) % 4
    h = full.shape[1] // 2
    one = [
        send(full.at[x], full.at[x], sems, 0, right),
        send(full.at[x], full.at[x], sems, 1, left),
    ]
    two = [
        send(full.at[xl, pl.ds(0, h)], full.at[xl, pl.ds(0, h)], sems, 2, right),
        send(full.at[xr, pl.ds(h, h)], full.at[xr, pl.ds(h, h)], sems, 3, left),
    ]
    return one, two


class Spread:
    def __init__(self, me, src, slot, z_first, sems, lsem):
        self.me, self.src, self.slot, self.z_first, self.sems, self.lsem = me, src, slot, z_first, sems, lsem

    def local(self):
        me = self.me
        return pltpu.make_async_copy(self.src, self.slot(me.z, me.y, me.core), self.lsem)

    def first(self, i):
        me = self.me
        peer = me.by_z(i + 1) if self.z_first else me.by_y(i + 1)
        return send(self.src, self.slot(me.z, me.y, me.core), self.sems, i, peer)

    def line(self, k):
        me = self.me
        if self.z_first:
            return self.slot((me.z + 4 - k) % 4, me.y, me.core)
        return self.slot(me.z, (me.y + 4 - k) % 4, me.core)

    def second(self, k, i):
        me = self.me
        peer = me.by_y(i + 1) if self.z_first else me.by_z(i + 1)
        block = self.line(k)
        return send(block, block, self.sems, 3 + k * 3 + i, peer)

    def third(self, i):
        me = self.me
        if self.z_first:
            block = self.slot((me.z + 4 - i // 4) % 4, (me.y + 4 - i % 4) % 4, me.core)
        else:
            block = self.slot((me.z + 4 - i % 4) % 4, (me.y + 4 - i // 4) % 4, me.core)
        return send(block, block, self.sems, 15 + i, me.partner())

    def start(self):
        self.local().start()
        each(3, lambda i: self.first(i).start())

    def turn(self):
        self.local().wait()
        each(3, lambda i: self.second(0, i).start())
        self.third(0).start()

        def arrived(k):
            self.first(k).wait_recv()
            each(3, lambda i: self.second(k + 1, i).start())
            self.third((k + 1) * 4).start()

        each(3, arrived)

    def cross(self):
        def arrived(j):
            k, i = j // 3, j % 3
            self.second(k, i).wait_recv()
            self.third(k * 4 + i + 1).start()

        each(12, arrived)

    def finish(self):
        each(16, lambda i: self.third(i).wait_recv())
        each(3, lambda i: self.first(i).wait_send())
        each(12, lambda j: self.second(j // 3, j % 3).wait_send())
        each(16, lambda i: self.third(i).wait_send())


def weight_slots(q, o, g, u, d):
    def ds(start, size):
        return pl.ds(pl.multiple_of(start, 128), size)

    return (
        lambda z, y, c: q.at[ds(perm_row(z, y, c), 128), ds((y % 2) * 256, 256)],
        lambda z, y, c: o.at[ds((y % 2) * 256, 256), ds(perm_row(z, y, c), 128)],
        lambda z, y, c: g.at[y % 2, ds(perm_row(z, y, c), 128)],
        lambda z, y, c: u.at[y % 2, ds(perm_row(z, y, c), 128)],
        lambda z, y, c: d.at[y % 2, :, ds(perm_row(z, y, c), 128)],
    )


def gather_kernel(tok, cot, wq, wo, wg, wu, wd, tok_f, cot_f, q, o, g, u, d, *sems):
    me = Place()
    peers = [me.by_x(1), me.by_x(3), me.partner()]
    peers += [me.by_z(i) for i in (1, 2, 3)] + [me.by_y(i) for i in (1, 2, 3)]
    greet_all(me)
    act_send, act_recv, w_send, w_recv, lsem = sems
    slots = weight_slots(q, o, g, u, d)
    first_z = (True, True, True, False, False)
    spreads = [
        Spread(me, src, slots[n], first_z[n], (w_send.at[n], w_recv.at[n]), lsem.at[2 + n])
        for n, src in enumerate((wq, wo, wg, wu, wd))
    ]
    in_copies, in_local = reshard_in(me, tok, tok_f, (act_send.at[0], act_recv.at[0]), lsem.at[0])
    cot_copies, cot_local = reshard_in(me, cot, cot_f, (act_send.at[1], act_recv.at[1]), lsem.at[1])
    for c in in_copies + [in_local] + cot_copies + [cot_local]:
        c.start()
    for s in spreads:
        s.start()
    rings = []
    for n, (copies, local, full) in enumerate(((in_copies, in_local, tok_f), (cot_copies, cot_local, cot_f))):
        for c in copies:
            c.wait_recv()
        local.wait()
        one, two = ring_gather(me, full, (act_send.at[2 + n], act_recv.at[2 + n]))
        for c in one:
            c.start()
        rings.append((one, two))
    for s in spreads:
        s.turn()
    for one, two in rings:
        for a, b in zip(one, two):
            a.wait_recv()
            b.start()
    for s in spreads:
        s.cross()
    for one, two in rings:
        for a in one:
            a.wait_send()
        for a in two:
            a.wait()
    for c in in_copies + cot_copies:
        c.wait_send()
    for s in spreads:
        s.finish()


def greet_all(me):
    peers = [me.by_x(i) for i in (1, 2, 3)]
    peers += [me.by_z(i) for i in (1, 2, 3)] + [me.by_y(i) for i in (1, 2, 3)]
    peers += [me.by_quarter(i) for i in (1, 2, 3)]
    greet(peers)


def gather_inputs(tok, cot, wq, wo, wg, wu, wd):
    full = jax.ShapeDtypeStruct((4, T, 512), BF16)
    ff = wg.shape[1]
    outs = [
        full, full,
        jax.ShapeDtypeStruct((2048, 512), BF16),
        jax.ShapeDtypeStruct((512, 2048), BF16),
        jax.ShapeDtypeStruct((2, 2048, ff), BF16),
        jax.ShapeDtypeStruct((2, 2048, ff), BF16),
        jax.ShapeDtypeStruct((2, ff, 2048), BF16),
    ]
    dma = pltpu.SemaphoreType.DMA
    return pl.pallas_call(
        gather_kernel, out_shape=outs, in_specs=[ANY] * 7, out_specs=[ANY] * 7,
        scratch_shapes=[dma((4, 4)), dma((4, 4)), dma((5, 31)), dma((5, 31)), dma((7,))],
        compiler_params=pltpu.CompilerParams(collective_id=0, has_side_effects=True),
    )(tok, cot, wq, wo, wg, wu, wd)


def quarters_kernel(mine, everyone, ss, rs, ls):
    me = Place()
    greet([me.by_quarter(i) for i in (1, 2, 3)])
    slots = (me.quarter, 7 - me.quarter)
    copies = []
    for h in (0, 1):
        for d in (1, 2, 3):
            copies.append(send(mine.at[h], everyone.at[slots[h]], (ss, rs), h * 4 + d, me.by_quarter(d)))
    local = [pltpu.make_async_copy(mine.at[h], everyone.at[slots[h]], ls.at[h]) for h in (0, 1)]
    for c in copies + local:
        c.start()
    for c in copies + local:
        c.wait()


def quarters_gather(mine, cid):
    dma = pltpu.SemaphoreType.DMA
    return pl.pallas_call(
        quarters_kernel, out_shape=jax.ShapeDtypeStruct((8,) + mine.shape[1:], mine.dtype),
        in_specs=[ANY], out_specs=ANY, scratch_shapes=[dma((8,)), dma((8,)), dma((2,))],
        compiler_params=pltpu.CompilerParams(collective_id=cid, has_side_effects=True),
    )(mine)


def quarters_back_kernel(parts, got, ss, rs):
    me = Place()
    greet([me.by_quarter(i) for i in (1, 2, 3)])
    copies = []
    for d in (1, 2, 3):
        q = (me.quarter + d) % 4
        for h, slot in ((0, q), (1, 7 - q)):
            copies.append(send(parts.at[slot], got.at[d - 1, h], (ss, rs), h * 4 + d, me.by_quarter(d)))
    for c in copies:
        c.start()
    for c in copies:
        c.wait()


def quarters_back(parts, cid):
    dma = pltpu.SemaphoreType.DMA
    return pl.pallas_call(
        quarters_back_kernel, out_shape=jax.ShapeDtypeStruct((3, 2) + parts.shape[1:], parts.dtype),
        in_specs=[ANY], out_specs=ANY, scratch_shapes=[dma((8,)), dma((8,))],
        compiler_params=pltpu.CompilerParams(collective_id=cid, has_side_effects=True),
    )(parts)


def return_kernel(pieces, home, ss, rs, ls):
    me = Place()
    greet([me.by_quarter(i) for i in (1, 2, 3)])

    def piece(q):
        half, block = q // 2, q % 2
        row = jnp.where(half == 0, me.quarter, 3 - me.quarter)
        return pieces.at[half, block], home.at[pl.ds(pl.multiple_of(row * CHUNK, CHUNK), CHUNK)]

    copies = []
    for d in (1, 2, 3):
        src, dst = piece((me.quarter + d) % 4)
        copies.append(send(src, dst, (ss, rs), d, me.by_quarter(d)))
    src, dst = piece(me.quarter)
    copies.append(pltpu.make_async_copy(src, dst, ls))
    for c in copies:
        c.start()
    for c in copies:
        c.wait()


def return_home(pieces, cid):
    dma = pltpu.SemaphoreType.DMA
    return pl.pallas_call(
        return_kernel, out_shape=jax.ShapeDtypeStruct((1024, 256), pieces.dtype),
        in_specs=[ANY], out_specs=ANY, scratch_shapes=[dma((4,)), dma((4,)), dma],
        compiler_params=pltpu.CompilerParams(collective_id=cid, has_side_effects=True),
    )(pieces)


def x_scatter_kernel(parts, got, ss, rs):
    me = Place()
    greet([me.by_x(i) for i in (1, 2, 3)])
    copies = [send(parts.at[(me.x + d) % 4], got.at[d - 1], (ss, rs), d, me.by_x(d)) for d in (1, 2, 3)]
    for c in copies:
        c.start()
    for c in copies:
        c.wait()


def x_scatter(parts, cid):
    dma = pltpu.SemaphoreType.DMA
    got = pl.pallas_call(
        x_scatter_kernel, out_shape=jax.ShapeDtypeStruct((3,) + parts.shape[1:], parts.dtype),
        in_specs=[ANY], out_specs=ANY, scratch_shapes=[dma((4,)), dma((4,))],
        compiler_params=pltpu.CompilerParams(collective_id=cid, has_side_effects=True),
    )(parts)
    own = lax.dynamic_index_in_dim(parts, lax.axis_index("col") % 4, 0, keepdims=False)
    return own.astype(F32) + jnp.sum(got.astype(F32), 0)


def x_gather_kernel(mine, full, ss, rs, ls):
    me = Place()
    greet([me.by_x(1), me.by_x(3)])
    local = pltpu.make_async_copy(mine, full.at[me.x], ls)
    local.start()
    local.wait()
    one, two = ring_gather(me, full, (ss, rs))
    for c in one:
        c.start()
    for a, b in zip(one, two):
        a.wait_recv()
        b.start()
    for a in one:
        a.wait_send()
    for b in two:
        b.wait()


def x_gather(mine, cid):
    dma = pltpu.SemaphoreType.DMA
    return pl.pallas_call(
        x_gather_kernel, out_shape=jax.ShapeDtypeStruct((4,) + mine.shape, mine.dtype),
        in_specs=[pl.BlockSpec(memory_space=pltpu.VMEM)], out_specs=ANY, scratch_shapes=[dma((4,)), dma((4,)), dma],
        compiler_params=pltpu.CompilerParams(collective_id=cid, has_side_effects=True),
    )(mine)


def core_kernel(count, *refs):
    me = Place()
    greet([me.partner()])
    parts, got, ss, rs = refs[:count], refs[count:2 * count], refs[-2], refs[-1]
    copies = [send(p.at[1 - me.core], g, (ss, rs), n, me.partner()) for n, (p, g) in enumerate(zip(parts, got))]
    for c in copies:
        c.start()
    for c in copies:
        c.wait()


def line_kernel(axes, *refs):
    me = Place()
    greet([me.by_z(i) for i in (1, 2, 3)] + [me.by_y(i) for i in (1, 2, 3)])
    count = len(axes)
    parts, got, ss, rs = refs[:count], refs[count:2 * count], refs[-2], refs[-1]
    copies = []
    for n, (p, g) in enumerate(zip(parts, got)):
        for d in (1, 2, 3):
            if axes[n] == "z":
                copies.append(send(p.at[(me.z + d) % 4], g.at[d - 1], (ss, rs), n * 4 + d, me.by_z(d)))
            else:
                copies.append(send(p.at[(me.y + d) % 4], g.at[d - 1], (ss, rs), n * 4 + d, me.by_y(d)))
    for c in copies:
        c.start()
    for c in copies:
        c.wait()


def scatter_grads(grads, first_z, cid):
    count = len(grads)
    dma = pltpu.SemaphoreType.DMA
    params = dict(in_specs=[ANY] * count, out_specs=[ANY] * count)
    me = Place()
    got = pl.pallas_call(
        functools.partial(core_kernel, count),
        out_shape=[jax.ShapeDtypeStruct(g.shape[1:], BF16) for g in grads],
        scratch_shapes=[dma((count,)), dma((count,))],
        compiler_params=pltpu.CompilerParams(collective_id=cid, has_side_effects=True), **params,
    )(*grads)
    sums = []
    for g, h, fz in zip(grads, got, first_z):
        s = lax.dynamic_index_in_dim(g, me.core, 0, keepdims=False).astype(F32) + h.astype(F32)
        s = s.astype(BF16)
        sums.append(s if fz else jnp.swapaxes(s, 0, 1))
    for step in (0, 1):
        axes = tuple("z" if fz == (step == 0) else "y" for fz in first_z)
        got = pl.pallas_call(
            functools.partial(line_kernel, axes),
            out_shape=[jax.ShapeDtypeStruct((3,) + s.shape[1:], BF16) for s in sums],
            scratch_shapes=[dma((4 * count,)), dma((4 * count,))],
            compiler_params=pltpu.CompilerParams(collective_id=cid + 1 + step, has_side_effects=True), **params,
        )(*sums)
        new = []
        for s, h, axis in zip(sums, got, axes):
            own = lax.dynamic_index_in_dim(s, me.z if axis == "z" else me.y, 0, keepdims=False)
            total = own.astype(F32) + jnp.sum(h.astype(F32), 0)
            new.append(total.astype(BF16) if step == 0 else total)
        sums = new
    return sums


def angles(positions, half):
    freq = jnp.exp(-math.log(10000.0) * jnp.arange(half, dtype=jnp.float32) / half)
    turned = positions.astype(jnp.float32)[:, None] * freq[None, :]
    return (jnp.cos(turned), jnp.sin(turned))


def rotate(values, cosine, sine, sign):
    count = values.shape[0]
    parts = values.reshape(count, -1, 2, cosine.shape[1])
    first = parts[:, :, 0]
    second = parts[:, :, 1]
    cos_b = cosine[:, None, :]
    sin_b = sine[:, None, :] * sign
    return jnp.stack([first * cos_b - second * sin_b, second * cos_b + first * sin_b], 2).reshape(
        values.shape
    )


def dot_plain(left, right):
    return jnp.dot(left, right, preferred_element_type=F32)


def dot_tn(left, right):
    return lax.dot_general(left, right, (((0,), (0,)), ((), ())), preferred_element_type=F32)


def dot_nt(left, right):
    return lax.dot_general(left, right, (((1,), (1,)), ((), ())), preferred_element_type=F32)


def flat(full):
    return full.transpose(1, 0, 2).reshape(T, 2048)


def blocks(value):
    return value.reshape(T, 4, 512).transpose(1, 0, 2)


def norm_back(partial_value, rows_f, rstd, gain):
    scaled = partial_value * gain
    inner = jnp.sum(scaled * rows_f, -1, keepdims=True)
    term = rstd * scaled - rows_f * (rstd * rstd * rstd / rows_f.shape[1]) * inner
    gain_grad = jnp.sum(partial_value * rows_f * rstd, 0)
    return term, gain_grad


def by_row(value, cols):
    v = value.reshape(2, 2, 2, 2, 128, cols)
    return v.transpose(3, 2, 0, 1, 4, 5).reshape(2, 4, 2, 128, cols)


def by_row_cols(value, rows):
    v = value.reshape(rows, 2, 2, 2, 2, 128)
    return v.transpose(4, 3, 1, 2, 0, 5).reshape(2, 4, 2, rows, 128)


def to_device_order(vector):
    return vector.reshape(2, 4, 256).transpose(1, 0, 2).reshape((2048,) + vector.shape[1:])


def shards(tokens, segment_ids, norm_one, w_query, w_key, w_value, w_out, norm_two, w_gate, w_up, w_down, cotangent):
    me = Place()
    x = me.x
    tok_f, cot_f, q_w, o_w, g_w, u_w, d_w = gather_inputs(tokens, cotangent, w_query, w_out, w_gate, w_up, w_down)

    def kv_cols(w):
        w = w.reshape(2, 4, 256, 2, 2, 64)
        w = lax.dynamic_index_in_dim(w, x // 2, 4, keepdims=False)
        return w.transpose(1, 0, 2, 3, 4).reshape(2048, 128)

    kv_w = jnp.concatenate([kv_cols(w_key), kv_cols(w_value)], 1)
    gain_one = to_device_order(norm_one.astype(F32))
    gain_two = to_device_order(norm_two.astype(F32))

    seq = me.z * 2 + me.yh
    seq_ids = lax.dynamic_slice_in_dim(segment_ids, seq * 2048, 2048).reshape(8, CHUNK)
    i = me.quarter
    chunk_at = jnp.stack([i, 7 - i])
    own_ids = jnp.concatenate([lax.dynamic_index_in_dim(seq_ids, i, 0, False), lax.dynamic_index_in_dim(seq_ids, 7 - i, 0, False)])
    place = (chunk_at[:, None] * CHUNK + jnp.arange(CHUNK, dtype=jnp.int32)[None]).reshape(T)
    seq_ids = seq_ids.reshape(2048)
    before = jnp.sum((seq_ids[None, :] < own_ids[:, None]).astype(jnp.int32), 1)
    cosine, sine = angles(place - before, HEAD // 2)
    allowed = (own_ids[:, None] == seq_ids[None, :]) & (jnp.arange(2048)[None, :] <= place[:, None])

    inputs_f = flat(tok_f).astype(F32)
    rstd_one = lax.rsqrt(jnp.mean(inputs_f * inputs_f, -1, keepdims=True) + eps)
    normed_one = (inputs_f * rstd_one * gain_one).astype(BF16)
    queries = rotate(dot_plain(normed_one, q_w), cosine, sine, 1.0).astype(BF16)
    kv_pre = dot_plain(normed_one, kv_w)
    keys = rotate(kv_pre[:, :128], cosine, sine, 1.0).astype(BF16)
    kv = jnp.concatenate([keys, kv_pre[:, 128:].astype(BF16)], 1).reshape(2, CHUNK, 256)
    kv_all = quarters_gather(kv, 1).reshape(2048, 256)

    def key_of(head):
        return kv_all[:, (head // 4) * 64:(head // 4 + 1) * 64]

    def value_of(head):
        return kv_all[:, 128 + (head // 4) * 64:128 + (head // 4 + 1) * 64]

    outputs, logs = [], []
    for head in range(8):
        qh = queries[:, head * HEAD:(head + 1) * HEAD]
        s = jnp.where(allowed, dot_nt(qh, key_of(head)) * 0.125, -1e30)
        top = jnp.max(s, 1, keepdims=True)
        w = jnp.where(allowed, jnp.exp(s - top), 0.0)
        total = jnp.sum(w, 1, keepdims=True)
        outputs.append(dot_plain((w / total).astype(BF16), value_of(head)))
        logs.append(top + jnp.log(total))
    attended = jnp.concatenate(outputs, 1).astype(BF16)
    own_tok = lax.dynamic_index_in_dim(tok_f, x, 0, False).astype(F32)
    own_cot = lax.dynamic_index_in_dim(cot_f, x, 0, False).astype(F32)
    stream = own_tok + x_scatter(blocks(dot_plain(attended, o_w).astype(BF16)), 2)
    middle = x_gather(stream.astype(BF16), 3)
    middle_f = flat(middle).astype(F32)
    rstd_two = lax.rsqrt(jnp.mean(middle_f * middle_f, -1, keepdims=True) + eps)
    normed_two = (middle_f * rstd_two * gain_two).astype(BF16)
    cot_rows = flat(cot_f)

    feed = 0.0
    d_normed_two = 0.0
    g_gate, g_up, g_down = [], [], []
    for b in (0, 1):
        gate = dot_plain(normed_two, g_w[b])
        up = dot_plain(normed_two, u_w[b])
        sigma = jax.nn.sigmoid(gate)
        active = gate * sigma
        hidden = (active * up).astype(BF16)
        feed = feed + dot_plain(hidden, d_w[b])
        d_hidden = dot_nt(cot_rows, d_w[b])
        g_down.append(dot_tn(hidden, cot_rows).astype(BF16))
        d_gate = (d_hidden * up * sigma * (1.0 + gate * (1.0 - sigma))).astype(BF16)
        d_up = (d_hidden * active).astype(BF16)
        g_gate.append(dot_tn(normed_two, d_gate).astype(BF16))
        g_up.append(dot_tn(normed_two, d_up).astype(BF16))
        d_normed_two = d_normed_two + dot_nt(d_gate, g_w[b]) + dot_nt(d_up, u_w[b])
    result = stream + x_scatter(blocks(feed.astype(BF16)), 4)
    mixed = return_home(result.astype(BF16).reshape(2, CHUNK, 2, 256).transpose(0, 2, 1, 3), 5)
    term_two, gain_two_grad = norm_back(d_normed_two, middle_f, rstd_two, gain_two)
    d_stream = own_cot + x_scatter(blocks(term_two.astype(BF16)), 6)
    d_rows = flat(x_gather(d_stream.astype(BF16), 7))
    d_attended = dot_nt(d_rows, o_w).astype(BF16)
    g_out = dot_tn(attended, d_rows).astype(BF16)

    dq_list, dk_list, dv_list = [], [0.0, 0.0], [0.0, 0.0]
    for head in range(8):
        qh = queries[:, head * HEAD:(head + 1) * HEAD]
        gh = d_attended[:, head * HEAD:(head + 1) * HEAD]
        s = jnp.where(allowed, dot_nt(qh, key_of(head)) * 0.125, -1e30)
        p = jnp.where(allowed, jnp.exp(s - logs[head]), 0.0)
        dp = dot_nt(gh, value_of(head))
        delta = jnp.sum(p * dp, 1, keepdims=True)
        ds = (p * (dp - delta) * 0.125).astype(BF16)
        dq_list.append(dot_plain(ds, key_of(head)))
        dk_list[head // 4] = dk_list[head // 4] + dot_tn(ds, qh)
        dv_list[head // 4] = dv_list[head // 4] + dot_tn(p.astype(BF16), gh)
    dkv = jnp.concatenate(dk_list + dv_list, 1).reshape(8, CHUNK, 256)
    got = quarters_back(dkv.astype(BF16), 8)
    own = jnp.stack([lax.dynamic_index_in_dim(dkv, i, 0, False), lax.dynamic_index_in_dim(dkv, 7 - i, 0, False)])
    dkv = (own + jnp.sum(got.astype(F32), 0)).reshape(T, 256)
    dq_pre = rotate(jnp.concatenate(dq_list, 1), cosine, sine, -1.0).astype(BF16)
    dkv_pre = jnp.concatenate([rotate(dkv[:, :128], cosine, sine, -1.0), dkv[:, 128:]], 1).astype(BF16)
    g_query = dot_tn(normed_one, dq_pre).astype(BF16)
    g_kv = dot_tn(normed_one, dkv_pre).astype(BF16)
    d_normed_one = dot_nt(dq_pre, q_w) + dot_nt(dkv_pre, kv_w)
    term_one, gain_one_grad = norm_back(d_normed_one, inputs_f, rstd_one, gain_one)
    d_tokens = d_stream + x_scatter(blocks(term_one.astype(BF16)), 9)
    input_grad = return_home(d_tokens.reshape(2, CHUNK, 2, 256).transpose(0, 2, 1, 3), 10)

    def with_y(v):
        return v.reshape((2, 4, 4) + v.shape[4:])

    gq = with_y(by_row(g_query, 512).reshape(2, 4, 2, 128, 2, 256).transpose(0, 1, 2, 4, 3, 5))
    go = with_y(by_row_cols(g_out, 512).reshape(2, 4, 2, 2, 256, 128))
    ff = w_gate.shape[1]
    gg, gu = [with_y(jnp.stack([by_row(v, ff) for v in gs], 3)) for gs in (g_gate, g_up)]
    gd = with_y(jnp.stack([by_row_cols(v, ff) for v in g_down], 3))
    gkv = with_y(by_row(g_kv, 256).reshape(2, 4, 2, 2, 64, 256))
    query_s, out_s, gate_s, up_s, down_s, kv_s = scatter_grads(
        [gq, go, gg, gu, gd, gkv], (True, True, True, False, False, True), 11
    )
    shape = (2048, 256)
    pos = ((me.z // 2) * 4 + (me.z % 2) * 2 + me.yh) * 256 + me.core * 128 + me.yl * 64
    empty = jnp.zeros((2048, 4, 64), F32)
    kv_s = kv_s.reshape(64, 4, 64)

    def spread(pair):
        part = lax.dynamic_update_slice(jnp.zeros((64, 4, 64), F32), pair[:, 0:1], (0, x // 2, 0))
        part = lax.dynamic_update_slice(part, pair[:, 1:2], (0, 2 + x // 2, 0))
        return lax.dynamic_update_slice(empty, part, (pos, 0, 0)).reshape(shape)

    stats = jnp.stack([jnp.sum(own_tok * own_tok), jnp.sum(stream * stream), jnp.sum(result * result)])
    key_total, value_total = lax.psum((spread(kv_s[:, :2]), spread(kv_s[:, 2:])), ("row", "col"))
    one_total, two_total, stat_total = lax.psum((gain_one_grad, gain_two_grad, stats), ("row", "col"))

    def from_device_order(v):
        return v.reshape(4, 2, 256).transpose(1, 0, 2).reshape(2048)

    rms = jnp.sqrt(stat_total / (16384 * 2048))
    return (
        mixed, input_grad, query_s, key_total, value_total, out_s, gate_s, up_s, down_s,
        from_device_order(one_total), from_device_order(two_total), rms,
    )


def solution(mesh):
    return jax.shard_map(
        shards,
        mesh=mesh,
        in_specs=(
            P("row", "col"), P(), P(), P("row", "col"), P(), P(), P("col", "row"), P(),
            P("row", "col"), P("row", "col"), P("col", "row"), P("row", "col"),
        ),
        out_specs=(
            P("row", "col"), P("row", "col"), P("row", "col"), P(), P(), P("col", "row"),
            P("row", "col"), P("row", "col"), P("col", "row"), P(), P(), P(),
        ),
        check_vma=False,
    )
```

```python
import functools
import math

import jax
import jax.numpy as jnp
from jax import lax
from jax.experimental import pallas as pl
from jax.experimental.pallas import tpu as pltpu
from jax.sharding import PartitionSpec as P

BF16 = jnp.bfloat16
F32 = jnp.float32
HEAD = 64
eps = 1e-05
MESH = pl.DeviceIdType.MESH
ANY = pl.BlockSpec(memory_space=pl.ANY)
CHUNK = 256
T = 512


class Place:
    def __init__(self):
        row = lax.axis_index("row")
        col = lax.axis_index("col")
        self.z = row // 4
        self.yh = (row // 2) % 2
        self.core = row % 2
        self.yl = col // 4
        self.x = col % 4
        self.y = self.yh * 2 + self.yl
        self.quarter = self.core * 2 + self.yl

    def at(self, z, y, core, x):
        return {"row": z * 4 + (y // 2) * 2 + core, "col": (y % 2) * 4 + x}

    def by_x(self, d):
        return self.at(self.z, self.y, self.core, (self.x + d) % 4)

    def by_z(self, d):
        return self.at((self.z + d) % 4, self.y, self.core, self.x)

    def by_y(self, d):
        return self.at(self.z, (self.y + d) % 4, self.core, self.x)

    def partner(self):
        return self.at(self.z, self.y, 1 - self.core, self.x)

    def by_quarter(self, d):
        q = (self.quarter + d) % 4
        return self.at(self.z, self.yh * 2 + q % 2, q // 2, self.x)


def greet(peers):
    barrier = pltpu.get_barrier_semaphore()
    for peer in peers:
        pl.semaphore_signal(barrier, inc=1, device_id=peer, device_id_type=MESH)
    pl.semaphore_wait(barrier, len(peers))


def send(src, dst, sems, k, peer):
    return pltpu.make_async_remote_copy(
        src_ref=src, dst_ref=dst, send_sem=sems[0].at[k], recv_sem=sems[1].at[k],
        device_id=peer, device_id_type=MESH,
    )


def each(count, act):
    def step(i, carry):
        act(i)
        return carry

    lax.fori_loop(0, count, step, 0)


def perm_row(z, y, core):
    yh = y // 2
    return ((z % 2) * 2 + yh) * 512 + (z // 2) * 256 + core * 128


def reshard_in(me, src, full, sems, base, lsem):
    def chunk(q):
        return src.at[pl.ds(pl.multiple_of(jnp.where(me.core == 0, q, 3 - q) * CHUNK, CHUNK), CHUNK)]

    half = pl.multiple_of(me.core * CHUNK, CHUNK)
    place = full.at[pl.ds(half, CHUNK), pl.ds(pl.multiple_of(me.x * 512 + me.yl * 256, 256), 256)]
    copies = []
    for d in (1, 2, 3):
        copies.append(send(chunk((me.quarter + d) % 4), place, sems, base + d, me.by_quarter(d)))
    local = pltpu.make_async_copy(chunk(me.quarter), place, lsem)
    return copies, local


def ring_gather(me, full, sems):
    x = me.x
    right, left = me.by_x(1), me.by_x(3)
    xl, xr = (x + 3) % 4, (x + 1) % 4
    h = full.shape[1] // 2
    one = [
        send(full.at[x], full.at[x], sems, 0, right),
        send(full.at[x], full.at[x], sems, 1, left),
    ]
    two = [
        send(full.at[xl, pl.ds(0, h)], full.at[xl, pl.ds(0, h)], sems, 2, right),
        send(full.at[xr, pl.ds(h, h)], full.at[xr, pl.ds(h, h)], sems, 3, left),
    ]
    return one, two


class Spread:
    def __init__(self, me, src, slot, z_first, sems, lsem):
        self.me, self.src, self.slot, self.z_first, self.sems, self.lsem = me, src, slot, z_first, sems, lsem

    def local(self):
        me = self.me
        return pltpu.make_async_copy(self.src, self.slot(me.z, me.y, me.core), self.lsem)

    def first(self, i):
        me = self.me
        peer = me.by_z(i + 1) if self.z_first else me.by_y(i + 1)
        return send(self.src, self.slot(me.z, me.y, me.core), self.sems, i, peer)

    def line(self, k):
        me = self.me
        if self.z_first:
            return self.slot((me.z + 4 - k) % 4, me.y, me.core)
        return self.slot(me.z, (me.y + 4 - k) % 4, me.core)

    def second(self, k, i):
        me = self.me
        peer = me.by_y(i + 1) if self.z_first else me.by_z(i + 1)
        block = self.line(k)
        return send(block, block, self.sems, 3 + k * 3 + i, peer)

    def third(self, i):
        me = self.me
        if self.z_first:
            block = self.slot((me.z + 4 - i // 4) % 4, (me.y + 4 - i % 4) % 4, me.core)
        else:
            block = self.slot((me.z + 4 - i % 4) % 4, (me.y + 4 - i // 4) % 4, me.core)
        return send(block, block, self.sems, 15 + i, me.partner())

    def start(self):
        self.local().start()
        each(3, lambda i: self.first(i).start())

    def turn(self):
        self.local().wait()
        each(3, lambda i: self.second(0, i).start())
        self.third(0).start()

        def arrived(k):
            self.first(k).wait_recv()
            each(3, lambda i: self.second(k + 1, i).start())
            self.third((k + 1) * 4).start()

        each(3, arrived)

    def cross(self):
        def arrived(j):
            k, i = j // 3, j % 3
            self.second(k, i).wait_recv()
            self.third(k * 4 + i + 1).start()

        each(12, arrived)

    def finish(self):
        each(16, lambda i: self.third(i).wait_recv())
        each(3, lambda i: self.first(i).wait_send())
        each(12, lambda j: self.second(j // 3, j % 3).wait_send())
        each(16, lambda i: self.third(i).wait_send())


def weight_slots(q, o, g, u, d):
    def ds(start, size):
        return pl.ds(pl.multiple_of(start, 128), size)

    return (
        lambda z, y, c: q.at[ds(perm_row(z, y, c), 128), ds((y % 2) * 256, 256)],
        lambda z, y, c: o.at[ds((y % 2) * 256, 256), ds(perm_row(z, y, c), 128)],
        lambda z, y, c: g.at[y % 2, ds(perm_row(z, y, c), 128)],
        lambda z, y, c: u.at[y % 2, ds(perm_row(z, y, c), 128)],
        lambda z, y, c: d.at[y % 2, :, ds(perm_row(z, y, c), 128)],
    )


def greet_all(me):
    peers = [me.by_x(i) for i in (1, 2, 3)]
    peers += [me.by_z(i) for i in (1, 2, 3)] + [me.by_y(i) for i in (1, 2, 3)]
    peers += [me.by_quarter(i) for i in (1, 2, 3)]
    greet(peers)


def dot_plain(left, right):
    return jnp.dot(left, right, preferred_element_type=F32)


def dot_tn(left, right):
    return lax.dot_general(left, right, (((0,), (0,)), ((), ())), preferred_element_type=F32)


def dot_nt(left, right):
    return lax.dot_general(left, right, (((1,), (1,)), ((), ())), preferred_element_type=F32)


def lanes(start, size):
    return pl.ds(pl.multiple_of(start, 128), size)


class Ring:
    def __init__(self, me, full, rows, sems, base):
        x = me.x
        right, left = me.by_x(1), me.by_x(3)
        xl, xr = (x + 3) % 4, (x + 1) % 4

        def at(b, off, size):
            return full.at[rows, lanes(b * 512 + off, size)]

        self.one = [
            send(at(x, 0, 512), at(x, 0, 512), sems, base + 0, right),
            send(at(x, 0, 512), at(x, 0, 512), sems, base + 1, left),
        ]
        self.two = [
            send(at(xl, 0, 256), at(xl, 0, 256), sems, base + 2, right),
            send(at(xr, 256, 256), at(xr, 256, 256), sems, base + 3, left),
        ]

    def start(self):
        for c in self.one:
            c.start()

    def turn(self):
        for a, b in zip(self.one, self.two):
            a.wait_recv()
            b.start()

    def finish(self):
        for a in self.one:
            a.wait_send()
        for b in self.two:
            b.wait()


class RingSum:
    def __init__(self, me, part, rows, hop, got, sems, base):
        x = me.x
        self.part, self.rows, self.hop, self.got, self.x = part, rows, hop, got, x
        right, left = me.by_x(1), me.by_x(3)
        far, xr, xl = (x + 2) % 4, (x + 1) % 4, (x + 3) % 4
        self.xr, self.xl = xr, xl

        def at(b, off):
            return part.at[rows, lanes(b * 512 + off, 256)]

        self.one = [
            send(at(far, 0), hop.at[0], sems, base + 0, right),
            send(at(far, 256), hop.at[1], sems, base + 1, left),
            send(at(xr, 256), got.at[0, :, pl.ds(256, 256)], sems, base + 2, right),
            send(at(xl, 0), got.at[1, :, pl.ds(0, 256)], sems, base + 3, left),
        ]
        self.two = [
            send(at(xr, 0), got.at[0, :, pl.ds(0, 256)], sems, base + 4, right),
            send(at(xl, 256), got.at[1, :, pl.ds(256, 256)], sems, base + 5, left),
        ]

    def start(self):
        for c in self.one:
            c.start()

    def turn(self):
        for k, (b, off) in enumerate(((self.xr, 0), (self.xl, 256))):
            self.one[k].wait_recv()
            cols = lanes(b * 512 + off, 256)
            total = self.part[self.rows, cols].astype(F32) + self.hop[k].astype(F32)
            self.part[self.rows, cols] = total.astype(BF16)
            self.two[k].start()

    def finish(self):
        for k in (2, 3):
            self.one[k].wait_recv()
        for c in self.two:
            c.wait_recv()
        own = self.part[self.rows, lanes(self.x * 512, 512)].astype(F32)
        return own + self.got[0].astype(F32) + self.got[1].astype(F32)

    def drain(self):
        for c in self.one + self.two:
            c.wait_send()


def rope_rows(a, b, cosine, sine):
    return a * cosine - b * sine, b * cosine + a * sine


def document_starts(ids, seq, place):
    ids = ids[seq]

    def below(number):
        hit = (ids < number).astype(F32)
        return jnp.sum(jnp.sum(hit, 1, keepdims=True), 0, keepdims=True)

    second, third = below(3 * seq + 1).astype(jnp.int32), below(3 * seq + 2).astype(jnp.int32)
    return jnp.where(place >= third, third, jnp.where(place >= second, second, 0))


ORIGINAL = [(p % 2) * 4 + p // 2 for p in range(8)]


def device_order_row(ref):
    return jnp.concatenate([ref[:, b * 256:(b + 1) * 256].astype(F32) for b in ORIGINAL], 1)


def rms_rows(src, gain, dst, rstd):
    def step(k, carry):
        rows = pl.ds(pl.multiple_of(k * 64, 64), 64)
        v = src[rows, :].astype(F32)
        r = lax.rsqrt(jnp.sum(v * v, 1, keepdims=True) * (1.0 / 2048.0) + eps)
        rstd[rows, :] = r
        dst[rows, :] = (v * r * gain).astype(BF16)
        return carry

    lax.fori_loop(0, src.shape[0] // 64, step, 0)


def forward_kernel(
    tok, cot, wq_s, wo_s, wg_s, wu_s, wd_s, w_key, w_value, gain1, ids,
    xf, cf, mf, wq, wo, wg, wu, wd, qt, kvt, lse, ot, x1, h1, r1,
    part, hop, got, acc, mx, sm, kr, o_r, kv_tmp,
    a_s, a_r, w_s, w_r, lsem,
):
    me = Place()
    x = me.x
    acts = (a_s, a_r)
    greet_all(me)
    slots = weight_slots(wq, wo, wg, wu, wd)
    first_z = (True, True, True, False, False)
    spreads = [
        Spread(me, src, slots[n], first_z[n], (w_s.at[n], w_r.at[n]), lsem.at[2 + n])
        for n, src in enumerate((wq_s, wo_s, wg_s, wu_s, wd_s))
    ]
    in_copies, in_local = reshard_in(me, tok, xf, acts, 0, lsem.at[0])
    cot_copies, cot_local = reshard_in(me, cot, cf, acts, 4, lsem.at[1])
    for c in in_copies + [in_local]:
        c.start()
    for s in spreads:
        s.start()
    for c in cot_copies + [cot_local]:
        c.start()
    seq = me.z * 2 + me.yh
    chunk_of = (me.quarter, 7 - me.quarter)
    lane = lax.broadcasted_iota(jnp.int32, (1, CHUNK), 1)
    places = [c * CHUNK + lane for c in chunk_of]
    starts = [document_starts(ids, seq, p) for p in places]
    pos = jnp.concatenate([p - s for p, s in zip(places, starts)], 1).astype(F32)
    turn = lax.broadcasted_iota(jnp.int32, (32, 1), 0).astype(F32)
    angle = jnp.exp(-math.log(10000.0) * turn / 32.0) * pos
    cosine, sine = jnp.cos(angle), jnp.sin(angle)
    gain = device_order_row(gain1)

    for c in in_copies:
        c.wait_recv()
    in_local.wait()
    ring_tok = Ring(me, xf, pl.ds(0, T), acts, 8)
    ring_tok.start()
    spreads[0].turn()
    spreads[1].turn()
    for c in cot_copies:
        c.wait_recv()
    cot_local.wait()
    ring_tok.turn()
    ring_cot = Ring(me, cf, pl.ds(0, T), acts, 12)
    ring_cot.start()
    spreads[0].cross()
    for s in spreads[2:]:
        s.turn()
    ring_tok.finish()
    for c in in_copies + cot_copies:
        c.wait_send()

    rms_rows(xf, gain, h1, r1)
    spreads[0].finish()
    for n, w in enumerate((w_key, w_value)):
        total = None
        for p, b in enumerate(ORIGINAL):
            d = dot_plain(h1[:, p * 256:(p + 1) * 256], w[b * 256:(b + 1) * 256, :])
            total = d if total is None else total + d
        kv_tmp[n * 256:(n + 1) * 256, :] = total.T
    for g in (0, 1):
        head = pl.multiple_of((2 * g + x // 2) * HEAD, HEAD)
        a, b = rope_rows(kv_tmp[pl.ds(head, 32), :], kv_tmp[pl.ds(head + 32, 32), :], cosine, sine)
        v = kv_tmp[pl.ds(256 + head, HEAD), :]
        for h in (0, 1):
            cols = slice(h * CHUNK, (h + 1) * CHUNK)
            kvt[chunk_of[h], g * 64:g * 64 + 32, :] = a[:, cols].astype(BF16)
            kvt[chunk_of[h], g * 64 + 32:g * 64 + 64, :] = b[:, cols].astype(BF16)
            kvt[chunk_of[h], 128 + g * 64:192 + g * 64, :] = v[:, cols].astype(BF16)
    kv_copies = []
    for h in (0, 1):
        for d in (1, 2, 3):
            block = kvt.at[chunk_of[h]]
            kv_copies.append(send(block, block, acts, 16 + h * 4 + d, me.by_quarter(d)))
    for c in kv_copies:
        c.start()
    for n in (0, 1):
        q = dot_plain(h1[...], wq[:, n * 256:(n + 1) * 256]).T
        for hd in range(4):
            base = hd * HEAD
            a, b = rope_rows(q[base:base + 32], q[base + 32:base + 64], cosine, sine)
            qt[n * 256 + base:n * 256 + base + 32, :] = (a * 0.125).astype(BF16)
            qt[n * 256 + base + 32:n * 256 + base + 64, :] = (b * 0.125).astype(BF16)
    ring_cot.turn()
    spreads[1].cross()
    for c in kv_copies:
        c.wait()

    def key_rows(j, carry):
        for g in (0, 1):
            kr[j, g] = kvt[j, g * 64:(g + 1) * 64, :].astype(F32).T.astype(BF16)
        return carry

    lax.fori_loop(0, 8, key_rows, 0)

    def attend_begin():
        mx[...] = jnp.full(mx.shape, -1e30, F32)
        sm[...] = jnp.zeros(sm.shape, F32)
        acc[...] = jnp.zeros(acc.shape, F32)

    def attend(h, low, high):
        cols = slice(h * CHUNK, (h + 1) * CHUNK)

        def step(j, carry):
            at = lax.broadcasted_iota(jnp.int32, (CHUNK, CHUNK), 0) + j * CHUNK
            ok = (at >= starts[h]) & (at <= places[h])
            for hd in range(8):
                g = hd // 4
                s = jnp.where(ok, dot_plain(kr[j, g], qt[hd * 64:(hd + 1) * 64, cols]), -1e30)
                old = mx[hd:hd + 1, :]
                new = jnp.maximum(old, jnp.max(s, 0, keepdims=True))
                p = jnp.exp(s - new)
                shrink = jnp.exp(old - new)
                mx[hd:hd + 1, :] = new
                sm[hd:hd + 1, :] = sm[hd:hd + 1, :] * shrink + jnp.sum(p, 0, keepdims=True)
                acc[hd * 64:(hd + 1) * 64, :] = acc[hd * 64:(hd + 1) * 64, :] * shrink + dot_plain(
                    kvt[j, 128 + g * 64:192 + g * 64, :], p.astype(BF16)
                )
            return carry

        lax.fori_loop(low, high, step, 0)

    def attend_end(h):
        cols = slice(h * CHUNK, (h + 1) * CHUNK)
        lse[h] = mx[...] + jnp.log(sm[...])
        for hd in range(8):
            rows = slice(hd * 64, (hd + 1) * 64)
            acc[rows, :] = acc[rows, :] / sm[hd:hd + 1, :]
        ot[:, cols] = acc[...].astype(BF16)
        o_r[cols, :] = acc[...].T.astype(BF16)

    def project(h):
        rows = slice(h * CHUNK, (h + 1) * CHUNK)

        def step(n, carry):
            cols = lanes(n * 256, 256)
            part[rows, cols] = dot_plain(o_r[rows, :], wo[:, cols]).astype(BF16)
            return carry

        lax.fori_loop(0, 8, step, 0)

    sums = [RingSum(me, part, pl.ds(h * CHUNK, CHUNK), hop.at[h], got.at[h], acts, 24 + 6 * h) for h in (0, 1)]
    rings = [Ring(me, mf, pl.ds(h * CHUNK, CHUNK), acts, 36 + 4 * h) for h in (0, 1)]
    own = lanes(x * 512, 512)

    def stream(h):
        rows = pl.ds(h * CHUNK, CHUNK)
        total = xf[rows, own].astype(F32) + sums[h].finish()
        x1[rows, :] = total
        mf[rows, own] = total.astype(BF16)

    attend_begin()
    attend(0, 0, chunk_of[0] + 1)
    attend_end(0)
    spreads[1].finish()
    project(0)
    sums[0].start()
    attend_begin()
    attend(1, 0, 3)
    sums[0].turn()
    for s in spreads[2:]:
        s.cross()
    attend(1, 3, chunk_of[1] + 1)
    attend_end(1)
    stream(0)
    rings[0].start()
    project(1)
    sums[1].start()
    rings[0].turn()
    sums[1].turn()
    stream(1)
    rings[1].start()
    ring_cot.finish()
    for s in spreads[2:]:
        s.finish()
    rings[1].turn()
    for h in (0, 1):
        rings[h].finish()
        sums[h].drain()


def forward(tok, cot, wq, wo, wg, wu, wd, w_key, w_value, gain1, ids):
    ff = wg.shape[1]
    sds = jax.ShapeDtypeStruct
    outs = [
        sds((T, 2048), BF16), sds((T, 2048), BF16), sds((T, 2048), BF16),
        sds((2048, 512), BF16), sds((512, 2048), BF16),
        sds((2, 2048, ff), BF16), sds((2, 2048, ff), BF16), sds((2, ff, 2048), BF16),
        sds((512, T), BF16), sds((8, 256, CHUNK), BF16), sds((2, 8, CHUNK), F32), sds((512, T), BF16),
        sds((T, 512), F32), sds((T, 2048), BF16), sds((T, 1), F32),
    ]
    dma = pltpu.SemaphoreType.DMA
    vm = pl.BlockSpec(memory_space=pltpu.VMEM)
    return pl.pallas_call(
        forward_kernel, out_shape=outs, in_specs=[ANY] * 7 + [vm] * 4, out_specs=[vm] * len(outs),
        scratch_shapes=[
            pltpu.VMEM((T, 2048), BF16), pltpu.VMEM((2, 2, 256, 256), BF16), pltpu.VMEM((2, 2, 256, 512), BF16),
            pltpu.VMEM((512, CHUNK), F32), pltpu.VMEM((8, CHUNK), F32), pltpu.VMEM((8, CHUNK), F32),
            pltpu.VMEM((8, 2, CHUNK, 64), BF16), pltpu.VMEM((T, 512), BF16), pltpu.VMEM((512, T), F32),
            dma((44,)), dma((44,)), dma((5, 31)), dma((5, 31)), dma((7,)),
        ],
        compiler_params=pltpu.CompilerParams(collective_id=0, has_side_effects=True, vmem_limit_bytes=60 << 20),
    )(tok, cot, wq, wo, wg, wu, wd, w_key, w_value, gain1, ids)


def quarters_kernel(mine, everyone, ss, rs, ls):
    me = Place()
    greet([me.by_quarter(i) for i in (1, 2, 3)])
    slots = (me.quarter, 7 - me.quarter)
    copies = []
    for h in (0, 1):
        for d in (1, 2, 3):
            copies.append(send(mine.at[h], everyone.at[slots[h]], (ss, rs), h * 4 + d, me.by_quarter(d)))
    local = [pltpu.make_async_copy(mine.at[h], everyone.at[slots[h]], ls.at[h]) for h in (0, 1)]
    for c in copies + local:
        c.start()
    for c in copies + local:
        c.wait()


def quarters_gather(mine, cid):
    dma = pltpu.SemaphoreType.DMA
    return pl.pallas_call(
        quarters_kernel, out_shape=jax.ShapeDtypeStruct((8,) + mine.shape[1:], mine.dtype),
        in_specs=[ANY], out_specs=ANY, scratch_shapes=[dma((8,)), dma((8,)), dma((2,))],
        compiler_params=pltpu.CompilerParams(collective_id=cid, has_side_effects=True),
    )(mine)


def quarters_back_kernel(parts, got, ss, rs):
    me = Place()
    greet([me.by_quarter(i) for i in (1, 2, 3)])
    copies = []
    for d in (1, 2, 3):
        q = (me.quarter + d) % 4
        for h, slot in ((0, q), (1, 7 - q)):
            copies.append(send(parts.at[slot], got.at[d - 1, h], (ss, rs), h * 4 + d, me.by_quarter(d)))
    for c in copies:
        c.start()
    for c in copies:
        c.wait()


def quarters_back(parts, cid):
    dma = pltpu.SemaphoreType.DMA
    return pl.pallas_call(
        quarters_back_kernel, out_shape=jax.ShapeDtypeStruct((3, 2) + parts.shape[1:], parts.dtype),
        in_specs=[ANY], out_specs=ANY, scratch_shapes=[dma((8,)), dma((8,))],
        compiler_params=pltpu.CompilerParams(collective_id=cid, has_side_effects=True),
    )(parts)


def return_kernel(pieces, home, ss, rs, ls):
    me = Place()
    greet([me.by_quarter(i) for i in (1, 2, 3)])

    def piece(q):
        half, block = q // 2, q % 2
        row = jnp.where(half == 0, me.quarter, 3 - me.quarter)
        return pieces.at[half, block], home.at[pl.ds(pl.multiple_of(row * CHUNK, CHUNK), CHUNK)]

    copies = []
    for d in (1, 2, 3):
        src, dst = piece((me.quarter + d) % 4)
        copies.append(send(src, dst, (ss, rs), d, me.by_quarter(d)))
    src, dst = piece(me.quarter)
    copies.append(pltpu.make_async_copy(src, dst, ls))
    for c in copies:
        c.start()
    for c in copies:
        c.wait()


def return_home(pieces, cid):
    dma = pltpu.SemaphoreType.DMA
    return pl.pallas_call(
        return_kernel, out_shape=jax.ShapeDtypeStruct((1024, 256), pieces.dtype),
        in_specs=[ANY], out_specs=ANY, scratch_shapes=[dma((4,)), dma((4,)), dma],
        compiler_params=pltpu.CompilerParams(collective_id=cid, has_side_effects=True),
    )(pieces)


def x_scatter_kernel(parts, got, ss, rs):
    me = Place()
    greet([me.by_x(i) for i in (1, 2, 3)])
    copies = [send(parts.at[(me.x + d) % 4], got.at[d - 1], (ss, rs), d, me.by_x(d)) for d in (1, 2, 3)]
    for c in copies:
        c.start()
    for c in copies:
        c.wait()


def x_scatter(parts, cid):
    dma = pltpu.SemaphoreType.DMA
    got = pl.pallas_call(
        x_scatter_kernel, out_shape=jax.ShapeDtypeStruct((3,) + parts.shape[1:], parts.dtype),
        in_specs=[ANY], out_specs=ANY, scratch_shapes=[dma((4,)), dma((4,))],
        compiler_params=pltpu.CompilerParams(collective_id=cid, has_side_effects=True),
    )(parts)
    own = lax.dynamic_index_in_dim(parts, lax.axis_index("col") % 4, 0, keepdims=False)
    return own.astype(F32) + jnp.sum(got.astype(F32), 0)


def x_gather_kernel(mine, full, ss, rs, ls):
    me = Place()
    greet([me.by_x(1), me.by_x(3)])
    local = pltpu.make_async_copy(mine, full.at[me.x], ls)
    local.start()
    local.wait()
    one, two = ring_gather(me, full, (ss, rs))
    for c in one:
        c.start()
    for a, b in zip(one, two):
        a.wait_recv()
        b.start()
    for a in one:
        a.wait_send()
    for b in two:
        b.wait()


def x_gather(mine, cid):
    dma = pltpu.SemaphoreType.DMA
    return pl.pallas_call(
        x_gather_kernel, out_shape=jax.ShapeDtypeStruct((4,) + mine.shape, mine.dtype),
        in_specs=[pl.BlockSpec(memory_space=pltpu.VMEM)], out_specs=ANY, scratch_shapes=[dma((4,)), dma((4,)), dma],
        compiler_params=pltpu.CompilerParams(collective_id=cid, has_side_effects=True),
    )(mine)


def core_kernel(count, *refs):
    me = Place()
    greet([me.partner()])
    parts, got, ss, rs = refs[:count], refs[count:2 * count], refs[-2], refs[-1]
    copies = [send(p.at[1 - me.core], g, (ss, rs), n, me.partner()) for n, (p, g) in enumerate(zip(parts, got))]
    for c in copies:
        c.start()
    for c in copies:
        c.wait()


def line_kernel(axes, *refs):
    me = Place()
    greet([me.by_z(i) for i in (1, 2, 3)] + [me.by_y(i) for i in (1, 2, 3)])
    count = len(axes)
    parts, got, ss, rs = refs[:count], refs[count:2 * count], refs[-2], refs[-1]
    copies = []
    for n, (p, g) in enumerate(zip(parts, got)):
        for d in (1, 2, 3):
            if axes[n] == "z":
                copies.append(send(p.at[(me.z + d) % 4], g.at[d - 1], (ss, rs), n * 4 + d, me.by_z(d)))
            else:
                copies.append(send(p.at[(me.y + d) % 4], g.at[d - 1], (ss, rs), n * 4 + d, me.by_y(d)))
    for c in copies:
        c.start()
    for c in copies:
        c.wait()


def scatter_grads(grads, first_z, cid):
    count = len(grads)
    dma = pltpu.SemaphoreType.DMA
    params = dict(in_specs=[ANY] * count, out_specs=[ANY] * count)
    me = Place()
    got = pl.pallas_call(
        functools.partial(core_kernel, count),
        out_shape=[jax.ShapeDtypeStruct(g.shape[1:], BF16) for g in grads],
        scratch_shapes=[dma((count,)), dma((count,))],
        compiler_params=pltpu.CompilerParams(collective_id=cid, has_side_effects=True), **params,
    )(*grads)
    sums = []
    for g, h, fz in zip(grads, got, first_z):
        s = lax.dynamic_index_in_dim(g, me.core, 0, keepdims=False).astype(F32) + h.astype(F32)
        s = s.astype(BF16)
        sums.append(s if fz else jnp.swapaxes(s, 0, 1))
    for step in (0, 1):
        axes = tuple("z" if fz == (step == 0) else "y" for fz in first_z)
        got = pl.pallas_call(
            functools.partial(line_kernel, axes),
            out_shape=[jax.ShapeDtypeStruct((3,) + s.shape[1:], BF16) for s in sums],
            scratch_shapes=[dma((4 * count,)), dma((4 * count,))],
            compiler_params=pltpu.CompilerParams(collective_id=cid + 1 + step, has_side_effects=True), **params,
        )(*sums)
        new = []
        for s, h, axis in zip(sums, got, axes):
            own = lax.dynamic_index_in_dim(s, me.z if axis == "z" else me.y, 0, keepdims=False)
            total = own.astype(F32) + jnp.sum(h.astype(F32), 0)
            new.append(total.astype(BF16) if step == 0 else total)
        sums = new
    return sums


def angles(positions, half):
    freq = jnp.exp(-math.log(10000.0) * jnp.arange(half, dtype=jnp.float32) / half)
    turned = positions.astype(jnp.float32)[:, None] * freq[None, :]
    return (jnp.cos(turned), jnp.sin(turned))


def rotate(values, cosine, sine, sign):
    count = values.shape[0]
    parts = values.reshape(count, -1, 2, cosine.shape[1])
    first = parts[:, :, 0]
    second = parts[:, :, 1]
    cos_b = cosine[:, None, :]
    sin_b = sine[:, None, :] * sign
    return jnp.stack([first * cos_b - second * sin_b, second * cos_b + first * sin_b], 2).reshape(
        values.shape
    )


def flat(full):
    return full.transpose(1, 0, 2).reshape(T, 2048)


def blocks(value):
    return value.reshape(T, 4, 512).transpose(1, 0, 2)


def norm_back(partial_value, rows_f, rstd, gain):
    scaled = partial_value * gain
    inner = jnp.sum(scaled * rows_f, -1, keepdims=True)
    term = rstd * scaled - rows_f * (rstd * rstd * rstd / rows_f.shape[1]) * inner
    gain_grad = jnp.sum(partial_value * rows_f * rstd, 0)
    return term, gain_grad


def by_row(value, cols):
    v = value.reshape(2, 2, 2, 2, 128, cols)
    return v.transpose(3, 2, 0, 1, 4, 5).reshape(2, 4, 2, 128, cols)


def by_row_cols(value, rows):
    v = value.reshape(rows, 2, 2, 2, 2, 128)
    return v.transpose(4, 3, 1, 2, 0, 5).reshape(2, 4, 2, rows, 128)


def to_device_order(vector):
    return vector.reshape(2, 4, 256).transpose(1, 0, 2).reshape((2048,) + vector.shape[1:])


def shards(tokens, segment_ids, norm_one, w_query, w_key, w_value, w_out, norm_two, w_gate, w_up, w_down, cotangent):
    me = Place()
    x = me.x
    ids = segment_ids.reshape(8, 16, 128)
    (xf, cf, mf, q_w, o_w, g_w, u_w, d_w, qt, kvt, lse, ot, stream, normed_one, rstd_one) = forward(
        tokens, cotangent, w_query, w_out, w_gate, w_up, w_down, w_key, w_value, norm_one.reshape(1, 2048), ids
    )

    def kv_cols(w):
        w = w.reshape(2, 4, 256, 2, 2, 64)
        w = lax.dynamic_index_in_dim(w, x // 2, 4, keepdims=False)
        return w.transpose(1, 0, 2, 3, 4).reshape(2048, 128)

    kv_w = jnp.concatenate([kv_cols(w_key), kv_cols(w_value)], 1)
    gain_one = to_device_order(norm_one.astype(F32))
    gain_two = to_device_order(norm_two.astype(F32))

    seq = me.z * 2 + me.yh
    seq_ids = lax.dynamic_slice_in_dim(segment_ids, seq * 2048, 2048).reshape(8, CHUNK)
    i = me.quarter
    chunk_at = jnp.stack([i, 7 - i])
    own_ids = jnp.concatenate([lax.dynamic_index_in_dim(seq_ids, i, 0, False), lax.dynamic_index_in_dim(seq_ids, 7 - i, 0, False)])
    place = (chunk_at[:, None] * CHUNK + jnp.arange(CHUNK, dtype=jnp.int32)[None]).reshape(T)
    seq_ids = seq_ids.reshape(2048)
    before = jnp.sum((seq_ids[None, :] < own_ids[:, None]).astype(jnp.int32), 1)
    cosine, sine = angles(place - before, HEAD // 2)
    allowed = (own_ids[:, None] == seq_ids[None, :]) & (jnp.arange(2048)[None, :] <= place[:, None])
    inputs_f = xf.astype(F32)
    queries = (qt * 8).T
    kv_all = kvt.transpose(0, 2, 1).reshape(2048, 256)

    def key_of(head):
        return kv_all[:, (head // 4) * 64:(head // 4 + 1) * 64]

    def value_of(head):
        return kv_all[:, 128 + (head // 4) * 64:128 + (head // 4 + 1) * 64]

    logs = [lse[:, head].reshape(T, 1) for head in range(8)]
    attended = ot.T
    own_tok = lax.dynamic_slice_in_dim(xf, x * 512, 512, 1).astype(F32)
    own_cot = lax.dynamic_slice_in_dim(cf, x * 512, 512, 1).astype(F32)
    middle_f = mf.astype(F32)
    cot_rows = cf
    rstd_two = lax.rsqrt(jnp.mean(middle_f * middle_f, -1, keepdims=True) + eps)
    normed_two = (middle_f * rstd_two * gain_two).astype(BF16)

    feed = 0.0
    d_normed_two = 0.0
    g_gate, g_up, g_down = [], [], []
    for b in (0, 1):
        gate = dot_plain(normed_two, g_w[b])
        up = dot_plain(normed_two, u_w[b])
        sigma = jax.nn.sigmoid(gate)
        active = gate * sigma
        hidden = (active * up).astype(BF16)
        feed = feed + dot_plain(hidden, d_w[b])
        d_hidden = dot_nt(cot_rows, d_w[b])
        g_down.append(dot_tn(hidden, cot_rows).astype(BF16))
        d_gate = (d_hidden * up * sigma * (1.0 + gate * (1.0 - sigma))).astype(BF16)
        d_up = (d_hidden * active).astype(BF16)
        g_gate.append(dot_tn(normed_two, d_gate).astype(BF16))
        g_up.append(dot_tn(normed_two, d_up).astype(BF16))
        d_normed_two = d_normed_two + dot_nt(d_gate, g_w[b]) + dot_nt(d_up, u_w[b])
    result = stream + x_scatter(blocks(feed.astype(BF16)), 4)
    mixed = return_home(result.astype(BF16).reshape(2, CHUNK, 2, 256).transpose(0, 2, 1, 3), 5)
    term_two, gain_two_grad = norm_back(d_normed_two, middle_f, rstd_two, gain_two)
    d_stream = own_cot + x_scatter(blocks(term_two.astype(BF16)), 6)
    d_rows = flat(x_gather(d_stream.astype(BF16), 7))
    d_attended = dot_nt(d_rows, o_w).astype(BF16)
    g_out = dot_tn(attended, d_rows).astype(BF16)

    dq_list, dk_list, dv_list = [], [0.0, 0.0], [0.0, 0.0]
    for head in range(8):
        qh = queries[:, head * HEAD:(head + 1) * HEAD]
        gh = d_attended[:, head * HEAD:(head + 1) * HEAD]
        s = jnp.where(allowed, dot_nt(qh, key_of(head)) * 0.125, -1e30)
        p = jnp.where(allowed, jnp.exp(s - logs[head]), 0.0)
        dp = dot_nt(gh, value_of(head))
        delta = jnp.sum(p * dp, 1, keepdims=True)
        ds = (p * (dp - delta) * 0.125).astype(BF16)
        dq_list.append(dot_plain(ds, key_of(head)))
        dk_list[head // 4] = dk_list[head // 4] + dot_tn(ds, qh)
        dv_list[head // 4] = dv_list[head // 4] + dot_tn(p.astype(BF16), gh)
    dkv = jnp.concatenate(dk_list + dv_list, 1).reshape(8, CHUNK, 256)
    got = quarters_back(dkv.astype(BF16), 8)
    own = jnp.stack([lax.dynamic_index_in_dim(dkv, i, 0, False), lax.dynamic_index_in_dim(dkv, 7 - i, 0, False)])
    dkv = (own + jnp.sum(got.astype(F32), 0)).reshape(T, 256)
    dq_pre = rotate(jnp.concatenate(dq_list, 1), cosine, sine, -1.0).astype(BF16)
    dkv_pre = jnp.concatenate([rotate(dkv[:, :128], cosine, sine, -1.0), dkv[:, 128:]], 1).astype(BF16)
    g_query = dot_tn(normed_one, dq_pre).astype(BF16)
    g_kv = dot_tn(normed_one, dkv_pre).astype(BF16)
    d_normed_one = dot_nt(dq_pre, q_w) + dot_nt(dkv_pre, kv_w)
    term_one, gain_one_grad = norm_back(d_normed_one, inputs_f, rstd_one, gain_one)
    d_tokens = d_stream + x_scatter(blocks(term_one.astype(BF16)), 9)
    input_grad = return_home(d_tokens.reshape(2, CHUNK, 2, 256).transpose(0, 2, 1, 3), 10)

    def with_y(v):
        return v.reshape((2, 4, 4) + v.shape[4:])

    gq = with_y(by_row(g_query, 512).reshape(2, 4, 2, 128, 2, 256).transpose(0, 1, 2, 4, 3, 5))
    go = with_y(by_row_cols(g_out, 512).reshape(2, 4, 2, 2, 256, 128))
    ff = w_gate.shape[1]
    gg, gu = [with_y(jnp.stack([by_row(v, ff) for v in gs], 3)) for gs in (g_gate, g_up)]
    gd = with_y(jnp.stack([by_row_cols(v, ff) for v in g_down], 3))
    gkv = with_y(by_row(g_kv, 256).reshape(2, 4, 2, 2, 64, 256))
    query_s, out_s, gate_s, up_s, down_s, kv_s = scatter_grads(
        [gq, go, gg, gu, gd, gkv], (True, True, True, False, False, True), 11
    )
    shape = (2048, 256)
    pos = ((me.z // 2) * 4 + (me.z % 2) * 2 + me.yh) * 256 + me.core * 128 + me.yl * 64
    empty = jnp.zeros((2048, 4, 64), F32)
    kv_s = kv_s.reshape(64, 4, 64)

    def spread(pair):
        part = lax.dynamic_update_slice(jnp.zeros((64, 4, 64), F32), pair[:, 0:1], (0, x // 2, 0))
        part = lax.dynamic_update_slice(part, pair[:, 1:2], (0, 2 + x // 2, 0))
        return lax.dynamic_update_slice(empty, part, (pos, 0, 0)).reshape(shape)

    stats = jnp.stack([jnp.sum(own_tok * own_tok), jnp.sum(stream * stream), jnp.sum(result * result)])
    key_total, value_total = lax.psum((spread(kv_s[:, :2]), spread(kv_s[:, 2:])), ("row", "col"))
    one_total, two_total, stat_total = lax.psum((gain_one_grad, gain_two_grad, stats), ("row", "col"))

    def from_device_order(v):
        return v.reshape(4, 2, 256).transpose(1, 0, 2).reshape(2048)

    rms = jnp.sqrt(stat_total / (16384 * 2048))
    return (
        mixed, input_grad, query_s, key_total, value_total, out_s, gate_s, up_s, down_s,
        from_device_order(one_total), from_device_order(two_total), rms,
    )


def solution(mesh):
    return jax.shard_map(
        shards,
        mesh=mesh,
        in_specs=(
            P("row", "col"), P(), P(), P("row", "col"), P(), P(), P("col", "row"), P(),
            P("row", "col"), P("row", "col"), P("col", "row"), P("row", "col"),
        ),
        out_specs=(
            P("row", "col"), P("row", "col"), P("row", "col"), P(), P(), P("col", "row"),
            P("row", "col"), P("row", "col"), P("col", "row"), P(), P(), P(),
        ),
        check_vma=False,
    )
```

```python
import functools
import math

import jax
import jax.numpy as jnp
from jax import lax
from jax.experimental import pallas as pl
from jax.experimental.pallas import tpu as pltpu
from jax.sharding import PartitionSpec as P

BF16 = jnp.bfloat16
F32 = jnp.float32
HEAD = 64
eps = 1e-05
MESH = pl.DeviceIdType.MESH
ANY = pl.BlockSpec(memory_space=pl.ANY)
CHUNK = 256
T = 512


class Place:
    def __init__(self):
        row = lax.axis_index("row")
        col = lax.axis_index("col")
        self.z = row // 4
        self.yh = (row // 2) % 2
        self.core = row % 2
        self.yl = col // 4
        self.x = col % 4
        self.y = self.yh * 2 + self.yl
        self.quarter = self.core * 2 + self.yl

    def at(self, z, y, core, x):
        return {"row": z * 4 + (y // 2) * 2 + core, "col": (y % 2) * 4 + x}

    def by_x(self, d):
        return self.at(self.z, self.y, self.core, (self.x + d) % 4)

    def by_z(self, d):
        return self.at((self.z + d) % 4, self.y, self.core, self.x)

    def by_y(self, d):
        return self.at(self.z, (self.y + d) % 4, self.core, self.x)

    def partner(self):
        return self.at(self.z, self.y, 1 - self.core, self.x)

    def by_quarter(self, d):
        q = (self.quarter + d) % 4
        return self.at(self.z, self.yh * 2 + q % 2, q // 2, self.x)


def greet(peers):
    barrier = pltpu.get_barrier_semaphore()
    for peer in peers:
        pl.semaphore_signal(barrier, inc=1, device_id=peer, device_id_type=MESH)
    pl.semaphore_wait(barrier, len(peers))


def send(src, dst, sems, k, peer):
    return pltpu.make_async_remote_copy(
        src_ref=src, dst_ref=dst, send_sem=sems[0].at[k], recv_sem=sems[1].at[k],
        device_id=peer, device_id_type=MESH,
    )


def each(count, act):
    def step(i, carry):
        act(i)
        return carry

    lax.fori_loop(0, count, step, 0)


def perm_row(z, y, core):
    yh = y // 2
    return ((z % 2) * 2 + yh) * 512 + (z // 2) * 256 + core * 128


def reshard_in(me, src, full, sems, base, lsem):
    def chunk(q):
        return src.at[pl.ds(pl.multiple_of(jnp.where(me.core == 0, q, 3 - q) * CHUNK, CHUNK), CHUNK)]

    half = pl.multiple_of(me.core * CHUNK, CHUNK)
    place = full.at[pl.ds(half, CHUNK), pl.ds(pl.multiple_of(me.x * 512 + me.yl * 256, 256), 256)]
    copies = []
    for d in (1, 2, 3):
        copies.append(send(chunk((me.quarter + d) % 4), place, sems, base + d, me.by_quarter(d)))
    local = pltpu.make_async_copy(chunk(me.quarter), place, lsem)
    return copies, local


class Spread:
    def __init__(self, me, src, slot, z_first, sems, lsem):
        self.me, self.src, self.slot, self.z_first, self.sems, self.lsem = me, src, slot, z_first, sems, lsem

    def local(self):
        me = self.me
        return pltpu.make_async_copy(self.src, self.slot(me.z, me.y, me.core), self.lsem)

    def first(self, i):
        me = self.me
        peer = me.by_z(i + 1) if self.z_first else me.by_y(i + 1)
        return send(self.src, self.slot(me.z, me.y, me.core), self.sems, i, peer)

    def line(self, k):
        me = self.me
        if self.z_first:
            return self.slot((me.z + 4 - k) % 4, me.y, me.core)
        return self.slot(me.z, (me.y + 4 - k) % 4, me.core)

    def second(self, k, i):
        me = self.me
        peer = me.by_y(i + 1) if self.z_first else me.by_z(i + 1)
        block = self.line(k)
        return send(block, block, self.sems, 3 + k * 3 + i, peer)

    def third(self, i):
        me = self.me
        if self.z_first:
            block = self.slot((me.z + 4 - i // 4) % 4, (me.y + 4 - i % 4) % 4, me.core)
        else:
            block = self.slot((me.z + 4 - i % 4) % 4, (me.y + 4 - i // 4) % 4, me.core)
        return send(block, block, self.sems, 15 + i, me.partner())

    def start(self):
        self.local().start()
        each(3, lambda i: self.first(i).start())

    def turn(self):
        self.local().wait()
        each(3, lambda i: self.second(0, i).start())
        self.third(0).start()

        def arrived(k):
            self.first(k).wait_recv()
            each(3, lambda i: self.second(k + 1, i).start())
            self.third((k + 1) * 4).start()

        each(3, arrived)

    def cross(self):
        def arrived(j):
            k, i = j // 3, j % 3
            self.second(k, i).wait_recv()
            self.third(k * 4 + i + 1).start()

        each(12, arrived)

    def finish(self):
        each(16, lambda i: self.third(i).wait_recv())
        each(3, lambda i: self.first(i).wait_send())
        each(12, lambda j: self.second(j // 3, j % 3).wait_send())
        each(16, lambda i: self.third(i).wait_send())


def weight_slots(q, o, g, u, d):
    def ds(start, size):
        return pl.ds(pl.multiple_of(start, 128), size)

    return (
        lambda z, y, c: q.at[ds(perm_row(z, y, c), 128), ds((y % 2) * 256, 256)],
        lambda z, y, c: o.at[ds((y % 2) * 256, 256), ds(perm_row(z, y, c), 128)],
        lambda z, y, c: g.at[y % 2, ds(perm_row(z, y, c), 128)],
        lambda z, y, c: u.at[y % 2, ds(perm_row(z, y, c), 128)],
        lambda z, y, c: d.at[y % 2, :, ds(perm_row(z, y, c), 128)],
    )


def dot_plain(left, right):
    return jnp.dot(left, right, preferred_element_type=F32)


def dot_tn(left, right):
    return lax.dot_general(left, right, (((0,), (0,)), ((), ())), preferred_element_type=F32)


def dot_nt(left, right):
    return lax.dot_general(left, right, (((1,), (1,)), ((), ())), preferred_element_type=F32)


def lanes(start, size):
    return pl.ds(pl.multiple_of(start, 128), size)


class Ring:
    def __init__(self, me, full, rows, sems, base):
        x = me.x
        right, left = me.by_x(1), me.by_x(3)
        xl, xr = (x + 3) % 4, (x + 1) % 4

        def at(b, off, size):
            return full.at[rows, lanes(b * 512 + off, size)]

        self.one = [
            send(at(x, 0, 512), at(x, 0, 512), sems, base + 0, right),
            send(at(x, 0, 512), at(x, 0, 512), sems, base + 1, left),
        ]
        self.two = [
            send(at(xl, 0, 256), at(xl, 0, 256), sems, base + 2, right),
            send(at(xr, 256, 256), at(xr, 256, 256), sems, base + 3, left),
        ]

    def start(self):
        for c in self.one:
            c.start()

    def turn(self):
        for a, b in zip(self.one, self.two):
            a.wait_recv()
            b.start()

    def finish(self):
        for a in self.one:
            a.wait_send()
        for b in self.two:
            b.wait()


class RingSum:
    def __init__(self, me, part, rows, hop, got, sems, base):
        x = me.x
        self.part, self.rows, self.hop, self.got, self.x = part, rows, hop, got, x
        right, left = me.by_x(1), me.by_x(3)
        far, xr, xl = (x + 2) % 4, (x + 1) % 4, (x + 3) % 4
        self.xr, self.xl = xr, xl

        def at(b, off):
            return part.at[rows, lanes(b * 512 + off, 256)]

        self.one = [
            send(at(far, 0), hop.at[0], sems, base + 0, right),
            send(at(far, 256), hop.at[1], sems, base + 1, left),
            send(at(xr, 256), got.at[0, :, pl.ds(256, 256)], sems, base + 2, right),
            send(at(xl, 0), got.at[1, :, pl.ds(0, 256)], sems, base + 3, left),
        ]
        self.two = [
            send(at(xr, 0), got.at[0, :, pl.ds(0, 256)], sems, base + 4, right),
            send(at(xl, 256), got.at[1, :, pl.ds(256, 256)], sems, base + 5, left),
        ]

    def start(self):
        for c in self.one:
            c.start()

    def turn(self):
        for k, (b, off) in enumerate(((self.xr, 0), (self.xl, 256))):
            self.one[k].wait_recv()
            cols = lanes(b * 512 + off, 256)
            total = self.part[self.rows, cols].astype(F32) + self.hop[k].astype(F32)
            self.part[self.rows, cols] = total.astype(BF16)
            self.two[k].start()

    def finish(self):
        for k in (2, 3):
            self.one[k].wait_recv()
        for c in self.two:
            c.wait_recv()
        own = self.part[self.rows, lanes(self.x * 512, 512)].astype(F32)
        return own + self.got[0].astype(F32) + self.got[1].astype(F32)

    def drain(self):
        for c in self.one + self.two:
            c.wait_send()


def rope_rows(a, b, cosine, sine):
    return a * cosine - b * sine, b * cosine + a * sine


def document_starts(ids, seq, place):
    ids = ids[seq]

    def below(number):
        hit = (ids < number).astype(F32)
        return jnp.sum(jnp.sum(hit, 1, keepdims=True), 0, keepdims=True)

    second, third = below(3 * seq + 1).astype(jnp.int32), below(3 * seq + 2).astype(jnp.int32)
    return jnp.where(place >= third, third, jnp.where(place >= second, second, 0))


ORIGINAL = [(p % 2) * 4 + p // 2 for p in range(8)]


def device_order_row(ref):
    return jnp.concatenate([ref[:, b * 256:(b + 1) * 256].astype(F32) for b in ORIGINAL], 1)


def rms_rows(src, gain, dst, rstd, first, count):
    def step(k, carry):
        rows = pl.ds(pl.multiple_of(first + k * 64, 64), 64)
        v = src[rows, :].astype(F32)
        r = lax.rsqrt(jnp.sum(v * v, 1, keepdims=True) * (1.0 / 2048.0) + eps)
        rstd[rows, :] = r
        dst[rows, :] = (v * r * gain).astype(BF16)
        return carry

    lax.fori_loop(0, count // 64, step, 0)


def column_squares(value):
    return jnp.sum(value * value, 0, keepdims=True)


class GradSum:
    def __init__(self, me, own, land, out, rows, halves, sems, base):
        self.me, self.own, self.land, self.out, self.rows, self.halves = me, own, land, out, rows, halves
        self.sems, self.base = sems, base

    def first(self, i):
        me = self.me
        return send(self.own((me.z + 1 + i // 2) % 4, i % 2), self.land(i), self.sems, self.base + i, me.by_z(1 + i // 2))

    def start(self):
        each(6, lambda i: self.first(i).start())

    def add(self, view, others):
        def step(k, carry):
            rows = pl.ds(pl.multiple_of(k * 64, 64), 64)
            total = view[rows, :].astype(F32)
            for other in others:
                total = total + other[rows, :].astype(F32)
            view[rows, :] = total.astype(BF16)
            return carry

        lax.fori_loop(0, self.rows // 64, step, 0)

    def sum_z(self):
        each(6, lambda i: self.first(i).wait_recv())
        for yh in (0, 1):
            self.add(self.own(self.me.z, yh), [self.land(d * 2 + yh) for d in range(3)])
        each(6, lambda i: self.first(i).wait_send())

    def second(self, yh):
        me = self.me
        to = yh * 2 + me.core
        step = (to + 4 - me.y) % 4
        slot = (step + 3) % 4
        copy = pltpu.make_async_remote_copy(
            src_ref=self.own(me.z, yh), dst_ref=self.land(slot), send_sem=self.sems[0].at[self.base + 6 + yh],
            recv_sem=self.sems[1].at[self.base + 6 + slot], device_id=me.at(me.z, to, me.core, me.x), device_id_type=MESH,
        )
        return step, copy

    def send_y(self):
        for yh in (0, 1):
            step, copy = self.second(yh)
            pl.when(step != 0)(copy.start)

    def last(self):
        me = self.me
        view = self.halves(self.own(me.z, me.yh), 1 - me.core)
        return send(view, self.out, self.sems, self.base + 9, me.partner())

    def keep(self):
        me = self.me
        return pltpu.make_async_copy(self.halves(self.own(me.z, me.yh), me.core), self.out, self.sems[0].at[self.base + 10])

    def sum_y(self):
        me = self.me

        def work():
            for slot in range(3):
                pltpu.make_async_remote_copy(
                    src_ref=self.land(slot), dst_ref=self.land(slot), send_sem=self.sems[0].at[self.base + 8],
                    recv_sem=self.sems[1].at[self.base + 6 + slot], device_id=me.partner(), device_id_type=MESH,
                ).wait_recv()
            self.add(self.own(me.z, me.yh), [self.land(slot) for slot in range(3)])
            self.last().start()
            self.keep().start()

        pl.when(me.yl == me.core)(work)

    def finish(self):
        me = self.me

        def sender():
            self.last().wait_send()
            self.keep().wait()

        pl.when(me.yl == me.core)(sender)
        pl.when(me.yl != me.core)(lambda: self.last().wait_recv())
        for yh in (0, 1):
            step, copy = self.second(yh)
            pl.when(step != 0)(copy.wait_send)


def layer_kernel(
    tok, cot, wq_s, wo_s, wg_s, wu_s, wd_s, w_key, w_value, gain1, gain2, ids,
    o_mixed, o_in, o_q, o_out, o_gate, o_up, o_down, o_kv, o_small, xs,
    xf, cf, mf, h1, h2p, cfp, wq, wo, wg, wu, wd, qt, ot, o_r, kvt, x1, dx1, part, hop, got, acc, mx, sm, lse, delta,
    hid, dg, du, hp, dhf, r1, r2, mix, gains, squares, small, small_r,
    a_s, a_r, w_s, w_r, lsem, hs,
):
    me = Place()
    x, core = me.x, me.core
    h2, kv_tmp = xf, dx1
    acts = (a_s, a_r)
    count = [0]

    def sems(n):
        count[0] += n
        assert count[0] <= ACTS
        return count[0] - n

    def shake(k, peers):
        for peer in peers:
            pl.semaphore_signal(hs.at[k], inc=1, device_id=peer, device_id_type=MESH)

    def unshake(k, peers):
        pl.semaphore_wait(hs.at[k], len(peers))

    xs_line = [me.by_x(i) for i in (1, 2, 3)]
    ys_line = [me.by_y(i) for i in (1, 2, 3)]
    zs_line = [me.by_z(i) for i in (1, 2, 3)]
    four = [me.by_quarter(i) for i in (1, 2, 3)]
    partner = me.partner()
    greet(xs_line + ys_line + zs_line + four)
    slots = weight_slots(wq, wo, wg, wu, wd)
    first_z = (True, True, True, False, False)
    spreads = [
        Spread(me, src, slots[n], first_z[n], (w_s.at[n], w_r.at[n]), lsem.at[2 + n])
        for n, src in enumerate((wq_s, wo_s, wg_s, wu_s, wd_s))
    ]
    in_copies, in_local = reshard_in(me, tok, xf, acts, sems(4), lsem.at[0])
    cot_copies, cot_local = reshard_in(me, cot, cf, acts, sems(4), lsem.at[1])
    for c in in_copies + [in_local]:
        c.start()
    for s in spreads:
        s.start()
    for c in cot_copies + [cot_local]:
        c.start()
    seq = me.z * 2 + me.yh
    chunk_of = (me.quarter, 7 - me.quarter)
    lane = lax.broadcasted_iota(jnp.int32, (1, CHUNK), 1)
    places = [c * CHUNK + lane for c in chunk_of]
    starts = [document_starts(ids, seq, p) for p in places]
    pos = jnp.concatenate([p - s for p, s in zip(places, starts)], 1).astype(F32)
    turn = lax.broadcasted_iota(jnp.int32, (32, 1), 0).astype(F32)
    angle = jnp.exp(-math.log(10000.0) * turn / 32.0) * pos
    cosine, sine = jnp.cos(angle), jnp.sin(angle)
    gains[...] = jnp.zeros(gains.shape, F32)
    squares[...] = jnp.zeros(squares.shape, F32)
    small[...] = jnp.zeros(small.shape, F32)

    for c in in_copies:
        c.wait_recv()
    in_local.wait()
    ring_tok = Ring(me, xf, pl.ds(0, T), acts, sems(4))
    ring_tok.start()
    spreads[0].turn()
    spreads[1].turn()
    for c in cot_copies:
        c.wait_recv()
    cot_local.wait()
    ring_tok.turn()
    ring_cot = Ring(me, cf, pl.ds(0, T), acts, sems(4))
    ring_cot.start()
    spreads[0].cross()
    for s in spreads[2:]:
        s.turn()
    ring_tok.finish()
    for c in in_copies + cot_copies:
        c.wait_send()
    stash = pltpu.make_async_copy(xf, xs, lsem.at[7])
    stash.start()

    rms_rows(xf, device_order_row(gain1), h1, r1, 0, T)
    spreads[0].finish()
    for n, w in enumerate((w_key, w_value)):
        total = None
        for p, b in enumerate(ORIGINAL):
            d = dot_plain(h1[:, p * 256:(p + 1) * 256], w[b * 256:(b + 1) * 256, :])
            total = d if total is None else total + d
        kv_tmp[n * 256:(n + 1) * 256, :] = total.T
    heads = [pl.multiple_of((2 * g + x // 2) * HEAD, HEAD) for g in (0, 1)]
    for g in (0, 1):
        head = heads[g]
        a, b = rope_rows(kv_tmp[pl.ds(head, 32), :], kv_tmp[pl.ds(head + 32, 32), :], cosine, sine)
        v = kv_tmp[pl.ds(256 + head, HEAD), :]
        for h in (0, 1):
            cols = slice(h * CHUNK, (h + 1) * CHUNK)
            kvt[chunk_of[h], g * 64:g * 64 + 32, :] = a[:, cols].astype(BF16)
            kvt[chunk_of[h], g * 64 + 32:g * 64 + 64, :] = b[:, cols].astype(BF16)
            kvt[chunk_of[h], 128 + g * 64:192 + g * 64, :] = v[:, cols].astype(BF16)
    kv_copies = []
    base = sems(8)
    for h in (0, 1):
        for d in (1, 2, 3):
            block = kvt.at[chunk_of[h]]
            kv_copies.append(send(block, block, acts, base + h * 4 + d, me.by_quarter(d)))
    for c in kv_copies:
        c.start()
    for n in (0, 1):
        q = dot_plain(h1[...], wq[:, n * 256:(n + 1) * 256]).T
        for hd in range(4):
            at = hd * HEAD
            a, b = rope_rows(q[at:at + 32], q[at + 32:at + 64], cosine, sine)
            qt[n * 256 + at:n * 256 + at + 32, :] = (a * 0.125).astype(BF16)
            qt[n * 256 + at + 32:n * 256 + at + 64, :] = (b * 0.125).astype(BF16)
    ring_cot.turn()
    spreads[1].cross()
    for c in kv_copies:
        c.wait()

    def row_form(block):
        return block.astype(F32).T.astype(BF16)

    def allowed(h, j):
        at = lax.broadcasted_iota(jnp.int32, (CHUNK, CHUNK), 0) + j * CHUNK
        return (at >= starts[h]) & (at <= places[h])

    def attend_begin():
        mx[...] = jnp.full(mx.shape, -1e30, F32)
        sm[...] = jnp.zeros(sm.shape, F32)
        acc[...] = jnp.zeros(acc.shape, F32)

    def attend(h, low, high):
        cols = slice(h * CHUNK, (h + 1) * CHUNK)

        def step(j, carry):
            ok = allowed(h, j)
            keys = [row_form(kvt[j, g * 64:(g + 1) * 64, :]) for g in (0, 1)]
            for hd in range(8):
                g = hd // 4
                s = jnp.where(ok, dot_plain(keys[g], qt[hd * 64:(hd + 1) * 64, cols]), -1e30)
                old = mx[hd:hd + 1, :]
                new = jnp.maximum(old, jnp.max(s, 0, keepdims=True))
                p = jnp.exp(s - new)
                shrink = jnp.exp(old - new)
                mx[hd:hd + 1, :] = new
                sm[hd:hd + 1, :] = sm[hd:hd + 1, :] * shrink + jnp.sum(p, 0, keepdims=True)
                acc[hd * 64:(hd + 1) * 64, :] = acc[hd * 64:(hd + 1) * 64, :] * shrink + dot_plain(
                    kvt[j, 128 + g * 64:192 + g * 64, :], p.astype(BF16)
                )
            return carry

        lax.fori_loop(low, high, step, 0)

    def attend_end(h):
        cols = slice(h * CHUNK, (h + 1) * CHUNK)
        lse[h] = mx[...] + jnp.log(sm[...])
        for hd in range(8):
            rows = slice(hd * 64, (hd + 1) * 64)
            acc[rows, :] = acc[rows, :] / sm[hd:hd + 1, :]
        ot[:, cols] = acc[...].astype(BF16)
        o_r[cols, :] = acc[...].T.astype(BF16)

    def rows_of(h):
        return pl.ds(h * CHUNK, CHUNK)

    def project(h):
        rows = rows_of(h)

        def step(n, carry):
            cols = lanes(n * 256, 256)
            part[rows, cols] = dot_plain(o_r[rows, :], wo[:, cols]).astype(BF16)
            return carry

        lax.fori_loop(0, 8, step, 0)

    def ring_sums():
        return [RingSum(me, part, rows_of(h), hop.at[h], got.at[h], acts, sems(6)) for h in (0, 1)]

    def rings():
        return [Ring(me, mf, rows_of(h), acts, sems(4)) for h in (0, 1)]

    sums, ring = ring_sums(), rings()
    own = lanes(x * 512, 512)

    def stream(h):
        rows = rows_of(h)
        mine = xf[rows, own].astype(F32)
        total = mine + sums[h].finish()
        squares[0:1, :] += column_squares(mine)
        squares[1:2, :] += column_squares(total)
        x1[rows, :] = total
        mf[rows, own] = total.astype(BF16)

    attend_begin()
    attend(0, 0, chunk_of[0] + 1)
    attend_end(0)
    spreads[1].finish()
    project(0)
    sums[0].start()
    attend_begin()
    attend(1, 0, 3)
    sums[0].turn()
    for s in spreads[2:]:
        s.cross()
    attend(1, 3, chunk_of[1] + 1)
    attend_end(1)
    stream(0)
    ring[0].start()
    project(1)
    sums[1].start()
    ring[0].turn()
    sums[1].turn()
    stream(1)
    ring[1].start()
    ring_cot.finish()
    cot_over = send(cf, cfp, acts, sems(1), partner)
    cot_over.start()
    stash.wait()
    ring[0].finish()

    row_two = device_order_row(gain2)
    rms_rows(mf, row_two, h2, r2, 0, CHUNK)
    for s in spreads[2:]:
        s.finish()
    ring[1].turn()

    def feed_forward(h):
        rows = rows_of(h)

        def step(b, carry):
            for at, size in ((0, 256), (256, 256), (512, 192)):
                cols = slice(at, at + size)
                gate = dot_plain(h2[rows, :], wg[b, :, cols])
                up = dot_plain(h2[rows, :], wu[b, :, cols])
                d_hidden = dot_nt(cf[rows, :], wd[b, cols, :])
                sigma = 1.0 / (1.0 + jnp.exp(-gate))
                active = gate * sigma
                hid[b, rows, cols] = (active * up).astype(BF16)
                dg[b, rows, cols] = (d_hidden * up * sigma * (1.0 + gate * (1.0 - sigma))).astype(BF16)
                du[b, rows, cols] = (d_hidden * active).astype(BF16)
            return carry

        lax.fori_loop(0, 2, step, 0)

    def norm_back(h, u_ref, rstd, gain, k):
        def step(i, carry):
            at = pl.multiple_of(i * 64, 64)
            full = pl.ds(pl.multiple_of(h * CHUNK + i * 64, 64), 64)
            d = dhf[pl.ds(at, 64), :]
            u = u_ref[full, :].astype(F32)
            r = rstd[full, :]
            scaled = d * gain
            inner = jnp.sum(scaled * u, 1, keepdims=True)
            part[full, :] = (r * scaled - u * (r * r * r * (1.0 / 2048.0) * inner)).astype(BF16)
            gains[k:k + 1, :] += jnp.sum(d * u * r, 0, keepdims=True)
            return carry

        lax.fori_loop(0, CHUNK // 64, step, 0)

    def back_two(h):
        rows = rows_of(h)

        def step(n, carry):
            feats = lanes(n * 256, 256)
            total = dot_nt(dg[0, rows, :], wg[0, feats, :]) + dot_nt(dg[1, rows, :], wg[1, feats, :])
            total = total + dot_nt(du[0, rows, :], wu[0, feats, :]) + dot_nt(du[1, rows, :], wu[1, feats, :])
            dhf[:, feats] = total
            return carry

        lax.fori_loop(0, 8, step, 0)
        norm_back(h, mf, r2, row_two, 1)

    feed_forward(0)
    back_two_sums, ring_two = ring_sums(), rings()
    ring[1].finish()
    sums[0].drain()
    back_two(0)
    back_two_sums[0].start()
    rms_rows(mf, row_two, h2, r2, CHUNK, CHUNK)
    feed_forward(1)
    h2_over = send(h2, h2p, acts, sems(1), partner)
    h2_over.start()
    base = sems(3)
    hid_over = [send(ref.at[1 - core], hp.at[n], acts, base + n, partner) for n, ref in enumerate((hid, dg, du))]
    for c in hid_over:
        c.start()
    back_two_sums[0].turn()
    sums[1].drain()
    back_two(1)
    back_two_sums[1].start()

    def d_stream(h):
        rows = rows_of(h)
        total = cf[rows, own].astype(F32) + back_two_sums[h].finish()
        dx1[rows, :] = total
        mf[rows, own] = total.astype(BF16)

    d_stream(0)
    ring_two[0].start()
    h2_over.wait()
    for c in hid_over:
        c.wait()
    cot_over.wait()

    def feed(h):
        rows = rows_of(h)

        def step(n, carry):
            cols = lanes(n * 256, 256)
            part[rows, cols] = (dot_plain(hid[0, rows, :], wd[0, :, cols]) + dot_plain(hid[1, rows, :], wd[1, :, cols])).astype(BF16)
            return carry

        lax.fori_loop(0, 8, step, 0)

    def grads_in(low, high):
        def step(m, carry):
            feats = lanes(m * 256, 256)
            mine = h2[:, feats].T
            other = h2p[:, feats].T
            wg[core, feats, :] = (dot_plain(mine, dg[core]) + dot_plain(other, hp[1])).astype(BF16)
            wu[core, feats, :] = (dot_plain(mine, du[core]) + dot_plain(other, hp[2])).astype(BF16)
            return carry

        lax.fori_loop(low, high, step, 0)

    grads_in(0, 4)
    back_two_sums[1].turn()
    ring_two[0].turn()
    back_two_sums[0].drain()
    feed_sums = ring_sums()
    feed(0)
    feed_sums[0].start()
    grads_in(4, 8)
    d_stream(1)
    ring_two[1].start()
    ring_two[0].finish()
    back_two_sums[1].drain()
    ring_two[1].turn()
    feed(1)
    feed_sums[1].start()
    feed_sums[0].turn()

    for at, size in ((0, 256), (256, 256), (512, 192)):
        mine = hid[core, :, at:at + size].T
        other = hp[0, :, at:at + size].T

        def down(n, carry):
            cols = lanes(n * 512, 512)
            wd[core, at:at + size, cols] = (dot_plain(mine, cf[:, cols]) + dot_plain(other, cfp[:, cols])).astype(BF16)
            return carry

        lax.fori_loop(0, 4, down, 0)

    shake(0, zs_line + ys_line + four)
    unstash = pltpu.make_async_copy(xs, cf, lsem.at[7])
    unstash.start()

    def d_attended(h):
        cols = slice(h * CHUNK, (h + 1) * CHUNK)
        rows = rows_of(h)
        for k in (0, 1):
            feats = slice(k * 256, (k + 1) * 256)
            d = dot_nt(wo[feats, :], mf[rows, :])
            o_r[feats, cols] = d.astype(BF16)
            both = d.astype(BF16).astype(F32) * ot[feats, cols].astype(F32)
            for hd in range(4):
                delta[h, k * 4 + hd:k * 4 + hd + 1, :] = jnp.sum(both[hd * 64:(hd + 1) * 64], 0, keepdims=True)

    def attend_back(h, low, high):
        cols = slice(h * CHUNK, (h + 1) * CHUNK)

        def step(j, carry):
            ok = allowed(h, j)
            keys_at = lanes(j * CHUNK, CHUNK)
            for g in (0, 1):
                key_t = kvt[j, g * 64:(g + 1) * 64, :]
                key, value = row_form(key_t), row_form(kvt[j, 128 + g * 64:192 + g * 64, :])
                ps, ds = [], []
                for hd in range(4 * g, 4 * g + 4):
                    feats = slice(hd * 64, (hd + 1) * 64)
                    s = jnp.where(ok, dot_plain(key, qt[feats, cols]), -1e30)
                    p = jnp.exp(s - lse[h, hd:hd + 1, :])
                    dp = dot_plain(value, o_r[feats, cols])
                    d = (p * (dp - delta[h, hd:hd + 1, :])).astype(BF16)
                    acc[feats, :] += dot_plain(key_t, d)
                    ps.append(p.astype(BF16))
                    ds.append(d)
                q4 = jnp.concatenate([qt[hd * 64:(hd + 1) * 64, cols] for hd in range(4 * g, 4 * g + 4)], 1)
                do4 = jnp.concatenate([o_r[hd * 64:(hd + 1) * 64, cols] for hd in range(4 * g, 4 * g + 4)], 1)
                dhf[g * 64:(g + 1) * 64, keys_at] += dot_nt(q4, jnp.concatenate(ds, 1))
                dhf[128 + g * 64:192 + g * 64, keys_at] += dot_nt(do4, jnp.concatenate(ps, 1))
            return carry

        lax.fori_loop(low, high, step, 0)

    def attend_back_end(h):
        cols = slice(h * CHUNK, (h + 1) * CHUNK)
        for hd in range(8):
            at = hd * 64
            a, b = rope_rows(acc[at:at + 32, :] * 0.125, acc[at + 32:at + 64, :] * 0.125, cosine[:, cols], -sine[:, cols])
            acc[at:at + 32, :] = a
            acc[at + 32:at + 64, :] = b
        qt[:, cols] = acc[...].astype(BF16)
        du[0, rows_of(h), 0:512] = acc[...].T.astype(BF16)

    d_attended(0)
    dhf[...] = jnp.zeros(dhf.shape, F32)
    acc[...] = jnp.zeros(acc.shape, F32)
    feed_sums[1].turn()
    unshake(0, zs_line + ys_line + four)
    ff = wg.shape[2]
    gate_sum, up_sum = [
        GradSum(
            me, lambda z, yh, w=w: w.at[core, lanes((z % 2) * 1024 + yh * 512 + (z // 2) * 256, 256)],
            lambda i, w=w: w.at[1 - core, lanes(i * 256, 256)], out, 256, lambda v, c: v.at[lanes(c * 128, 128)], acts, sems(11),
        ) for w, out in ((wg, o_gate), (wu, o_up))
    ]
    down_sum = GradSum(
        me, lambda z, yh: wd.at[core, :, lanes((z % 2) * 1024 + yh * 512 + (z // 2) * 256, 256)],
        lambda i: wd.at[1 - core, :, lanes(i * 256, 256)], o_down, ff, lambda v, c: v.at[:, lanes(c * 128, 128)], acts, sems(11),
    )
    out_sum = GradSum(
        me, lambda z, yh: wo.at[lanes(core * 256, 256), lanes((z % 2) * 1024 + yh * 512 + (z // 2) * 256, 256)],
        lambda i: wo.at[lanes((1 - core) * 256, 256), lanes(i * 256, 256)], o_out, 256,
        lambda v, c: v.at[:, lanes(c * 128, 128)], acts, sems(11),
    )
    query_sum = GradSum(
        me, lambda z, yh: h2.at[pl.ds(0, 256), lanes((z % 2) * 1024 + yh * 512 + (z // 2) * 256, 256)],
        lambda i: h2.at[pl.ds(256, 256), lanes(i * 256, 256)], o_q, 256,
        lambda v, c: v.at[:, lanes(c * 128, 128)], acts, sems(11),
    )
    gate_sum.start()
    up_sum.start()
    down_sum.start()
    base = sems(5)
    h1_over = send(h1, cfp, acts, base, partner)
    ot_over = send(ot.at[lanes((1 - core) * 256, 256)], hp.at[2, pl.ds(0, 256), pl.ds(0, 512)], acts, base + 1, partner)
    da_over = send(mf, h2p, acts, base + 2, partner)
    dq_over = send(qt.at[lanes((1 - core) * 256, 256)], hp.at[0, pl.ds(0, 256), pl.ds(0, 512)], acts, base + 3, partner)
    own_dkv = hp.at[1, pl.ds(256, 256), pl.ds(0, 512)]
    dkv_over = send(
        hp.at[1, lanes(256 + (1 - core) * 128, 128), pl.ds(0, 512)], hp.at[1, pl.ds(0, 128), pl.ds(0, 512)], acts, base + 4, partner
    )
    h1_over.start()
    ot_over.start()
    attend_back(0, 0, chunk_of[0] + 1)
    attend_back_end(0)
    ring_two[1].finish()
    da_over.start()
    d_attended(1)
    acc[...] = jnp.zeros(acc.shape, F32)

    def mixed_rows(h):
        rows = rows_of(h)
        total = x1[rows, :] + feed_sums[h].finish()
        squares[2:3, :] += column_squares(total)
        mix[rows, :] = total.astype(BF16)

    def homeward(src, home, at):
        def piece(q):
            half, block = q // 2, q % 2
            row = jnp.where(half == 0, me.quarter, 3 - me.quarter)
            return (
                src.at[lanes(half * 256, 256), lanes(block * 256, 256)],
                home.at[pl.ds(pl.multiple_of(row * CHUNK, CHUNK), CHUNK)],
            )

        copies = []
        for d in (1, 2, 3):
            s, t = piece((me.quarter + d) % 4)
            copies.append(send(s, t, acts, at + d, me.by_quarter(d)))
        s, t = piece(me.quarter)
        copies.append(pltpu.make_async_copy(s, t, acts[0].at[at]))
        return copies

    mixed_rows(0)
    mixed_rows(1)
    feed_sums[0].drain()
    feed_sums[1].drain()
    shake(1, [me.by_x(1), me.by_x(3)])
    home_mixed = homeward(mix, o_mixed, sems(4))
    for c in home_mixed:
        c.start()
    attend_back(1, 0, 3)
    gate_sum.sum_z()
    shake(2, ys_line)
    attend_back(1, 3, chunk_of[1] + 1)
    attend_back_end(1)
    dq_over.start()

    def dkv_slot(ref, k):
        return ref.at[k // 4, pl.ds(((k // 2) % 2) * 256, 256), pl.ds((k % 2) * 256, 256)]

    for j in range(8):
        dkv_slot(hid, j)[...] = dhf[:, j * CHUNK:(j + 1) * CHUNK].astype(BF16)
    base = sems(8)
    dkv_copies = []
    for d in (1, 2, 3):
        q = (me.quarter + d) % 4
        for h, k in ((0, q), (1, 7 - q)):
            src = hid.at[k // 4, lanes(((k // 2) % 2) * 256, 256), lanes((k % 2) * 256, 256)]
            dkv_copies.append(send(src, dkv_slot(dg, (d - 1) * 2 + h), acts, base + h * 4 + d, me.by_quarter(d)))
    for c in dkv_copies:
        c.start()
    da_over.wait()
    ot_over.wait()

    def out_grad(n, carry):
        cols = lanes(n * 256, 256)
        wo[lanes(core * 256, 256), cols] = (
            dot_plain(ot[lanes(core * 256, 256), :], mf[:, cols]) + dot_plain(hp[2, 0:256, 0:512], h2p[:, cols])
        ).astype(BF16)
        return carry

    lax.fori_loop(0, 8, out_grad, 0)
    shake(3, xs_line + ys_line + zs_line)
    unshake(2, ys_line)
    gate_sum.send_y()
    up_sum.sum_z()
    shake(4, ys_line)
    for c in dkv_copies:
        c.wait_recv()
    x1[...] = jnp.zeros(x1.shape, F32)
    for h in (0, 1):
        cols = slice(h * CHUNK, (h + 1) * CHUNK)
        total = dhf[:, lanes(chunk_of[h] * CHUNK, CHUNK)]
        for d in range(3):
            total = total + dkv_slot(dg, d * 2 + h)[...].astype(F32)
        for g in (0, 1):
            a, b = rope_rows(total[g * 64:g * 64 + 32], total[g * 64 + 32:g * 64 + 64], cosine[:, cols], -sine[:, cols])
            v = total[128 + g * 64:192 + g * 64]
            x1[pl.ds(heads[g], 32), cols] = a
            x1[pl.ds(heads[g] + 32, 32), cols] = b
            x1[pl.ds(256 + heads[g], 64), cols] = v
            hp[1, 256 + g * 64:288 + g * 64, cols] = a.astype(BF16)
            hp[1, 288 + g * 64:320 + g * 64, cols] = b.astype(BF16)
            hp[1, 384 + g * 64:448 + g * 64, cols] = v.astype(BF16)
    dkv_over.start()
    du[1, :, 0:512] = x1[...].T.astype(BF16)
    for c in dkv_copies:
        c.wait_send()
    unstash.wait()

    def back_one(h):
        rows = rows_of(h)

        def step(n, carry):
            feats = lanes(n * 256, 256)
            orig = lanes(((n % 2) * 4 + n // 2) * 256, 256)
            total = dot_nt(du[0, rows, 0:512], wq[feats, :])
            total = total + dot_nt(du[1, rows, 0:256], w_key[orig, :]) + dot_nt(du[1, rows, 256:512], w_value[orig, :])
            dhf[:, feats] = total
            return carry

        lax.fori_loop(0, 8, step, 0)
        norm_back(h, cf, r1, row_one, 0)

    row_one = device_order_row(gain1)
    unshake(1, [me.by_x(1), me.by_x(3)])
    one_sums = ring_sums()
    back_one(0)
    one_sums[0].start()
    back_one(1)
    one_sums[1].start()
    one_sums[0].turn()
    dkv_over.wait()
    dq_over.wait()
    h1_over.wait()

    def late_grads(n, carry):
        cols = lanes(n * 256, 256)
        mf[256:384, cols] = (
            dot_plain(hp[1, lanes(256 + core * 128, 128), 0:512], h1[:, cols]) + dot_plain(hp[1, 0:128, 0:512], cfp[:, cols])
        ).astype(BF16)
        h2[0:256, cols] = (
            dot_plain(qt[lanes(core * 256, 256), :], h1[:, cols]) + dot_plain(hp[0, 0:256, 0:512], cfp[:, cols])
        ).astype(BF16)
        return carry

    lax.fori_loop(0, 8, late_grads, 0)
    unshake(3, xs_line + ys_line + zs_line)
    base = sems(25)
    kv_z = [
        send(mf.at[pl.ds(256, 128), lanes(((me.z + d) % 4) * 512, 512)], mf.at[pl.ds(384, 128), pl.ds((d - 1) * 512, 512)],
             acts, base + d, me.by_z(d)) for d in (1, 2, 3)
    ]
    for c in kv_z:
        c.start()
    out_sum.start()
    query_sum.start()
    for k in range(2):
        small[k:k + 1, :] = gains[0:1, k * 1024:(k + 1) * 1024]
        small[2 + k:3 + k, :] = gains[1:2, k * 1024:(k + 1) * 1024]
    small[4:7, 0:512] = squares[0:3, :]

    def small_copies(n, peers, at):
        return [send(small, small_r.at[n, d], acts, at + d, p) for d, p in enumerate(peers)]

    def small_add(n, copies):
        for c in copies:
            c.wait()
        total = small[...]
        for d in range(len(copies)):
            total = total + small_r[n, d]
        small[...] = total

    small_z = small_copies(0, zs_line, sems(3))
    for c in small_z:
        c.start()
    one_sums[1].turn()
    unshake(4, ys_line)
    up_sum.send_y()
    down_sum.sum_z()
    shake(5, ys_line)

    def in_rows(h):
        rows = rows_of(h)
        dx1[rows, :] += one_sums[h].finish()

    in_rows(0)
    for c in kv_z:
        c.wait()
    z_at = lanes(me.z * 512, 512)
    mf[256:384, z_at] = (
        mf[256:384, z_at].astype(F32) + mf[384:512, 0:512].astype(F32) + mf[384:512, 512:1024].astype(F32)
        + mf[384:512, 1024:1536].astype(F32)
    ).astype(BF16)
    kv_y = [
        send(mf.at[pl.ds(256, 128), lanes(me.z * 512 + ((me.y + d) % 4) * 128, 128)],
             mf.at[pl.ds(384, 128), pl.ds(1536 + (d - 1) * 128, 128)], acts, base + 3 + d, me.by_y(d)) for d in (1, 2, 3)
    ]
    for c in kv_y:
        c.start()
    small_add(0, small_z)
    small_y = small_copies(1, ys_line, sems(3))
    for c in small_y:
        c.start()
    in_rows(1)
    home_in = homeward(dx1, o_in, sems(4))
    for c in home_in:
        c.start()
    unshake(5, ys_line)
    down_sum.send_y()
    out_sum.sum_z()
    query_sum.sum_z()
    shake(6, ys_line)
    for c in kv_y:
        c.wait()
    zy_at = lanes(me.z * 512 + me.y * 128, 128)
    mf[256:384, zy_at] = (
        mf[256:384, zy_at].astype(F32) + mf[384:512, 1536:1664].astype(F32) + mf[384:512, 1664:1792].astype(F32)
        + mf[384:512, 1792:1920].astype(F32)
    ).astype(BF16)
    pair = me.at(me.z, me.y, core, x + 1 - 2 * (x % 2))
    kv_pair = send(mf.at[pl.ds(256, 128), zy_at], mf.at[pl.ds(384, 128), pl.ds(1920, 128)], acts, base + 7, pair)
    kv_pair.start()
    small_add(1, small_y)
    small_x = small_copies(2, xs_line, sems(3))
    for c in small_x:
        c.start()
    unshake(6, ys_line)
    out_sum.send_y()
    query_sum.send_y()
    gate_sum.sum_y()
    up_sum.sum_y()
    kv_pair.wait()
    g_rows = lanes((x % 2) * 64, 64)
    mine = mf[pl.ds(pl.multiple_of(256 + (x % 2) * 64, 64), 64), zy_at].astype(F32)
    mine = mine + mf[pl.ds(pl.multiple_of(384 + (x % 2) * 64, 64), 64), 1920:2048].astype(F32)
    head_at = pl.ds(pl.multiple_of((2 * (x % 2) + x // 2) * 64, 64), 64)
    mf[head_at, zy_at] = mine.astype(BF16)
    kv_x = [send(mf.at[head_at, zy_at], mf.at[head_at, zy_at], acts, base + 7 + d, me.by_x(d)) for d in (1, 2, 3)]
    for c in kv_x:
        c.start()
    small_add(2, small_x)
    small_c = small_copies(3, [partner], sems(1))
    for c in small_c:
        c.start()
    for c in kv_x:
        c.wait()
    block = mf.at[pl.ds(0, 256), zy_at]
    kv_y2 = [send(block, block, acts, base + 11 + d, me.by_y(d)) for d in (1, 2, 3)]
    for c in kv_y2:
        c.start()
    down_sum.sum_y()
    small_add(3, small_c)
    for c in kv_y2:
        c.wait()
    block2 = mf.at[pl.ds(0, 256), z_at]
    kv_z2 = [send(block2, block2, acts, base + 15 + d, me.by_z(d)) for d in (1, 2, 3)]
    for c in kv_z2:
        c.start()
    out_sum.sum_y()
    query_sum.sum_y()
    small_out = pltpu.make_async_copy(small, o_small, lsem.at[8])
    small_out.start()
    for c in kv_z2:
        c.wait()
    kv_last = send(mf.at[pl.ds(0, 256)], o_kv.at[core], acts, base + 20, partner)
    kv_keep = pltpu.make_async_copy(mf.at[pl.ds(0, 256)], o_kv.at[core], lsem.at[9])
    kv_last.start()
    kv_keep.start()
    for s in (gate_sum, up_sum, down_sum, out_sum, query_sum):
        s.finish()
    for c in home_mixed + home_in:
        c.wait()
    for h in (0, 1):
        one_sums[h].drain()
    small_out.wait()
    kv_last.wait()
    kv_keep.wait()


ACTS = 220


def layer(tok, cot, wq, wo, wg, wu, wd, w_key, w_value, gain1, gain2, ids):
    ff = wg.shape[1]
    sds = jax.ShapeDtypeStruct
    outs = [
        sds((1024, 256), BF16), sds((1024, 256), F32), sds((256, 128), BF16), sds((256, 128), BF16),
        sds((128, ff), BF16), sds((128, ff), BF16), sds((ff, 128), BF16), sds((2, 256, 2048), BF16), sds((8, 1024), F32),
        sds((T, 2048), BF16),
    ]
    dma = pltpu.SemaphoreType.DMA
    vm = pl.BlockSpec(memory_space=pltpu.VMEM)
    wide = pltpu.VMEM((T, 2048), BF16)
    square = pltpu.VMEM((T, 512), BF16)
    inner = pltpu.VMEM((2, T, ff), BF16)
    row8 = pltpu.VMEM((8, CHUNK), F32)
    pair8 = pltpu.VMEM((2, 8, CHUNK), F32)
    return pl.pallas_call(
        layer_kernel, out_shape=outs, in_specs=[ANY] * 7 + [vm] * 5, out_specs=[ANY] * len(outs),
        scratch_shapes=[
            wide, wide, wide, wide, wide, wide,
            pltpu.VMEM((2048, 512), BF16), pltpu.VMEM((512, 2048), BF16),
            pltpu.VMEM((2, 2048, ff), BF16), pltpu.VMEM((2, 2048, ff), BF16), pltpu.VMEM((2, ff, 2048), BF16),
            square, square, square, pltpu.VMEM((8, 256, CHUNK), BF16),
            pltpu.VMEM((T, 512), F32), pltpu.VMEM((T, 512), F32),
            wide, pltpu.VMEM((2, 2, 256, 256), BF16), pltpu.VMEM((2, 2, 256, 512), BF16),
            pltpu.VMEM((512, CHUNK), F32), row8, row8, pair8, pair8,
            inner, inner, inner, pltpu.VMEM((3, T, ff), BF16), pltpu.VMEM((CHUNK, 2048), F32),
            pltpu.VMEM((T, 1), F32), pltpu.VMEM((T, 1), F32), square,
            pltpu.VMEM((2, 2048), F32), pltpu.VMEM((8, 512), F32), pltpu.VMEM((8, 1024), F32), pltpu.VMEM((4, 3, 8, 1024), F32),
            dma((ACTS,)), dma((ACTS,)), dma((5, 31)), dma((5, 31)), dma((10,)), pltpu.SemaphoreType.REGULAR((8,)),
        ],
        compiler_params=pltpu.CompilerParams(collective_id=0, has_side_effects=True, vmem_limit_bytes=64 << 20),
    )(tok, cot, wq, wo, wg, wu, wd, w_key, w_value, gain1, gain2, ids)


def from_device_order(v):
    return v.reshape((4, 2, 256) + v.shape[1:]).swapaxes(0, 1).reshape(v.shape)


def shards(tokens, segment_ids, norm_one, w_query, w_key, w_value, w_out, norm_two, w_gate, w_up, w_down, cotangent):
    mixed, input_grad, gq, go, gg, gu, gd, gkv, small, _ = layer(
        tokens, cotangent, w_query, w_out, w_gate, w_up, w_down, w_key, w_value,
        norm_one.reshape(1, 2048), norm_two.reshape(1, 2048), segment_ids.reshape(8, 16, 128),
    )
    key_total, value_total = [from_device_order(gkv[n].T.astype(F32)) for n in (0, 1)]
    rms = jnp.sqrt(jnp.sum(small[4:7, :512], 1) / (16384 * 2048))
    return (
        mixed, input_grad, gq.T.astype(F32), key_total, value_total, go.astype(F32), gg.astype(F32), gu.astype(F32),
        gd.astype(F32), from_device_order(small[0:2].reshape(2048)), from_device_order(small[2:4].reshape(2048)), rms,
    )


def solution(mesh):
    return jax.shard_map(
        shards,
        mesh=mesh,
        in_specs=(
            P("row", "col"), P(), P(), P("row", "col"), P(), P(), P("col", "row"), P(),
            P("row", "col"), P("row", "col"), P("col", "row"), P("row", "col"),
        ),
        out_specs=(
            P("row", "col"), P("row", "col"), P("row", "col"), P(), P(), P("col", "row"),
            P("row", "col"), P("row", "col"), P("col", "row"), P(), P(), P(),
        ),
        check_vma=False,
    )
```

```python
import functools
import math

import jax
import jax.numpy as jnp
from jax import lax
from jax.experimental import pallas as pl
from jax.experimental.pallas import tpu as pltpu
from jax.sharding import PartitionSpec as P

BF16 = jnp.bfloat16
F32 = jnp.float32
HEAD = 64
eps = 1e-05
MESH = pl.DeviceIdType.MESH
ANY = pl.BlockSpec(memory_space=pl.ANY)
CHUNK = 256
T = 512


class Place:
    def __init__(self):
        row = lax.axis_index("row")
        col = lax.axis_index("col")
        self.z = row // 4
        self.yh = (row // 2) % 2
        self.core = row % 2
        self.yl = col // 4
        self.x = col % 4
        self.y = self.yh * 2 + self.yl
        self.quarter = self.core * 2 + self.yl

    def at(self, z, y, core, x):
        return {"row": z * 4 + (y // 2) * 2 + core, "col": (y % 2) * 4 + x}

    def by_x(self, d):
        return self.at(self.z, self.y, self.core, (self.x + d) % 4)

    def by_z(self, d):
        return self.at((self.z + d) % 4, self.y, self.core, self.x)

    def by_y(self, d):
        return self.at(self.z, (self.y + d) % 4, self.core, self.x)

    def partner(self):
        return self.at(self.z, self.y, 1 - self.core, self.x)

    def by_quarter(self, d):
        q = (self.quarter + d) % 4
        return self.at(self.z, self.yh * 2 + q % 2, q // 2, self.x)


def greet(peers):
    barrier = pltpu.get_barrier_semaphore()
    for peer in peers:
        pl.semaphore_signal(barrier, inc=1, device_id=peer, device_id_type=MESH)
    pl.semaphore_wait(barrier, len(peers))


def send(src, dst, sems, k, peer):
    return pltpu.make_async_remote_copy(
        src_ref=src, dst_ref=dst, send_sem=sems[0].at[k], recv_sem=sems[1].at[k],
        device_id=peer, device_id_type=MESH,
    )


def each(count, act):
    def step(i, carry):
        act(i)
        return carry

    lax.fori_loop(0, count, step, 0)


def perm_row(z, y, core):
    yh = y // 2
    return ((z % 2) * 2 + yh) * 512 + (z // 2) * 256 + core * 128


def reshard_in(me, src, full, sems, base, lsem):
    def chunk(q):
        return src.at[pl.ds(pl.multiple_of(jnp.where(me.core == 0, q, 3 - q) * CHUNK, CHUNK), CHUNK)]

    half = pl.multiple_of(me.core * CHUNK, CHUNK)
    place = full.at[pl.ds(half, CHUNK), pl.ds(pl.multiple_of(me.x * 512 + me.yl * 256, 256), 256)]
    copies = []
    for d in (1, 2, 3):
        copies.append(send(chunk((me.quarter + d) % 4), place, sems, base + d, me.by_quarter(d)))
    local = pltpu.make_async_copy(chunk(me.quarter), place, lsem)
    return copies, local


class Spread:
    def __init__(self, me, src, slot, z_first, sems, lsem):
        self.me, self.src, self.slot, self.z_first, self.sems, self.lsem = me, src, slot, z_first, sems, lsem

    def local(self):
        me = self.me
        return pltpu.make_async_copy(self.src, self.slot(me.z, me.y, me.core), self.lsem)

    def first(self, i):
        me = self.me
        peer = me.by_z(i + 1) if self.z_first else me.by_y(i + 1)
        return send(self.src, self.slot(me.z, me.y, me.core), self.sems, i, peer)

    def line(self, k):
        me = self.me
        if self.z_first:
            return self.slot((me.z + 4 - k) % 4, me.y, me.core)
        return self.slot(me.z, (me.y + 4 - k) % 4, me.core)

    def second(self, k, i):
        me = self.me
        peer = me.by_y(i + 1) if self.z_first else me.by_z(i + 1)
        block = self.line(k)
        return send(block, block, self.sems, 3 + k * 3 + i, peer)

    def third(self, i):
        me = self.me
        if self.z_first:
            block = self.slot((me.z + 4 - i // 4) % 4, (me.y + 4 - i % 4) % 4, me.core)
        else:
            block = self.slot((me.z + 4 - i % 4) % 4, (me.y + 4 - i // 4) % 4, me.core)
        return send(block, block, self.sems, 15 + i, me.partner())

    def start(self):
        self.local().start()
        each(3, lambda i: self.first(i).start())

    def turn(self):
        self.local().wait()
        each(3, lambda i: self.second(0, i).start())
        self.third(0).start()

        def arrived(k):
            self.first(k).wait_recv()
            each(3, lambda i: self.second(k + 1, i).start())
            self.third((k + 1) * 4).start()

        each(3, arrived)

    def cross(self, k=None):
        def arrived(j):
            n, i = j // 3, j % 3
            self.second(n, i).wait_recv()
            self.third(n * 4 + i + 1).start()

        if k is None:
            each(12, arrived)
        else:
            each(3, lambda i: arrived(k * 3 + i))

    def finish(self):
        each(16, lambda i: self.third(i).wait_recv())
        each(3, lambda i: self.first(i).wait_send())
        each(12, lambda j: self.second(j // 3, j % 3).wait_send())
        each(16, lambda i: self.third(i).wait_send())


def weight_slots(q, o, g, u, d):
    def ds(start, size):
        return pl.ds(pl.multiple_of(start, 128), size)

    return (
        lambda z, y, c: q.at[ds(perm_row(z, y, c), 128), ds((y % 2) * 256, 256)],
        lambda z, y, c: o.at[ds((y % 2) * 256, 256), ds(perm_row(z, y, c), 128)],
        lambda z, y, c: g.at[y % 2, ds(perm_row(z, y, c), 128)],
        lambda z, y, c: u.at[y % 2, ds(perm_row(z, y, c), 128)],
        lambda z, y, c: d.at[y % 2, :, ds(perm_row(z, y, c), 128)],
    )


def dot_plain(left, right):
    return jnp.dot(left, right, preferred_element_type=F32)


def dot_tn(left, right):
    return lax.dot_general(left, right, (((0,), (0,)), ((), ())), preferred_element_type=F32)


def dot_nt(left, right):
    return lax.dot_general(left, right, (((1,), (1,)), ((), ())), preferred_element_type=F32)


def lanes(start, size):
    return pl.ds(pl.multiple_of(start, 128), size)


class Ring:
    def __init__(self, me, full, rows, sems, base):
        x = me.x
        right, left = me.by_x(1), me.by_x(3)
        xl, xr = (x + 3) % 4, (x + 1) % 4

        def at(b, off, size):
            return full.at[rows, lanes(b * 512 + off, size)]

        self.one = [
            send(at(x, 0, 512), at(x, 0, 512), sems, base + 0, right),
            send(at(x, 0, 512), at(x, 0, 512), sems, base + 1, left),
        ]
        self.two = [
            send(at(xl, 0, 256), at(xl, 0, 256), sems, base + 2, right),
            send(at(xr, 256, 256), at(xr, 256, 256), sems, base + 3, left),
        ]

    def start(self):
        for c in self.one:
            c.start()

    def turn(self):
        for a, b in zip(self.one, self.two):
            a.wait_recv()
            b.start()

    def finish(self):
        for a in self.one:
            a.wait_send()
        for b in self.two:
            b.wait()


class RingSum:
    def __init__(self, me, part, rows, hop, got, sems, base):
        x = me.x
        self.part, self.rows, self.hop, self.got, self.x = part, rows, hop, got, x
        right, left = me.by_x(1), me.by_x(3)
        far, xr, xl = (x + 2) % 4, (x + 1) % 4, (x + 3) % 4
        self.xr, self.xl = xr, xl

        def at(b, off):
            return part.at[rows, lanes(b * 512 + off, 256)]

        self.one = [
            send(at(far, 0), hop.at[0], sems, base + 0, right),
            send(at(far, 256), hop.at[1], sems, base + 1, left),
            send(at(xr, 256), got.at[0, :, pl.ds(256, 256)], sems, base + 2, right),
            send(at(xl, 0), got.at[1, :, pl.ds(0, 256)], sems, base + 3, left),
        ]
        self.two = [
            send(at(xr, 0), got.at[0, :, pl.ds(0, 256)], sems, base + 4, right),
            send(at(xl, 256), got.at[1, :, pl.ds(256, 256)], sems, base + 5, left),
        ]

    def start(self):
        for c in self.one:
            c.start()

    def turn(self):
        for k, (b, off) in enumerate(((self.xr, 0), (self.xl, 256))):
            self.one[k].wait_recv()
            cols = lanes(b * 512 + off, 256)
            total = self.part[self.rows, cols].astype(F32) + self.hop[k].astype(F32)
            self.part[self.rows, cols] = total.astype(BF16)
            self.two[k].start()

    def finish(self):
        for k in (2, 3):
            self.one[k].wait_recv()
        for c in self.two:
            c.wait_recv()
        own = self.part[self.rows, lanes(self.x * 512, 512)].astype(F32)
        return own + self.got[0].astype(F32) + self.got[1].astype(F32)

    def drain(self):
        for c in self.one + self.two:
            c.wait_send()


def rope_rows(a, b, cosine, sine):
    return a * cosine - b * sine, b * cosine + a * sine


def document_starts(ids, seq, place):
    ids = ids[seq]

    def below(number):
        hit = (ids < number).astype(F32)
        return jnp.sum(jnp.sum(hit, 1, keepdims=True), 0, keepdims=True)

    second, third = below(3 * seq + 1).astype(jnp.int32), below(3 * seq + 2).astype(jnp.int32)
    return jnp.where(place >= third, third, jnp.where(place >= second, second, 0))


ORIGINAL = [(p % 2) * 4 + p // 2 for p in range(8)]


def device_order_row(ref):
    return jnp.concatenate([ref[:, b * 256:(b + 1) * 256].astype(F32) for b in ORIGINAL], 1)


def rms_rows(src, gain, dst, rstd, first, count):
    def step(k, carry):
        rows = pl.ds(pl.multiple_of(first + k * 64, 64), 64)
        v = src[rows, :].astype(F32)
        r = lax.rsqrt(jnp.sum(v * v, 1, keepdims=True) * (1.0 / 2048.0) + eps)
        rstd[rows, :] = r
        dst[rows, :] = (v * r * gain).astype(BF16)
        return carry

    lax.fori_loop(0, count // 64, step, 0)


def column_squares(value):
    return jnp.sum(value * value, 0, keepdims=True)


class GradSum:
    def __init__(self, me, own, land, out, rows, halves, sems, base):
        self.me, self.own, self.land, self.out, self.rows, self.halves = me, own, land, out, rows, halves
        self.sems, self.base = sems, base

    def first(self, i):
        me = self.me
        return send(self.own((me.z + 1 + i // 2) % 4, i % 2), self.land(i), self.sems, self.base + i, me.by_z(1 + i // 2))

    def start(self):
        each(6, lambda i: self.first(i).start())

    def add(self, view, others):
        def step(k, carry):
            rows = pl.ds(pl.multiple_of(k * 64, 64), 64)
            total = view[rows, :].astype(F32)
            for other in others:
                total = total + other[rows, :].astype(F32)
            view[rows, :] = total.astype(BF16)
            return carry

        lax.fori_loop(0, self.rows // 64, step, 0)

    def sum_z(self):
        each(6, lambda i: self.first(i).wait_recv())
        for yh in (0, 1):
            self.add(self.own(self.me.z, yh), [self.land(d * 2 + yh) for d in range(3)])
        each(6, lambda i: self.first(i).wait_send())

    def second(self, yh):
        me = self.me
        to = yh * 2 + me.core
        step = (to + 4 - me.y) % 4
        slot = (step + 3) % 4
        copy = pltpu.make_async_remote_copy(
            src_ref=self.own(me.z, yh), dst_ref=self.land(slot), send_sem=self.sems[0].at[self.base + 6 + yh],
            recv_sem=self.sems[1].at[self.base + 6 + slot], device_id=me.at(me.z, to, me.core, me.x), device_id_type=MESH,
        )
        return step, copy

    def send_y(self):
        for yh in (0, 1):
            step, copy = self.second(yh)
            pl.when(step != 0)(copy.start)

    def last(self):
        me = self.me
        view = self.halves(self.own(me.z, me.yh), 1 - me.core)
        return send(view, self.out, self.sems, self.base + 9, me.partner())

    def keep(self):
        me = self.me
        return pltpu.make_async_copy(self.halves(self.own(me.z, me.yh), me.core), self.out, self.sems[0].at[self.base + 10])

    def sum_y(self):
        me = self.me

        def work():
            for slot in range(3):
                pltpu.make_async_remote_copy(
                    src_ref=self.land(slot), dst_ref=self.land(slot), send_sem=self.sems[0].at[self.base + 8],
                    recv_sem=self.sems[1].at[self.base + 6 + slot], device_id=me.partner(), device_id_type=MESH,
                ).wait_recv()
            self.add(self.own(me.z, me.yh), [self.land(slot) for slot in range(3)])
            self.last().start()
            self.keep().start()

        pl.when(me.yl == me.core)(work)

    def finish(self):
        me = self.me

        def sender():
            self.last().wait_send()
            self.keep().wait()

        pl.when(me.yl == me.core)(sender)
        pl.when(me.yl != me.core)(lambda: self.last().wait_recv())
        for yh in (0, 1):
            step, copy = self.second(yh)
            pl.when(step != 0)(copy.wait_send)


class GradSumY(GradSum):
    def __init__(self, me, own, land, extra, out, rows, halves, sems, base):
        super().__init__(me, own, land, out, rows, halves, sems, base)
        self.extra = extra

    def landing(self, step, k):
        return self.extra(k) if step == 3 else self.land((step - 1) * 4 + k)

    def first_y(self, yh, step, k):
        me = self.me
        return pltpu.make_async_remote_copy(
            src_ref=self.own(k, yh), dst_ref=self.landing(step, k), send_sem=self.sems[0].at[self.base + yh * 4 + k],
            recv_sem=self.sems[1].at[self.base + (step - 1) * 4 + k],
            device_id=me.at(me.z, yh * 2 + me.core, me.core, me.x), device_id_type=MESH,
        )

    def steps(self, act):
        me = self.me
        for yh in (0, 1):
            away = (yh * 2 + me.core + 4 - me.y) % 4
            for step in (1, 2, 3):
                pl.when(away == step)(functools.partial(act, yh, step))

    def start(self):
        self.steps(lambda yh, step: each(4, lambda k: self.first_y(yh, step, k).start()))

    def sum_y(self):
        me = self.me

        def work():
            for step in (1, 2, 3):
                each(4, lambda k: self.first_y(0, step, k).wait_recv())

            def one(k):
                self.add(self.own(k, me.yh), [self.landing(step, k) for step in (1, 2, 3)])

            each(4, one)

        pl.when(me.yl == me.core)(work)
        self.steps(lambda yh, step: each(4, lambda k: self.first_y(yh, step, k).wait_send()))

    def second_z(self, d):
        me = self.me
        return send(self.own((me.z + d) % 4, me.yh), self.land(d - 1), self.sems, self.base + 11 + d, me.by_z(d))

    def send_z(self):
        def work():
            for d in (1, 2, 3):
                self.second_z(d).start()

        pl.when(self.me.yl == self.me.core)(work)

    def last(self):
        me = self.me
        view = self.halves(self.own(me.z, me.yh), 1 - me.core)
        return send(view, self.out, self.sems, self.base + 15, me.partner())

    def keep(self):
        me = self.me
        return pltpu.make_async_copy(self.halves(self.own(me.z, me.yh), me.core), self.out, self.sems[0].at[self.base + 16])

    def sum_z(self):
        me = self.me

        def work():
            for d in (1, 2, 3):
                self.second_z(d).wait_recv()
            self.add(self.own(me.z, me.yh), [self.land(d) for d in range(3)])
            self.last().start()
            self.keep().start()

        pl.when(me.yl == me.core)(work)

    def finish(self):
        me = self.me

        def sender():
            for d in (1, 2, 3):
                self.second_z(d).wait_send()
            self.last().wait_send()
            self.keep().wait()

        pl.when(me.yl == me.core)(sender)
        pl.when(me.yl != me.core)(lambda: self.last().wait_recv())


def layer_kernel(
    tok, cot, wq_s, wo_s, wg_s, wu_s, wd_s, w_key, w_value, gain1, gain2, ids,
    o_mixed, o_in, o_q, o_out, o_gate, o_up, o_down, o_kv, o_small, xs,
    xf, cf, mf, h1, h2p, cfp, wq, wo, wg, wu, wd, qt, ot, o_r, kvt, x1, dx1, part, hop, got, acc, mx, sm, lse, delta,
    hid, dg, du, hp, dhf, r1, r2, mix, gains, squares, small, small_r,
    a_s, a_r, w_s, w_r, lsem, hs,
):
    me = Place()
    x, core = me.x, me.core
    h2, kv_tmp = xf, dx1
    acts = (a_s, a_r)
    count = [0]

    def sems(n):
        count[0] += n
        assert count[0] <= ACTS
        return count[0] - n

    def shake(k, peers):
        for peer in peers:
            pl.semaphore_signal(hs.at[k], inc=1, device_id=peer, device_id_type=MESH)

    def unshake(k, peers):
        pl.semaphore_wait(hs.at[k], len(peers))

    xs_line = [me.by_x(i) for i in (1, 2, 3)]
    ys_line = [me.by_y(i) for i in (1, 2, 3)]
    zs_line = [me.by_z(i) for i in (1, 2, 3)]
    four = [me.by_quarter(i) for i in (1, 2, 3)]
    partner = me.partner()
    greet(xs_line + ys_line + zs_line + four)
    slots = weight_slots(wq, wo, wg, wu, wd)
    first_z = (False, True, False, True, False)
    spreads = [
        Spread(me, src, slots[n], first_z[n], (w_s.at[n], w_r.at[n]), lsem.at[2 + n])
        for n, src in enumerate((wq_s, wo_s, wg_s, wu_s, wd_s))
    ]
    in_copies, in_local = reshard_in(me, tok, xf, acts, sems(4), lsem.at[0])
    cot_copies, cot_local = reshard_in(me, cot, cf, acts, sems(4), lsem.at[1])
    for c in in_copies + [in_local]:
        c.start()
    s_q, s_o, s_g, s_u, s_d = spreads
    s_q.start()
    seq = me.z * 2 + me.yh
    chunk_of = (me.quarter, 7 - me.quarter)
    lane = lax.broadcasted_iota(jnp.int32, (1, CHUNK), 1)
    places = [c * CHUNK + lane for c in chunk_of]
    starts = [document_starts(ids, seq, p) for p in places]
    pos = jnp.concatenate([p - s for p, s in zip(places, starts)], 1).astype(F32)
    turn = lax.broadcasted_iota(jnp.int32, (32, 1), 0).astype(F32)
    angle = jnp.exp(-math.log(10000.0) * turn / 32.0) * pos
    cosine, sine = jnp.cos(angle), jnp.sin(angle)
    gains[...] = jnp.zeros(gains.shape, F32)
    squares[...] = jnp.zeros(squares.shape, F32)
    small[...] = jnp.zeros(small.shape, F32)

    for c in in_copies:
        c.wait_recv()
    in_local.wait()
    ring_tok = Ring(me, xf, pl.ds(0, T), acts, sems(4))
    ring_tok.start()
    s_q.turn()
    s_g.start()
    for c in cot_copies + [cot_local]:
        c.start()
    s_d.start()
    s_o.start()
    s_u.start()
    ring_tok.turn()
    ring_cot = Ring(me, cf, pl.ds(0, T), acts, sems(4))
    s_q.cross()
    ring_tok.finish()
    s_g.turn()
    s_d.turn()
    for c in cot_copies:
        c.wait_recv()
    cot_local.wait()
    ring_cot.start()
    for c in in_copies + cot_copies:
        c.wait_send()
    stash = pltpu.make_async_copy(xf, xs, lsem.at[7])
    stash.start()

    rms_rows(xf, device_order_row(gain1), h1, r1, 0, T)
    s_q.finish()
    for n, w in enumerate((w_key, w_value)):
        total = None
        for p, b in enumerate(ORIGINAL):
            d = dot_plain(h1[:, p * 256:(p + 1) * 256], w[b * 256:(b + 1) * 256, :])
            total = d if total is None else total + d
        kv_tmp[n * 256:(n + 1) * 256, :] = total.T
    heads = [pl.multiple_of((2 * g + x // 2) * HEAD, HEAD) for g in (0, 1)]
    for g in (0, 1):
        head = heads[g]
        a, b = rope_rows(kv_tmp[pl.ds(head, 32), :], kv_tmp[pl.ds(head + 32, 32), :], cosine, sine)
        v = kv_tmp[pl.ds(256 + head, HEAD), :]
        for h in (0, 1):
            cols = slice(h * CHUNK, (h + 1) * CHUNK)
            kvt[chunk_of[h], g * 64:g * 64 + 32, :] = a[:, cols].astype(BF16)
            kvt[chunk_of[h], g * 64 + 32:g * 64 + 64, :] = b[:, cols].astype(BF16)
            kvt[chunk_of[h], 128 + g * 64:192 + g * 64, :] = v[:, cols].astype(BF16)
    kv_copies = []
    base = sems(8)
    for h in (0, 1):
        for d in (1, 2, 3):
            block = kvt.at[chunk_of[h]]
            kv_copies.append(send(block, block, acts, base + h * 4 + d, me.by_quarter(d)))
    for c in kv_copies:
        c.start()
    for n in (0, 1):
        q = dot_plain(h1[...], wq[:, n * 256:(n + 1) * 256]).T
        for hd in range(4):
            at = hd * HEAD
            a, b = rope_rows(q[at:at + 32], q[at + 32:at + 64], cosine, sine)
            qt[n * 256 + at:n * 256 + at + 32, :] = (a * 0.125).astype(BF16)
            qt[n * 256 + at + 32:n * 256 + at + 64, :] = (b * 0.125).astype(BF16)
    ring_cot.turn()
    for c in kv_copies:
        c.wait()
    s_o.turn()

    def row_form(block):
        return block.astype(F32).T.astype(BF16)

    def allowed(h, j):
        at = lax.broadcasted_iota(jnp.int32, (CHUNK, CHUNK), 0) + j * CHUNK
        return (at >= starts[h]) & (at <= places[h])

    def attend_begin():
        mx[...] = jnp.full(mx.shape, -1e30, F32)
        sm[...] = jnp.zeros(sm.shape, F32)
        acc[...] = jnp.zeros(acc.shape, F32)

    def attend(h, low, high):
        cols = slice(h * CHUNK, (h + 1) * CHUNK)

        def step(j, carry):
            ok = allowed(h, j)
            keys = [row_form(kvt[j, g * 64:(g + 1) * 64, :]) for g in (0, 1)]
            for hd in range(8):
                g = hd // 4
                s = jnp.where(ok, dot_plain(keys[g], qt[hd * 64:(hd + 1) * 64, cols]), -1e30)
                old = mx[hd:hd + 1, :]
                new = jnp.maximum(old, jnp.max(s, 0, keepdims=True))
                p = jnp.exp(s - new)
                shrink = jnp.exp(old - new)
                mx[hd:hd + 1, :] = new
                sm[hd:hd + 1, :] = sm[hd:hd + 1, :] * shrink + jnp.sum(p, 0, keepdims=True)
                acc[hd * 64:(hd + 1) * 64, :] = acc[hd * 64:(hd + 1) * 64, :] * shrink + dot_plain(
                    kvt[j, 128 + g * 64:192 + g * 64, :], p.astype(BF16)
                )
            return carry

        lax.fori_loop(low, high, step, 0)

    def attend_end(h):
        cols = slice(h * CHUNK, (h + 1) * CHUNK)
        lse[h] = mx[...] + jnp.log(sm[...])
        for hd in range(8):
            rows = slice(hd * 64, (hd + 1) * 64)
            acc[rows, :] = acc[rows, :] / sm[hd:hd + 1, :]
        ot[:, cols] = acc[...].astype(BF16)
        o_r[cols, :] = acc[...].T.astype(BF16)

    def rows_of(h):
        return pl.ds(h * CHUNK, CHUNK)

    def project(h):
        rows = rows_of(h)

        def step(n, carry):
            cols = lanes(n * 256, 256)
            part[rows, cols] = dot_plain(o_r[rows, :], wo[:, cols]).astype(BF16)
            return carry

        lax.fori_loop(0, 8, step, 0)

    def ring_sums():
        return [RingSum(me, part, rows_of(h), hop.at[h], got.at[h], acts, sems(6)) for h in (0, 1)]

    def rings():
        return [Ring(me, mf, rows_of(h), acts, sems(4)) for h in (0, 1)]

    sums, ring = ring_sums(), rings()
    own = lanes(x * 512, 512)

    def stream(h):
        rows = rows_of(h)
        mine = xf[rows, own].astype(F32)
        total = mine + sums[h].finish()
        squares[0:1, :] += column_squares(mine)
        squares[1:2, :] += column_squares(total)
        x1[rows, :] = total
        mf[rows, own] = total.astype(BF16)

    attend_begin()
    attend(0, 0, chunk_of[0] + 1)
    attend_end(0)
    s_u.turn()
    s_o.cross()
    s_o.finish()
    project(0)
    sums[0].start()
    attend_begin()
    attend(1, 0, 3)
    sums[0].turn()
    attend(1, 3, chunk_of[1] + 1)
    attend_end(1)
    stream(0)
    ring[0].start()
    project(1)
    sums[1].start()
    ring[0].turn()
    sums[1].turn()
    stream(1)
    ring[1].start()
    ring_cot.finish()
    cot_over = send(cf, cfp, acts, sems(1), partner)
    cot_over.start()
    stash.wait()
    ring[0].finish()

    row_two = device_order_row(gain2)
    rms_rows(mf, row_two, h2, r2, 0, CHUNK)
    for s in spreads[2:]:
        s.cross()
    ring[1].turn()
    for s in spreads[2:]:
        s.finish()

    def feed_forward(h):
        rows = rows_of(h)

        def step(b, carry):
            for at, size in ((0, 256), (256, 256), (512, 192)):
                cols = slice(at, at + size)
                gate = dot_plain(h2[rows, :], wg[b, :, cols])
                up = dot_plain(h2[rows, :], wu[b, :, cols])
                d_hidden = dot_nt(cf[rows, :], wd[b, cols, :])
                sigma = 1.0 / (1.0 + jnp.exp(-gate))
                active = gate * sigma
                hid[b, rows, cols] = (active * up).astype(BF16)
                dg[b, rows, cols] = (d_hidden * up * sigma * (1.0 + gate * (1.0 - sigma))).astype(BF16)
                du[b, rows, cols] = (d_hidden * active).astype(BF16)
            return carry

        lax.fori_loop(0, 2, step, 0)

    def norm_back(h, u_ref, rstd, gain, k):
        def step(i, carry):
            at = pl.multiple_of(i * 64, 64)
            full = pl.ds(pl.multiple_of(h * CHUNK + i * 64, 64), 64)
            d = dhf[pl.ds(at, 64), :]
            u = u_ref[full, :].astype(F32)
            r = rstd[full, :]
            scaled = d * gain
            inner = jnp.sum(scaled * u, 1, keepdims=True)
            part[full, :] = (r * scaled - u * (r * r * r * (1.0 / 2048.0) * inner)).astype(BF16)
            gains[k:k + 1, :] += jnp.sum(d * u * r, 0, keepdims=True)
            return carry

        lax.fori_loop(0, CHUNK // 64, step, 0)

    def back_two(h):
        rows = rows_of(h)

        def step(n, carry):
            feats = lanes(n * 256, 256)
            total = dot_nt(dg[0, rows, :], wg[0, feats, :]) + dot_nt(dg[1, rows, :], wg[1, feats, :])
            total = total + dot_nt(du[0, rows, :], wu[0, feats, :]) + dot_nt(du[1, rows, :], wu[1, feats, :])
            dhf[:, feats] = total
            return carry

        lax.fori_loop(0, 8, step, 0)
        norm_back(h, mf, r2, row_two, 1)

    feed_forward(0)
    back_two_sums, ring_two = ring_sums(), rings()
    ring[1].finish()
    sums[0].drain()
    back_two(0)
    back_two_sums[0].start()
    rms_rows(mf, row_two, h2, r2, CHUNK, CHUNK)
    feed_forward(1)
    h2_over = send(h2, h2p, acts, sems(1), partner)
    h2_over.start()
    base = sems(3)
    hid_over = [send(ref.at[1 - core], hp.at[n], acts, base + n, partner) for n, ref in enumerate((hid, dg, du))]
    for c in hid_over:
        c.start()
    back_two_sums[0].turn()
    sums[1].drain()
    back_two(1)
    back_two_sums[1].start()

    def d_stream(h):
        rows = rows_of(h)
        total = cf[rows, own].astype(F32) + back_two_sums[h].finish()
        dx1[rows, :] = total
        mf[rows, own] = total.astype(BF16)

    d_stream(0)
    ring_two[0].start()
    h2_over.wait()
    for c in hid_over:
        c.wait()
    cot_over.wait()

    def feed(h):
        rows = rows_of(h)

        def step(n, carry):
            cols = lanes(n * 256, 256)
            part[rows, cols] = (dot_plain(hid[0, rows, :], wd[0, :, cols]) + dot_plain(hid[1, rows, :], wd[1, :, cols])).astype(BF16)
            return carry

        lax.fori_loop(0, 8, step, 0)

    def grads_in(low, high):
        def step(m, carry):
            feats = lanes(m * 256, 256)
            mine = h2[:, feats].T
            other = h2p[:, feats].T
            wg[core, feats, :] = (dot_plain(mine, dg[core]) + dot_plain(other, hp[1])).astype(BF16)
            wu[core, feats, :] = (dot_plain(mine, du[core]) + dot_plain(other, hp[2])).astype(BF16)
            return carry

        lax.fori_loop(low, high, step, 0)

    grads_in(0, 4)
    back_two_sums[1].turn()
    ring_two[0].turn()
    grads_in(4, 8)
    d_stream(1)
    ring_two[1].start()
    ring_two[0].finish()
    for h in (0, 1):
        back_two_sums[h].drain()
    feed_sums = ring_sums()
    feed(0)
    feed(1)
    ring_two[1].turn()
    feed_sums[0].start()

    for at, size in ((0, 256), (256, 256), (512, 192)):
        mine = hid[core, :, at:at + size].T
        other = hp[0, :, at:at + size].T

        def down(n, carry):
            cols = lanes(n * 512, 512)
            wd[core, at:at + size, cols] = (dot_plain(mine, cf[:, cols]) + dot_plain(other, cfp[:, cols])).astype(BF16)
            return carry

        lax.fori_loop(0, 4, down, 0)

    shake(0, zs_line + ys_line + four)
    unstash = pltpu.make_async_copy(xs, cf, lsem.at[7])
    unstash.start()

    def d_attended(h):
        cols = slice(h * CHUNK, (h + 1) * CHUNK)
        rows = rows_of(h)
        for k in (0, 1):
            feats = slice(k * 256, (k + 1) * 256)
            d = dot_nt(wo[feats, :], mf[rows, :])
            o_r[feats, cols] = d.astype(BF16)
            both = d.astype(BF16).astype(F32) * ot[feats, cols].astype(F32)
            for hd in range(4):
                delta[h, k * 4 + hd:k * 4 + hd + 1, :] = jnp.sum(both[hd * 64:(hd + 1) * 64], 0, keepdims=True)

    def attend_back(h, low, high):
        cols = slice(h * CHUNK, (h + 1) * CHUNK)

        def step(j, carry):
            ok = allowed(h, j)
            keys_at = lanes(j * CHUNK, CHUNK)
            for g in (0, 1):
                key_t = kvt[j, g * 64:(g + 1) * 64, :]
                key, value = row_form(key_t), row_form(kvt[j, 128 + g * 64:192 + g * 64, :])
                ps, ds = [], []
                for hd in range(4 * g, 4 * g + 4):
                    feats = slice(hd * 64, (hd + 1) * 64)
                    s = jnp.where(ok, dot_plain(key, qt[feats, cols]), -1e30)
                    p = jnp.exp(s - lse[h, hd:hd + 1, :])
                    dp = dot_plain(value, o_r[feats, cols])
                    d = (p * (dp - delta[h, hd:hd + 1, :])).astype(BF16)
                    acc[feats, :] += dot_plain(key_t, d)
                    ps.append(p.astype(BF16))
                    ds.append(d)
                q4 = jnp.concatenate([qt[hd * 64:(hd + 1) * 64, cols] for hd in range(4 * g, 4 * g + 4)], 1)
                do4 = jnp.concatenate([o_r[hd * 64:(hd + 1) * 64, cols] for hd in range(4 * g, 4 * g + 4)], 1)
                dhf[g * 64:(g + 1) * 64, keys_at] += dot_nt(q4, jnp.concatenate(ds, 1))
                dhf[128 + g * 64:192 + g * 64, keys_at] += dot_nt(do4, jnp.concatenate(ps, 1))
            return carry

        lax.fori_loop(low, high, step, 0)

    def attend_back_end(h):
        cols = slice(h * CHUNK, (h + 1) * CHUNK)
        for hd in range(8):
            at = hd * 64
            a, b = rope_rows(acc[at:at + 32, :] * 0.125, acc[at + 32:at + 64, :] * 0.125, cosine[:, cols], -sine[:, cols])
            acc[at:at + 32, :] = a
            acc[at + 32:at + 64, :] = b
        qt[:, cols] = acc[...].astype(BF16)
        du[0, rows_of(h), 0:512] = acc[...].T.astype(BF16)

    d_attended(0)
    dhf[...] = jnp.zeros(dhf.shape, F32)
    acc[...] = jnp.zeros(acc.shape, F32)
    unshake(0, zs_line + ys_line + four)
    ff = wg.shape[2]
    def row_slot(w):
        return lambda z, yh: w.at[core, lanes((z % 2) * 1024 + yh * 512 + (z // 2) * 256, 256)]

    def row_land(w):
        return lambda i: w.at[1 - core, lanes(i * 256, 256)]

    def row_half(v, c):
        return v.at[lanes(c * 128, 128)]

    gate_sum = GradSum(me, row_slot(wg), row_land(wg), o_gate, 256, row_half, acts, sems(11))
    up_sum = GradSumY(
        me, row_slot(wu), row_land(wu), lambda k: hp.at[k // 2, lanes((k % 2) * 256, 256)], o_up, 256, row_half, acts, sems(17)
    )
    down_sum = GradSum(
        me, lambda z, yh: wd.at[core, :, lanes((z % 2) * 1024 + yh * 512 + (z // 2) * 256, 256)],
        lambda i: wd.at[1 - core, :, lanes(i * 256, 256)], o_down, ff, lambda v, c: v.at[:, lanes(c * 128, 128)], acts, sems(11),
    )
    out_sum = GradSum(
        me, lambda z, yh: wo.at[lanes(core * 256, 256), lanes((z % 2) * 1024 + yh * 512 + (z // 2) * 256, 256)],
        lambda i: wo.at[lanes((1 - core) * 256, 256), lanes(i * 256, 256)], o_out, 256,
        lambda v, c: v.at[:, lanes(c * 128, 128)], acts, sems(11),
    )
    query_sum = GradSum(
        me, lambda z, yh: h2.at[pl.ds(0, 256), lanes((z % 2) * 1024 + yh * 512 + (z // 2) * 256, 256)],
        lambda i: h2.at[pl.ds(256, 256), lanes(i * 256, 256)], o_q, 256,
        lambda v, c: v.at[:, lanes(c * 128, 128)], acts, sems(11),
    )
    up_sum.start()
    gate_sum.start()
    down_sum.start()
    base = sems(5)
    h1_over = send(h1, cfp, acts, base, partner)
    ot_over = send(ot.at[lanes((1 - core) * 256, 256)], hp.at[2, pl.ds(0, 256), pl.ds(0, 512)], acts, base + 1, partner)
    da_over = send(mf, h2p, acts, base + 2, partner)
    dq_over = send(qt.at[lanes((1 - core) * 256, 256)], hp.at[2, pl.ds(256, 256), pl.ds(0, 512)], acts, base + 3, partner)
    dkv_over = send(dg.at[1, lanes(256 + (1 - core) * 128, 128), pl.ds(0, 512)], o_r.at[pl.ds(0, 128)], acts, base + 4, partner)
    h1_over.start()
    ot_over.start()
    attend_back(0, 0, chunk_of[0] + 1)
    attend_back_end(0)
    ring_two[1].finish()
    feed_sums[1].start()
    feed_sums[0].turn()
    da_over.start()
    d_attended(1)
    acc[...] = jnp.zeros(acc.shape, F32)

    def mixed_rows(h):
        rows = rows_of(h)
        total = x1[rows, :] + feed_sums[h].finish()
        squares[2:3, :] += column_squares(total)
        mix[rows, :] = total.astype(BF16)

    def homeward(src, home, at):
        def piece(q):
            half, block = q // 2, q % 2
            row = jnp.where(half == 0, me.quarter, 3 - me.quarter)
            return (
                src.at[lanes(half * 256, 256), lanes(block * 256, 256)],
                home.at[pl.ds(pl.multiple_of(row * CHUNK, CHUNK), CHUNK)],
            )

        copies = []
        for d in (1, 2, 3):
            s, t = piece((me.quarter + d) % 4)
            copies.append(send(s, t, acts, at + d, me.by_quarter(d)))
        s, t = piece(me.quarter)
        copies.append(pltpu.make_async_copy(s, t, acts[0].at[at]))
        return copies

    attend_back(1, 0, 3)
    feed_sums[1].turn()
    attend_back(1, 3, chunk_of[1] + 1)
    attend_back_end(1)
    dq_over.start()

    def dkv_slot(ref, k):
        return ref.at[k // 4, pl.ds(((k // 2) % 2) * 256, 256), pl.ds((k % 2) * 256, 256)]

    for j in range(8):
        dkv_slot(hid, j)[...] = dhf[:, j * CHUNK:(j + 1) * CHUNK].astype(BF16)
    base = sems(8)
    dkv_copies = []
    for d in (1, 2, 3):
        q = (me.quarter + d) % 4
        for h, k in ((0, q), (1, 7 - q)):
            src = hid.at[k // 4, lanes(((k // 2) % 2) * 256, 256), lanes((k % 2) * 256, 256)]
            dkv_copies.append(send(src, dkv_slot(dg, (d - 1) * 2 + h), acts, base + h * 4 + d, me.by_quarter(d)))
    for c in dkv_copies:
        c.start()
    mixed_rows(0)
    mixed_rows(1)
    feed_sums[0].drain()
    feed_sums[1].drain()
    shake(1, [me.by_x(1), me.by_x(3)])
    home_mixed = homeward(mix, o_mixed, sems(4))
    for c in home_mixed:
        c.start()
    da_over.wait()
    ot_over.wait()

    def out_grad(n, carry):
        cols = lanes(n * 256, 256)
        wo[lanes(core * 256, 256), cols] = (
            dot_plain(ot[lanes(core * 256, 256), :], mf[:, cols]) + dot_plain(hp[2, 0:256, 0:512], h2p[:, cols])
        ).astype(BF16)
        return carry

    lax.fori_loop(0, 8, out_grad, 0)
    shake(3, xs_line + ys_line + zs_line)
    up_sum.sum_y()
    shake(4, zs_line)
    for c in dkv_copies:
        c.wait_recv()
    x1[...] = jnp.zeros(x1.shape, F32)
    for h in (0, 1):
        cols = slice(h * CHUNK, (h + 1) * CHUNK)
        total = dhf[:, lanes(chunk_of[h] * CHUNK, CHUNK)]
        for d in range(3):
            total = total + dkv_slot(dg, d * 2 + h)[...].astype(F32)
        for g in (0, 1):
            a, b = rope_rows(total[g * 64:g * 64 + 32], total[g * 64 + 32:g * 64 + 64], cosine[:, cols], -sine[:, cols])
            v = total[128 + g * 64:192 + g * 64]
            x1[pl.ds(heads[g], 32), cols] = a
            x1[pl.ds(heads[g] + 32, 32), cols] = b
            x1[pl.ds(256 + heads[g], 64), cols] = v
            dg[1, 256 + g * 64:288 + g * 64, cols] = a.astype(BF16)
            dg[1, 288 + g * 64:320 + g * 64, cols] = b.astype(BF16)
            dg[1, 384 + g * 64:448 + g * 64, cols] = v.astype(BF16)
    dkv_over.start()
    du[1, :, 0:512] = x1[...].T.astype(BF16)
    for c in dkv_copies:
        c.wait_send()
    unstash.wait()

    def back_one(h):
        rows = rows_of(h)

        def step(n, carry):
            feats = lanes(n * 256, 256)
            orig = lanes(((n % 2) * 4 + n // 2) * 256, 256)
            total = dot_nt(du[0, rows, 0:512], wq[feats, :])
            total = total + dot_nt(du[1, rows, 0:256], w_key[orig, :]) + dot_nt(du[1, rows, 256:512], w_value[orig, :])
            dhf[:, feats] = total
            return carry

        lax.fori_loop(0, 8, step, 0)
        norm_back(h, cf, r1, row_one, 0)

    row_one = device_order_row(gain1)
    unshake(1, [me.by_x(1), me.by_x(3)])
    one_sums = ring_sums()
    back_one(0)
    one_sums[0].start()
    back_one(1)
    one_sums[1].start()
    one_sums[0].turn()
    dkv_over.wait()
    dq_over.wait()
    h1_over.wait()

    def late_grads(n, carry):
        cols = lanes(n * 256, 256)
        mf[256:384, cols] = (
            dot_plain(dg[1, lanes(256 + core * 128, 128), 0:512], h1[:, cols]) + dot_plain(o_r[0:128, :], cfp[:, cols])
        ).astype(BF16)
        h2[0:256, cols] = (
            dot_plain(qt[lanes(core * 256, 256), :], h1[:, cols]) + dot_plain(hp[2, 256:512, 0:512], cfp[:, cols])
        ).astype(BF16)
        return carry

    lax.fori_loop(0, 8, late_grads, 0)
    unshake(3, xs_line + ys_line + zs_line)
    base = sems(25)
    kv_z = [
        send(mf.at[pl.ds(256, 128), lanes(((me.z + d) % 4) * 512, 512)], mf.at[pl.ds(384, 128), pl.ds((d - 1) * 512, 512)],
             acts, base + d, me.by_z(d)) for d in (1, 2, 3)
    ]
    for c in kv_z:
        c.start()
    out_sum.start()
    query_sum.start()
    for k in range(2):
        small[k:k + 1, :] = gains[0:1, k * 1024:(k + 1) * 1024]
        small[2 + k:3 + k, :] = gains[1:2, k * 1024:(k + 1) * 1024]
    small[4:7, 0:512] = squares[0:3, :]

    def small_copies(n, peers, at):
        return [send(small, small_r.at[n, d], acts, at + d, p) for d, p in enumerate(peers)]

    def small_add(n, copies):
        for c in copies:
            c.wait()
        total = small[...]
        for d in range(len(copies)):
            total = total + small_r[n, d]
        small[...] = total

    small_z = small_copies(0, zs_line, sems(3))
    for c in small_z:
        c.start()
    one_sums[1].turn()
    unshake(4, zs_line)
    up_sum.send_z()
    gate_sum.sum_z()
    shake(2, ys_line)
    down_sum.sum_z()
    shake(5, ys_line)

    def in_rows(h):
        rows = rows_of(h)
        dx1[rows, :] += one_sums[h].finish()

    in_rows(0)
    for c in kv_z:
        c.wait()
    z_at = lanes(me.z * 512, 512)
    mf[256:384, z_at] = (
        mf[256:384, z_at].astype(F32) + mf[384:512, 0:512].astype(F32) + mf[384:512, 512:1024].astype(F32)
        + mf[384:512, 1024:1536].astype(F32)
    ).astype(BF16)
    kv_y = [
        send(mf.at[pl.ds(256, 128), lanes(me.z * 512 + ((me.y + d) % 4) * 128, 128)],
             mf.at[pl.ds(384, 128), pl.ds(1536 + (d - 1) * 128, 128)], acts, base + 3 + d, me.by_y(d)) for d in (1, 2, 3)
    ]
    for c in kv_y:
        c.start()
    small_add(0, small_z)
    small_y = small_copies(1, ys_line, sems(3))
    for c in small_y:
        c.start()
    in_rows(1)
    home_in = homeward(dx1, o_in, sems(4))
    for c in home_in:
        c.start()
    unshake(2, ys_line)
    gate_sum.send_y()
    unshake(5, ys_line)
    down_sum.send_y()
    out_sum.sum_z()
    query_sum.sum_z()
    shake(6, ys_line)
    for c in kv_y:
        c.wait()
    zy_at = lanes(me.z * 512 + me.y * 128, 128)
    mf[256:384, zy_at] = (
        mf[256:384, zy_at].astype(F32) + mf[384:512, 1536:1664].astype(F32) + mf[384:512, 1664:1792].astype(F32)
        + mf[384:512, 1792:1920].astype(F32)
    ).astype(BF16)
    pair = me.at(me.z, me.y, core, x + 1 - 2 * (x % 2))
    kv_pair = send(mf.at[pl.ds(256, 128), zy_at], mf.at[pl.ds(384, 128), pl.ds(1920, 128)], acts, base + 7, pair)
    kv_pair.start()
    small_add(1, small_y)
    small_x = small_copies(2, xs_line, sems(3))
    for c in small_x:
        c.start()
    unshake(6, ys_line)
    out_sum.send_y()
    query_sum.send_y()
    gate_sum.sum_y()
    up_sum.sum_z()
    kv_pair.wait()
    g_rows = lanes((x % 2) * 64, 64)
    mine = mf[pl.ds(pl.multiple_of(256 + (x % 2) * 64, 64), 64), zy_at].astype(F32)
    mine = mine + mf[pl.ds(pl.multiple_of(384 + (x % 2) * 64, 64), 64), 1920:2048].astype(F32)
    head_at = pl.ds(pl.multiple_of((2 * (x % 2) + x // 2) * 64, 64), 64)
    mf[head_at, zy_at] = mine.astype(BF16)
    kv_x = [send(mf.at[head_at, zy_at], mf.at[head_at, zy_at], acts, base + 7 + d, me.by_x(d)) for d in (1, 2, 3)]
    for c in kv_x:
        c.start()
    small_add(2, small_x)
    small_c = small_copies(3, [partner], sems(1))
    for c in small_c:
        c.start()
    for c in kv_x:
        c.wait()
    block = mf.at[pl.ds(0, 256), zy_at]
    kv_y2 = [send(block, block, acts, base + 11 + d, me.by_y(d)) for d in (1, 2, 3)]
    for c in kv_y2:
        c.start()
    down_sum.sum_y()
    small_add(3, small_c)
    for c in kv_y2:
        c.wait()
    block2 = mf.at[pl.ds(0, 256), z_at]
    kv_z2 = [send(block2, block2, acts, base + 15 + d, me.by_z(d)) for d in (1, 2, 3)]
    for c in kv_z2:
        c.start()
    out_sum.sum_y()
    query_sum.sum_y()
    small_out = pltpu.make_async_copy(small, o_small, lsem.at[8])
    small_out.start()
    for c in kv_z2:
        c.wait()
    kv_last = send(mf.at[pl.ds(0, 256)], mf.at[pl.ds(256, 256)], acts, base + 20, partner)
    kv_last.start()
    flights = []

    def lay_out(home, first, k):
        for p, b in enumerate(ORIGINAL):
            spot = (k * 8 + p) % 4
            if len(flights) >= 4:
                flights[-4].wait()
            stage = x1.at[pl.ds((spot // 2) * 256, 256), pl.ds((spot % 2) * 256, 256)]
            x1[(spot // 2) * 256:(spot // 2 + 1) * 256, (spot % 2) * 256:(spot % 2 + 1) * 256] = (
                mf[first:first + 256, p * 256:(p + 1) * 256].astype(F32).T
            )
            copy = pltpu.make_async_copy(stage, home.at[pl.ds(b * 256, 256)], lsem.at[10 + spot])
            copy.start()
            flights.append(copy)

    lay_out(o_kv.at[core], 0, 0)
    kv_last.wait()
    lay_out(o_kv.at[1 - core], 256, 1)
    for c in flights[-4:]:
        c.wait()
    for s in (gate_sum, up_sum, down_sum, out_sum, query_sum):
        s.finish()
    for c in home_mixed + home_in:
        c.wait()
    for h in (0, 1):
        one_sums[h].drain()
    small_out.wait()


ACTS = 240


def layer(tok, cot, wq, wo, wg, wu, wd, w_key, w_value, gain1, gain2, ids):
    ff = wg.shape[1]
    sds = jax.ShapeDtypeStruct
    outs = [
        sds((1024, 256), BF16), sds((1024, 256), F32), sds((256, 128), BF16), sds((256, 128), BF16),
        sds((128, ff), BF16), sds((128, ff), BF16), sds((ff, 128), BF16), sds((2, 2048, 256), F32), sds((8, 1024), F32),
        sds((T, 2048), BF16),
    ]
    dma = pltpu.SemaphoreType.DMA
    vm = pl.BlockSpec(memory_space=pltpu.VMEM)
    wide = pltpu.VMEM((T, 2048), BF16)
    square = pltpu.VMEM((T, 512), BF16)
    inner = pltpu.VMEM((2, T, ff), BF16)
    row8 = pltpu.VMEM((8, CHUNK), F32)
    pair8 = pltpu.VMEM((2, 8, CHUNK), F32)
    return pl.pallas_call(
        layer_kernel, out_shape=outs, in_specs=[ANY] * 7 + [vm] * 5, out_specs=[ANY] * len(outs),
        scratch_shapes=[
            wide, wide, wide, wide, wide, wide,
            pltpu.VMEM((2048, 512), BF16), pltpu.VMEM((512, 2048), BF16),
            pltpu.VMEM((2, 2048, ff), BF16), pltpu.VMEM((2, 2048, ff), BF16), pltpu.VMEM((2, ff, 2048), BF16),
            square, square, square, pltpu.VMEM((8, 256, CHUNK), BF16),
            pltpu.VMEM((T, 512), F32), pltpu.VMEM((T, 512), F32),
            wide, pltpu.VMEM((2, 2, 256, 256), BF16), pltpu.VMEM((2, 2, 256, 512), BF16),
            pltpu.VMEM((512, CHUNK), F32), row8, row8, pair8, pair8,
            inner, inner, inner, pltpu.VMEM((3, T, ff), BF16), pltpu.VMEM((CHUNK, 2048), F32),
            pltpu.VMEM((T, 1), F32), pltpu.VMEM((T, 1), F32), square,
            pltpu.VMEM((2, 2048), F32), pltpu.VMEM((8, 512), F32), pltpu.VMEM((8, 1024), F32), pltpu.VMEM((4, 3, 8, 1024), F32),
            dma((ACTS,)), dma((ACTS,)), dma((5, 31)), dma((5, 31)), dma((14,)), pltpu.SemaphoreType.REGULAR((8,)),
        ],
        compiler_params=pltpu.CompilerParams(collective_id=0, has_side_effects=True, vmem_limit_bytes=64 << 20),
    )(tok, cot, wq, wo, wg, wu, wd, w_key, w_value, gain1, gain2, ids)


def from_device_order(v):
    return v.reshape((4, 2, 256) + v.shape[1:]).swapaxes(0, 1).reshape(v.shape)


def shards(tokens, segment_ids, norm_one, w_query, w_key, w_value, w_out, norm_two, w_gate, w_up, w_down, cotangent):
    mixed, input_grad, gq, go, gg, gu, gd, gkv, small, _ = layer(
        tokens, cotangent, w_query, w_out, w_gate, w_up, w_down, w_key, w_value,
        norm_one.reshape(1, 2048), norm_two.reshape(1, 2048), segment_ids.reshape(8, 16, 128),
    )
    key_total, value_total = gkv[0], gkv[1]
    rms = jnp.sqrt(jnp.sum(small[4:7, :512], 1) / (16384 * 2048))
    return (
        mixed, input_grad, gq.T.astype(F32), key_total, value_total, go.astype(F32), gg.astype(F32), gu.astype(F32),
        gd.astype(F32), from_device_order(small[0:2].reshape(2048)), from_device_order(small[2:4].reshape(2048)), rms,
    )


def solution(mesh):
    return jax.shard_map(
        shards,
        mesh=mesh,
        in_specs=(
            P("row", "col"), P(), P(), P("row", "col"), P(), P(), P("col", "row"), P(),
            P("row", "col"), P("row", "col"), P("col", "row"), P("row", "col"),
        ),
        out_specs=(
            P("row", "col"), P("row", "col"), P("row", "col"), P(), P(), P("col", "row"),
            P("row", "col"), P("row", "col"), P("col", "row"), P(), P(), P(),
        ),
        check_vma=False,
    )
```

```python
import functools
import math

import jax
import jax.numpy as jnp
from jax import lax
from jax.experimental import pallas as pl
from jax.experimental.pallas import tpu as pltpu
from jax.sharding import PartitionSpec as P

BF16 = jnp.bfloat16
F32 = jnp.float32
HEAD = 64
eps = 1e-05
MESH = pl.DeviceIdType.MESH
ANY = pl.BlockSpec(memory_space=pl.ANY)
CHUNK = 256
T = 512


class Place:
    def __init__(self):
        row = lax.axis_index("row")
        col = lax.axis_index("col")
        self.z = row // 4
        self.yh = (row // 2) % 2
        self.core = row % 2
        self.yl = col // 4
        self.x = col % 4
        self.y = self.yh * 2 + self.yl
        self.quarter = self.core * 2 + self.yl

    def at(self, z, y, core, x):
        return {"row": z * 4 + (y // 2) * 2 + core, "col": (y % 2) * 4 + x}

    def by_x(self, d):
        return self.at(self.z, self.y, self.core, (self.x + d) % 4)

    def by_z(self, d):
        return self.at((self.z + d) % 4, self.y, self.core, self.x)

    def by_y(self, d):
        return self.at(self.z, (self.y + d) % 4, self.core, self.x)

    def partner(self):
        return self.at(self.z, self.y, 1 - self.core, self.x)

    def by_quarter(self, d):
        q = (self.quarter + d) % 4
        return self.at(self.z, self.yh * 2 + q % 2, q // 2, self.x)


def greet(peers):
    barrier = pltpu.get_barrier_semaphore()
    for peer in peers:
        pl.semaphore_signal(barrier, inc=1, device_id=peer, device_id_type=MESH)
    pl.semaphore_wait(barrier, len(peers))


def send(src, dst, sems, k, peer):
    return pltpu.make_async_remote_copy(
        src_ref=src, dst_ref=dst, send_sem=sems[0].at[k], recv_sem=sems[1].at[k],
        device_id=peer, device_id_type=MESH,
    )


def each(count, act):
    def step(i, carry):
        act(i)
        return carry

    lax.fori_loop(0, count, step, 0)


def perm_row(z, y, core):
    yh = y // 2
    return ((z % 2) * 2 + yh) * 512 + (z // 2) * 256 + core * 128


def reshard_in(me, src, full, sems, base, lsem):
    def chunk(q):
        return src.at[pl.ds(pl.multiple_of(jnp.where(me.core == 0, q, 3 - q) * CHUNK, CHUNK), CHUNK)]

    half = pl.multiple_of(me.core * CHUNK, CHUNK)
    place = full.at[pl.ds(half, CHUNK), pl.ds(pl.multiple_of(me.x * 512 + me.yl * 256, 256), 256)]
    copies = []
    for d in (1, 2, 3):
        copies.append(send(chunk((me.quarter + d) % 4), place, sems, base + d, me.by_quarter(d)))
    local = pltpu.make_async_copy(chunk(me.quarter), place, lsem)
    return copies, local


class Spread:
    def __init__(self, me, src, slot, z_first, sems, lsem):
        self.me, self.src, self.slot, self.z_first, self.sems, self.lsem = me, src, slot, z_first, sems, lsem

    def local(self):
        me = self.me
        return pltpu.make_async_copy(self.src, self.slot(me.z, me.y, me.core), self.lsem)

    def first(self, i):
        me = self.me
        peer = me.by_z(i + 1) if self.z_first else me.by_y(i + 1)
        return send(self.src, self.slot(me.z, me.y, me.core), self.sems, i, peer)

    def line(self, k):
        me = self.me
        if self.z_first:
            return self.slot((me.z + 4 - k) % 4, me.y, me.core)
        return self.slot(me.z, (me.y + 4 - k) % 4, me.core)

    def second(self, k, i):
        me = self.me
        peer = me.by_y(i + 1) if self.z_first else me.by_z(i + 1)
        block = self.line(k)
        return send(block, block, self.sems, 3 + k * 3 + i, peer)

    def third(self, i):
        me = self.me
        if self.z_first:
            block = self.slot((me.z + 4 - i // 4) % 4, (me.y + 4 - i % 4) % 4, me.core)
        else:
            block = self.slot((me.z + 4 - i % 4) % 4, (me.y + 4 - i // 4) % 4, me.core)
        return send(block, block, self.sems, 15 + i, me.partner())

    def start(self):
        self.local().start()
        each(3, lambda i: self.first(i).start())

    def turn(self):
        self.local().wait()
        each(3, lambda i: self.second(0, i).start())
        self.third(0).start()

        def arrived(k):
            self.first(k).wait_recv()
            each(3, lambda i: self.second(k + 1, i).start())
            self.third((k + 1) * 4).start()

        each(3, arrived)

    def cross(self, k=None):
        def arrived(j):
            n, i = j // 3, j % 3
            self.second(n, i).wait_recv()
            self.third(n * 4 + i + 1).start()

        if k is None:
            each(12, arrived)
        else:
            each(3, lambda i: arrived(k * 3 + i))

    def finish(self):
        each(16, lambda i: self.third(i).wait_recv())
        each(3, lambda i: self.first(i).wait_send())
        each(12, lambda j: self.second(j // 3, j % 3).wait_send())
        each(16, lambda i: self.third(i).wait_send())


def weight_slots(q, o, g, u, d):
    def ds(start, size):
        return pl.ds(pl.multiple_of(start, 128), size)

    return (
        lambda z, y, c: q.at[ds(perm_row(z, y, c), 128), ds((y % 2) * 256, 256)],
        lambda z, y, c: o.at[ds((y % 2) * 256, 256), ds(perm_row(z, y, c), 128)],
        lambda z, y, c: g.at[y % 2, ds(perm_row(z, y, c), 128)],
        lambda z, y, c: u.at[y % 2, ds(perm_row(z, y, c), 128)],
        lambda z, y, c: d.at[y % 2, :, ds(perm_row(z, y, c), 128)],
    )


def dot_plain(left, right):
    return jnp.dot(left, right, preferred_element_type=F32)


def dot_tn(left, right):
    return lax.dot_general(left, right, (((0,), (0,)), ((), ())), preferred_element_type=F32)


def dot_nt(left, right):
    return lax.dot_general(left, right, (((1,), (1,)), ((), ())), preferred_element_type=F32)


def lanes(start, size):
    return pl.ds(pl.multiple_of(start, 128), size)


class Ring:
    def __init__(self, me, full, rows, sems, base):
        x = me.x
        right, left = me.by_x(1), me.by_x(3)
        xl, xr = (x + 3) % 4, (x + 1) % 4

        def at(b, off, size):
            return full.at[rows, lanes(b * 512 + off, size)]

        self.one = [
            send(at(x, 0, 512), at(x, 0, 512), sems, base + 0, right),
            send(at(x, 0, 512), at(x, 0, 512), sems, base + 1, left),
        ]
        self.two = [
            send(at(xl, 0, 256), at(xl, 0, 256), sems, base + 2, right),
            send(at(xr, 256, 256), at(xr, 256, 256), sems, base + 3, left),
        ]

    def start(self):
        for c in self.one:
            c.start()

    def turn(self):
        for a, b in zip(self.one, self.two):
            a.wait_recv()
            b.start()

    def finish(self):
        for a in self.one:
            a.wait_send()
        for b in self.two:
            b.wait()


class RingSum:
    def __init__(self, me, part, rows, hop, got, sems, base):
        x = me.x
        self.part, self.rows, self.hop, self.got, self.x = part, rows, hop, got, x
        right, left = me.by_x(1), me.by_x(3)
        far, xr, xl = (x + 2) % 4, (x + 1) % 4, (x + 3) % 4
        self.xr, self.xl = xr, xl

        def at(b, off):
            return part.at[rows, lanes(b * 512 + off, 256)]

        self.one = [
            send(at(far, 0), hop.at[0], sems, base + 0, right),
            send(at(far, 256), hop.at[1], sems, base + 1, left),
            send(at(xr, 256), got.at[0, :, pl.ds(256, 256)], sems, base + 2, right),
            send(at(xl, 0), got.at[1, :, pl.ds(0, 256)], sems, base + 3, left),
        ]
        self.two = [
            send(at(xr, 0), got.at[0, :, pl.ds(0, 256)], sems, base + 4, right),
            send(at(xl, 256), got.at[1, :, pl.ds(256, 256)], sems, base + 5, left),
        ]

    def start(self):
        for c in self.one:
            c.start()

    def turn(self):
        for k, (b, off) in enumerate(((self.xr, 0), (self.xl, 256))):
            self.one[k].wait_recv()
            cols = lanes(b * 512 + off, 256)
            total = self.part[self.rows, cols].astype(F32) + self.hop[k].astype(F32)
            self.part[self.rows, cols] = total.astype(BF16)
            self.two[k].start()

    def finish(self):
        for k in (2, 3):
            self.one[k].wait_recv()
        for c in self.two:
            c.wait_recv()
        own = self.part[self.rows, lanes(self.x * 512, 512)].astype(F32)
        return own + self.got[0].astype(F32) + self.got[1].astype(F32)

    def drain(self):
        for c in self.one + self.two:
            c.wait_send()


def rope_rows(a, b, cosine, sine):
    return a * cosine - b * sine, b * cosine + a * sine


def document_starts(ids, seq, place):
    ids = ids[seq]

    def below(number):
        hit = (ids < number).astype(F32)
        return jnp.sum(jnp.sum(hit, 1, keepdims=True), 0, keepdims=True)

    second, third = below(3 * seq + 1).astype(jnp.int32), below(3 * seq + 2).astype(jnp.int32)
    return jnp.where(place >= third, third, jnp.where(place >= second, second, 0))


ORIGINAL = [(p % 2) * 4 + p // 2 for p in range(8)]


def device_order_row(ref):
    return jnp.concatenate([ref[:, b * 256:(b + 1) * 256].astype(F32) for b in ORIGINAL], 1)


def rms_rows(src, gain, dst, rstd, first, count):
    def step(k, carry):
        rows = pl.ds(pl.multiple_of(first + k * 64, 64), 64)
        v = src[rows, :].astype(F32)
        r = lax.rsqrt(jnp.sum(v * v, 1, keepdims=True) * (1.0 / 2048.0) + eps)
        rstd[rows, :] = r
        dst[rows, :] = (v * r * gain).astype(BF16)
        return carry

    lax.fori_loop(0, count // 64, step, 0)


def column_squares(value):
    return jnp.sum(value * value, 0, keepdims=True)


class GradSum:
    def __init__(self, me, own, land, out, rows, halves, sems, base):
        self.me, self.own, self.land, self.out, self.rows, self.halves = me, own, land, out, rows, halves
        self.sems, self.base = sems, base

    def first(self, i):
        me = self.me
        return send(self.own((me.z + 1 + i // 2) % 4, i % 2), self.land(i), self.sems, self.base + i, me.by_z(1 + i // 2))

    def start(self):
        each(6, lambda i: self.first(i).start())

    def add(self, view, others):
        def step(k, carry):
            rows = pl.ds(pl.multiple_of(k * 64, 64), 64)
            total = view[rows, :].astype(F32)
            for other in others:
                total = total + other[rows, :].astype(F32)
            view[rows, :] = total.astype(BF16)
            return carry

        lax.fori_loop(0, self.rows // 64, step, 0)

    def sum_z(self):
        each(6, lambda i: self.first(i).wait_recv())
        for yh in (0, 1):
            self.add(self.own(self.me.z, yh), [self.land(d * 2 + yh) for d in range(3)])
        each(6, lambda i: self.first(i).wait_send())

    def second(self, yh):
        me = self.me
        to = yh * 2 + me.core
        step = (to + 4 - me.y) % 4
        slot = (step + 3) % 4
        copy = pltpu.make_async_remote_copy(
            src_ref=self.own(me.z, yh), dst_ref=self.land(slot), send_sem=self.sems[0].at[self.base + 6 + yh],
            recv_sem=self.sems[1].at[self.base + 6 + slot], device_id=me.at(me.z, to, me.core, me.x), device_id_type=MESH,
        )
        return step, copy

    def send_y(self):
        for yh in (0, 1):
            step, copy = self.second(yh)
            pl.when(step != 0)(copy.start)

    def last(self):
        me = self.me
        view = self.halves(self.own(me.z, me.yh), 1 - me.core)
        return send(view, self.out, self.sems, self.base + 9, me.partner())

    def keep(self):
        me = self.me
        return pltpu.make_async_copy(self.halves(self.own(me.z, me.yh), me.core), self.out, self.sems[0].at[self.base + 10])

    def sum_y(self):
        me = self.me

        def work():
            for slot in range(3):
                pltpu.make_async_remote_copy(
                    src_ref=self.land(slot), dst_ref=self.land(slot), send_sem=self.sems[0].at[self.base + 8],
                    recv_sem=self.sems[1].at[self.base + 6 + slot], device_id=me.partner(), device_id_type=MESH,
                ).wait_recv()
            self.add(self.own(me.z, me.yh), [self.land(slot) for slot in range(3)])
            self.last().start()
            self.keep().start()

        pl.when(me.yl == me.core)(work)

    def finish(self):
        me = self.me

        def sender():
            self.last().wait_send()
            self.keep().wait()

        pl.when(me.yl == me.core)(sender)
        pl.when(me.yl != me.core)(lambda: self.last().wait_recv())
        for yh in (0, 1):
            step, copy = self.second(yh)
            pl.when(step != 0)(copy.wait_send)


class GradSumY(GradSum):
    def __init__(self, me, own, land, extra, out, rows, halves, sems, base):
        super().__init__(me, own, land, out, rows, halves, sems, base)
        self.extra = extra

    def landing(self, step, k):
        return self.extra(k) if step == 3 else self.land((step - 1) * 4 + k)

    def first_y(self, yh, step, k):
        me = self.me
        return pltpu.make_async_remote_copy(
            src_ref=self.own(k, yh), dst_ref=self.landing(step, k), send_sem=self.sems[0].at[self.base + yh * 4 + k],
            recv_sem=self.sems[1].at[self.base + (step - 1) * 4 + k],
            device_id=me.at(me.z, yh * 2 + me.core, me.core, me.x), device_id_type=MESH,
        )

    def steps(self, act):
        me = self.me
        for yh in (0, 1):
            away = (yh * 2 + me.core + 4 - me.y) % 4
            for step in (1, 2, 3):
                pl.when(away == step)(functools.partial(act, yh, step))

    def start(self):
        self.steps(lambda yh, step: each(4, lambda k: self.first_y(yh, step, k).start()))

    def sum_y(self):
        me = self.me

        def work():
            for step in (1, 2, 3):
                each(4, lambda k: self.first_y(0, step, k).wait_recv())

            def one(k):
                self.add(self.own(k, me.yh), [self.landing(step, k) for step in (1, 2, 3)])

            each(4, one)

        pl.when(me.yl == me.core)(work)
        self.steps(lambda yh, step: each(4, lambda k: self.first_y(yh, step, k).wait_send()))

    def second_z(self, d):
        me = self.me
        return send(self.own((me.z + d) % 4, me.yh), self.land(d - 1), self.sems, self.base + 11 + d, me.by_z(d))

    def send_z(self):
        def work():
            for d in (1, 2, 3):
                self.second_z(d).start()

        pl.when(self.me.yl == self.me.core)(work)

    def last(self):
        me = self.me
        view = self.halves(self.own(me.z, me.yh), 1 - me.core)
        return send(view, self.out, self.sems, self.base + 15, me.partner())

    def keep(self):
        me = self.me
        return pltpu.make_async_copy(self.halves(self.own(me.z, me.yh), me.core), self.out, self.sems[0].at[self.base + 16])

    def sum_z(self):
        me = self.me

        def work():
            for d in (1, 2, 3):
                self.second_z(d).wait_recv()
            self.add(self.own(me.z, me.yh), [self.land(d) for d in range(3)])
            self.last().start()
            self.keep().start()

        pl.when(me.yl == me.core)(work)

    def finish(self):
        me = self.me

        def sender():
            for d in (1, 2, 3):
                self.second_z(d).wait_send()
            self.last().wait_send()
            self.keep().wait()

        pl.when(me.yl == me.core)(sender)
        pl.when(me.yl != me.core)(lambda: self.last().wait_recv())


def layer_kernel(
    tok, cot, wq_s, wo_s, wg_s, wu_s, wd_s, w_key, w_value, gain1, gain2, ids,
    o_mixed, o_in, o_q, o_out, o_gate, o_up, o_down, o_kv, o_small, xs,
    xf, cf, mf, h1, h2p, cfp, wq, wo, wg, wu, wd, qt, ot, o_r, kvt, x1, dx1, part, hop, got, acc, mx, sm, lse, delta,
    hid, dg, du, hp, dhf, r1, r2, mix, gains, squares, small, small_r,
    a_s, a_r, w_s, w_r, lsem, hs,
):
    me = Place()
    x, core = me.x, me.core
    h2, kv_tmp = xf, dx1
    acts = (a_s, a_r)
    count = [0]

    def sems(n):
        count[0] += n
        assert count[0] <= ACTS
        return count[0] - n

    def shake(k, peers):
        for peer in peers:
            pl.semaphore_signal(hs.at[k], inc=1, device_id=peer, device_id_type=MESH)

    def unshake(k, peers):
        pl.semaphore_wait(hs.at[k], len(peers))

    xs_line = [me.by_x(i) for i in (1, 2, 3)]
    ys_line = [me.by_y(i) for i in (1, 2, 3)]
    zs_line = [me.by_z(i) for i in (1, 2, 3)]
    four = [me.by_quarter(i) for i in (1, 2, 3)]
    partner = me.partner()
    greet(xs_line + ys_line + zs_line + four)
    slots = weight_slots(wq, wo, wg, wu, wd)
    first_z = (False, True, False, True, False)
    spreads = [
        Spread(me, src, slots[n], first_z[n], (w_s.at[n], w_r.at[n]), lsem.at[2 + n])
        for n, src in enumerate((wq_s, wo_s, wg_s, wu_s, wd_s))
    ]
    in_copies, in_local = reshard_in(me, tok, xf, acts, sems(4), lsem.at[0])
    cot_copies, cot_local = reshard_in(me, cot, cf, acts, sems(4), lsem.at[1])
    for c in in_copies + [in_local]:
        c.start()
    s_q, s_o, s_g, s_u, s_d = spreads
    s_q.start()
    seq = me.z * 2 + me.yh
    chunk_of = (me.quarter, 7 - me.quarter)
    lane = lax.broadcasted_iota(jnp.int32, (1, CHUNK), 1)
    places = [c * CHUNK + lane for c in chunk_of]
    starts = [document_starts(ids, seq, p) for p in places]
    pos = jnp.concatenate([p - s for p, s in zip(places, starts)], 1).astype(F32)
    turn = lax.broadcasted_iota(jnp.int32, (32, 1), 0).astype(F32)
    angle = jnp.exp(-math.log(10000.0) * turn / 32.0) * pos
    cosine, sine = jnp.cos(angle), jnp.sin(angle)
    gains[...] = jnp.zeros(gains.shape, F32)
    squares[...] = jnp.zeros(squares.shape, F32)
    small[...] = jnp.zeros(small.shape, F32)

    for c in in_copies:
        c.wait_recv()
    in_local.wait()
    ring_tok = Ring(me, xf, pl.ds(0, T), acts, sems(4))
    ring_tok.start()
    s_q.turn()
    s_g.start()
    for c in cot_copies + [cot_local]:
        c.start()
    s_d.start()
    s_o.start()
    s_u.start()
    ring_tok.turn()
    ring_cot = Ring(me, cf, pl.ds(0, T), acts, sems(4))
    s_q.cross()
    ring_tok.finish()
    s_g.turn()
    s_d.turn()
    for c in cot_copies:
        c.wait_recv()
    cot_local.wait()
    ring_cot.start()
    for c in in_copies + cot_copies:
        c.wait_send()
    stash = pltpu.make_async_copy(xf, xs, lsem.at[7])
    stash.start()

    rms_rows(xf, device_order_row(gain1), h1, r1, 0, T)
    s_q.finish()
    for n, w in enumerate((w_key, w_value)):
        total = None
        for p, b in enumerate(ORIGINAL):
            d = dot_plain(h1[:, p * 256:(p + 1) * 256], w[b * 256:(b + 1) * 256, :])
            total = d if total is None else total + d
        kv_tmp[n * 256:(n + 1) * 256, :] = total.T
    heads = [pl.multiple_of((2 * g + x // 2) * HEAD, HEAD) for g in (0, 1)]
    for g in (0, 1):
        head = heads[g]
        a, b = rope_rows(kv_tmp[pl.ds(head, 32), :], kv_tmp[pl.ds(head + 32, 32), :], cosine, sine)
        v = kv_tmp[pl.ds(256 + head, HEAD), :]
        for h in (0, 1):
            cols = slice(h * CHUNK, (h + 1) * CHUNK)
            kvt[chunk_of[h], g * 64:g * 64 + 32, :] = a[:, cols].astype(BF16)
            kvt[chunk_of[h], g * 64 + 32:g * 64 + 64, :] = b[:, cols].astype(BF16)
            kvt[chunk_of[h], 128 + g * 64:192 + g * 64, :] = v[:, cols].astype(BF16)
    kv_copies = []
    base = sems(8)
    for h in (0, 1):
        for d in (1, 2, 3):
            block = kvt.at[chunk_of[h]]
            copy = send(block, block, acts, base + h * 4 + d, me.by_quarter(d))
            kv_copies.append((copy, h == 0 or (me.quarter + d) % 4 <= me.quarter, h == 0 or me.quarter <= (me.quarter + 4 - d) % 4))
    for c, goes, _ in kv_copies:
        pl.when(goes)(c.start)
    for n in (0, 1):
        q = dot_plain(h1[...], wq[:, n * 256:(n + 1) * 256]).T
        for hd in range(4):
            at = hd * HEAD
            a, b = rope_rows(q[at:at + 32], q[at + 32:at + 64], cosine, sine)
            qt[n * 256 + at:n * 256 + at + 32, :] = (a * 0.125).astype(BF16)
            qt[n * 256 + at + 32:n * 256 + at + 64, :] = (b * 0.125).astype(BF16)
    ring_cot.turn()
    for c, goes, comes in kv_copies:
        pl.when(comes)(c.wait_recv)
        pl.when(goes)(c.wait_send)
    s_o.turn()

    def row_form(block):
        return block.astype(F32).T.astype(BF16)

    def allowed(h, j):
        at = lax.broadcasted_iota(jnp.int32, (CHUNK, CHUNK), 0) + j * CHUNK
        return (at >= starts[h]) & (at <= places[h])

    def attend_begin():
        mx[...] = jnp.full(mx.shape, -1e30, F32)
        sm[...] = jnp.zeros(sm.shape, F32)
        acc[...] = jnp.zeros(acc.shape, F32)

    def attend(h, low, high):
        cols = slice(h * CHUNK, (h + 1) * CHUNK)

        def step(j, carry):
            ok = allowed(h, j)
            keys = [row_form(kvt[j, g * 64:(g + 1) * 64, :]) for g in (0, 1)]
            for hd in range(8):
                g = hd // 4
                s = jnp.where(ok, dot_plain(keys[g], qt[hd * 64:(hd + 1) * 64, cols]), -1e30)
                old = mx[hd:hd + 1, :]
                new = jnp.maximum(old, jnp.max(s, 0, keepdims=True))
                p = jnp.exp(s - new)
                shrink = jnp.exp(old - new)
                mx[hd:hd + 1, :] = new
                sm[hd:hd + 1, :] = sm[hd:hd + 1, :] * shrink + jnp.sum(p, 0, keepdims=True)
                acc[hd * 64:(hd + 1) * 64, :] = acc[hd * 64:(hd + 1) * 64, :] * shrink + dot_plain(
                    kvt[j, 128 + g * 64:192 + g * 64, :], p.astype(BF16)
                )
            return carry

        lax.fori_loop(low, high, step, 0)

    def attend_end(h):
        cols = slice(h * CHUNK, (h + 1) * CHUNK)
        lse[h] = mx[...] + jnp.log(sm[...])
        for hd in range(8):
            rows = slice(hd * 64, (hd + 1) * 64)
            acc[rows, :] = acc[rows, :] / sm[hd:hd + 1, :]
        ot[:, cols] = acc[...].astype(BF16)
        o_r[cols, :] = acc[...].T.astype(BF16)

    def rows_of(h):
        return pl.ds(h * CHUNK, CHUNK)

    def project(h):
        rows = rows_of(h)

        def step(n, carry):
            cols = lanes(n * 256, 256)
            part[rows, cols] = dot_plain(o_r[rows, :], wo[:, cols]).astype(BF16)
            return carry

        lax.fori_loop(0, 8, step, 0)

    def ring_sums():
        return [RingSum(me, part, rows_of(h), hop.at[h], got.at[h], acts, sems(6)) for h in (0, 1)]

    def rings():
        return [Ring(me, mf, rows_of(h), acts, sems(4)) for h in (0, 1)]

    sums, ring = ring_sums(), rings()
    own = lanes(x * 512, 512)

    def stream(h):
        rows = rows_of(h)
        mine = xf[rows, own].astype(F32)
        total = mine + sums[h].finish()
        squares[0:1, :] += column_squares(mine)
        squares[1:2, :] += column_squares(total)
        x1[rows, :] = total
        mf[rows, own] = total.astype(BF16)

    attend_begin()
    attend(0, 0, chunk_of[0] + 1)
    attend_end(0)
    s_u.turn()
    s_o.cross()
    s_o.finish()
    project(0)
    sums[0].start()
    attend_begin()
    attend(1, 0, 3)
    sums[0].turn()
    attend(1, 3, chunk_of[1] + 1)
    attend_end(1)
    stream(0)
    ring[0].start()
    project(1)
    sums[1].start()
    ring[0].turn()
    sums[1].turn()
    stream(1)
    ring[1].start()
    ring_cot.finish()
    cot_over = send(cf, cfp, acts, sems(1), partner)
    cot_over.start()
    stash.wait()
    ring[0].finish()

    row_two = device_order_row(gain2)
    rms_rows(mf, row_two, h2, r2, 0, CHUNK)
    for s in spreads[2:]:
        s.cross()
    ring[1].turn()
    for s in spreads[2:]:
        s.finish()

    def feed_forward(h):
        rows = rows_of(h)

        def step(b, carry):
            for at, size in ((0, 256), (256, 256), (512, 192)):
                cols = slice(at, at + size)
                gate = dot_plain(h2[rows, :], wg[b, :, cols])
                up = dot_plain(h2[rows, :], wu[b, :, cols])
                d_hidden = dot_nt(cf[rows, :], wd[b, cols, :])
                sigma = 1.0 / (1.0 + jnp.exp(-gate))
                active = gate * sigma
                hid[b, rows, cols] = (active * up).astype(BF16)
                dg[b, rows, cols] = (d_hidden * up * sigma * (1.0 + gate * (1.0 - sigma))).astype(BF16)
                du[b, rows, cols] = (d_hidden * active).astype(BF16)
            return carry

        lax.fori_loop(0, 2, step, 0)

    def norm_back(h, u_ref, rstd, gain, k):
        def step(i, carry):
            at = pl.multiple_of(i * 64, 64)
            full = pl.ds(pl.multiple_of(h * CHUNK + i * 64, 64), 64)
            d = dhf[pl.ds(at, 64), :]
            u = u_ref[full, :].astype(F32)
            r = rstd[full, :]
            scaled = d * gain
            inner = jnp.sum(scaled * u, 1, keepdims=True)
            part[full, :] = (r * scaled - u * (r * r * r * (1.0 / 2048.0) * inner)).astype(BF16)
            gains[k:k + 1, :] += jnp.sum(d * u * r, 0, keepdims=True)
            return carry

        lax.fori_loop(0, CHUNK // 64, step, 0)

    def back_two(h):
        rows = rows_of(h)

        def step(n, carry):
            feats = lanes(n * 256, 256)
            total = dot_nt(dg[0, rows, :], wg[0, feats, :]) + dot_nt(dg[1, rows, :], wg[1, feats, :])
            total = total + dot_nt(du[0, rows, :], wu[0, feats, :]) + dot_nt(du[1, rows, :], wu[1, feats, :])
            dhf[:, feats] = total
            return carry

        lax.fori_loop(0, 8, step, 0)
        norm_back(h, mf, r2, row_two, 1)

    feed_forward(0)
    back_two_sums, ring_two = ring_sums(), rings()
    ring[1].finish()
    sums[0].drain()
    back_two(0)
    back_two_sums[0].start()
    rms_rows(mf, row_two, h2, r2, CHUNK, CHUNK)
    feed_forward(1)
    h2_over = send(h2, h2p, acts, sems(1), partner)
    h2_over.start()
    base = sems(3)
    hid_over = [send(ref.at[1 - core], hp.at[n], acts, base + n, partner) for n, ref in enumerate((hid, dg, du))]
    for c in hid_over:
        c.start()
    back_two_sums[0].turn()
    sums[1].drain()
    back_two(1)
    back_two_sums[1].start()

    def d_stream(h):
        rows = rows_of(h)
        total = cf[rows, own].astype(F32) + back_two_sums[h].finish()
        dx1[rows, :] = total
        mf[rows, own] = total.astype(BF16)

    d_stream(0)
    ring_two[0].start()
    ff = wg.shape[2]

    def row_slot(w):
        return lambda z, yh: w.at[core, lanes((z % 2) * 1024 + yh * 512 + (z // 2) * 256, 256)]

    def row_land(w):
        return lambda i: w.at[1 - core, lanes(i * 256, 256)]

    def row_half(v, c):
        return v.at[lanes(c * 128, 128)]

    gate_sum = GradSum(me, row_slot(wg), row_land(wg), o_gate, 256, row_half, acts, sems(11))
    up_sum = GradSumY(
        me, row_slot(wu), row_land(wu), lambda k: hp.at[1 + k // 2, lanes((k % 2) * 256, 256)], o_up, 256, row_half, acts, sems(17)
    )
    down_sum = GradSum(
        me, lambda z, yh: wd.at[core, :, lanes((z % 2) * 1024 + yh * 512 + (z // 2) * 256, 256)],
        lambda i: wd.at[1 - core, :, lanes(i * 256, 256)], o_down, ff, lambda v, c: v.at[:, lanes(c * 128, 128)], acts, sems(11),
    )
    out_sum = GradSum(
        me, lambda z, yh: wo.at[lanes(core * 256, 256), lanes((z % 2) * 1024 + yh * 512 + (z // 2) * 256, 256)],
        lambda i: wo.at[lanes((1 - core) * 256, 256), lanes(i * 256, 256)], o_out, 256,
        lambda v, c: v.at[:, lanes(c * 128, 128)], acts, sems(11),
    )
    query_sum = GradSum(
        me, lambda z, yh: h2.at[pl.ds(0, 256), lanes((z % 2) * 1024 + yh * 512 + (z // 2) * 256, 256)],
        lambda i: h2.at[pl.ds(256, 256), lanes(i * 256, 256)], o_q, 256,
        lambda v, c: v.at[:, lanes(c * 128, 128)], acts, sems(11),
    )
    h2_over.wait()
    for c in hid_over:
        c.wait()
    cot_over.wait()

    def feed(h):
        rows = rows_of(h)

        def step(n, carry):
            cols = lanes(n * 256, 256)
            part[rows, cols] = (dot_plain(hid[0, rows, :], wd[0, :, cols]) + dot_plain(hid[1, rows, :], wd[1, :, cols])).astype(BF16)
            return carry

        lax.fori_loop(0, 8, step, 0)

    def grads_in(low, high):
        def step(m, carry):
            feats = lanes(m * 256, 256)
            mine = h2[:, feats].T
            other = h2p[:, feats].T
            wg[core, feats, :] = (dot_plain(mine, dg[core]) + dot_plain(other, hp[1])).astype(BF16)
            wu[core, feats, :] = (dot_plain(mine, du[core]) + dot_plain(other, hp[2])).astype(BF16)
            return carry

        lax.fori_loop(low, high, step, 0)

    grads_in(0, 4)
    back_two_sums[1].turn()
    ring_two[0].turn()
    grads_in(4, 8)
    shake(7, zs_line + ys_line)
    d_stream(1)
    ring_two[1].start()
    unshake(7, zs_line + ys_line)
    up_sum.start()
    gate_sum.start()
    ring_two[0].finish()
    for h in (0, 1):
        back_two_sums[h].drain()
    feed_sums = ring_sums()
    feed(0)
    feed(1)
    ring_two[1].turn()
    feed_sums[0].start()

    for at, size in ((0, 256), (256, 256), (512, 192)):
        mine = hid[core, :, at:at + size].T
        other = hp[0, :, at:at + size].T

        def down(n, carry):
            cols = lanes(n * 512, 512)
            wd[core, at:at + size, cols] = (dot_plain(mine, cf[:, cols]) + dot_plain(other, cfp[:, cols])).astype(BF16)
            return carry

        lax.fori_loop(0, 4, down, 0)

    shake(0, zs_line + ys_line + four)
    unstash = pltpu.make_async_copy(xs, cf, lsem.at[7])
    unstash.start()

    def d_attended(h):
        cols = slice(h * CHUNK, (h + 1) * CHUNK)
        rows = rows_of(h)
        for k in (0, 1):
            feats = slice(k * 256, (k + 1) * 256)
            d = dot_nt(wo[feats, :], mf[rows, :])
            o_r[feats, cols] = d.astype(BF16)
            both = d.astype(BF16).astype(F32) * ot[feats, cols].astype(F32)
            for hd in range(4):
                delta[h, k * 4 + hd:k * 4 + hd + 1, :] = jnp.sum(both[hd * 64:(hd + 1) * 64], 0, keepdims=True)

    def attend_back(h, low, high):
        cols = slice(h * CHUNK, (h + 1) * CHUNK)

        def step(j, carry):
            ok = allowed(h, j)
            keys_at = lanes(j * CHUNK, CHUNK)
            for g in (0, 1):
                key_t = kvt[j, g * 64:(g + 1) * 64, :]
                key, value = row_form(key_t), row_form(kvt[j, 128 + g * 64:192 + g * 64, :])
                ps, ds = [], []
                for hd in range(4 * g, 4 * g + 4):
                    feats = slice(hd * 64, (hd + 1) * 64)
                    s = jnp.where(ok, dot_plain(key, qt[feats, cols]), -1e30)
                    p = jnp.exp(s - lse[h, hd:hd + 1, :])
                    dp = dot_plain(value, o_r[feats, cols])
                    d = (p * (dp - delta[h, hd:hd + 1, :])).astype(BF16)
                    acc[feats, :] += dot_plain(key_t, d)
                    ps.append(p.astype(BF16))
                    ds.append(d)
                q4 = jnp.concatenate([qt[hd * 64:(hd + 1) * 64, cols] for hd in range(4 * g, 4 * g + 4)], 1)
                do4 = jnp.concatenate([o_r[hd * 64:(hd + 1) * 64, cols] for hd in range(4 * g, 4 * g + 4)], 1)
                dhf[g * 64:(g + 1) * 64, keys_at] += dot_nt(q4, jnp.concatenate(ds, 1))
                dhf[128 + g * 64:192 + g * 64, keys_at] += dot_nt(do4, jnp.concatenate(ps, 1))
            return carry

        lax.fori_loop(low, high, step, 0)

    def attend_back_end(h):
        cols = slice(h * CHUNK, (h + 1) * CHUNK)
        for hd in range(8):
            at = hd * 64
            a, b = rope_rows(acc[at:at + 32, :] * 0.125, acc[at + 32:at + 64, :] * 0.125, cosine[:, cols], -sine[:, cols])
            acc[at:at + 32, :] = a
            acc[at + 32:at + 64, :] = b
        qt[:, cols] = acc[...].astype(BF16)
        du[0, rows_of(h), 0:512] = acc[...].T.astype(BF16)

    d_attended(0)
    dhf[...] = jnp.zeros(dhf.shape, F32)
    acc[...] = jnp.zeros(acc.shape, F32)
    unshake(0, zs_line + ys_line + four)
    down_sum.start()
    base = sems(5)
    h1_over = send(h1, cfp, acts, base, partner)
    ot_over = send(ot.at[lanes((1 - core) * 256, 256)], hp.at[0, pl.ds(0, 256), pl.ds(0, 512)], acts, base + 1, partner)
    da_over = send(mf, h2p, acts, base + 2, partner)
    dq_over = send(qt.at[lanes((1 - core) * 256, 256)], hp.at[0, pl.ds(256, 256), pl.ds(0, 512)], acts, base + 3, partner)
    dkv_over = send(dg.at[1, lanes(256 + (1 - core) * 128, 128), pl.ds(0, 512)], o_r.at[pl.ds(0, 128)], acts, base + 4, partner)
    h1_over.start()
    ot_over.start()
    attend_back(0, 0, chunk_of[0] + 1)
    attend_back_end(0)
    ring_two[1].finish()
    feed_sums[1].start()
    feed_sums[0].turn()
    da_over.start()
    d_attended(1)
    acc[...] = jnp.zeros(acc.shape, F32)

    def mixed_rows(h):
        rows = rows_of(h)
        total = x1[rows, :] + feed_sums[h].finish()
        squares[2:3, :] += column_squares(total)
        mix[rows, :] = total.astype(BF16)

    def homeward(src, home, at):
        def piece(q):
            half, block = q // 2, q % 2
            row = jnp.where(half == 0, me.quarter, 3 - me.quarter)
            return (
                src.at[lanes(half * 256, 256), lanes(block * 256, 256)],
                home.at[pl.ds(pl.multiple_of(row * CHUNK, CHUNK), CHUNK)],
            )

        copies = []
        for d in (1, 2, 3):
            s, t = piece((me.quarter + d) % 4)
            copies.append(send(s, t, acts, at + d, me.by_quarter(d)))
        s, t = piece(me.quarter)
        copies.append(pltpu.make_async_copy(s, t, acts[0].at[at]))
        return copies

    attend_back(1, 0, 3)
    feed_sums[1].turn()
    attend_back(1, 3, chunk_of[1] + 1)
    attend_back_end(1)
    dq_over.start()

    def dkv_slot(ref, k):
        return ref.at[k // 4, pl.ds(((k // 2) % 2) * 256, 256), pl.ds((k % 2) * 256, 256)]

    for j in range(8):
        dkv_slot(hid, j)[...] = dhf[:, j * CHUNK:(j + 1) * CHUNK].astype(BF16)
    base = sems(8)
    dkv_copies = []
    for d in (1, 2, 3):
        q = (me.quarter + d) % 4
        for h, k in ((0, q), (1, 7 - q)):
            src = hid.at[k // 4, lanes(((k // 2) % 2) * 256, 256), lanes((k % 2) * 256, 256)]
            copy = send(src, dkv_slot(dg, (d - 1) * 2 + h), acts, base + h * 4 + d, me.by_quarter(d))
            dkv_copies.append((copy, h == 0 or me.quarter <= q, h == 0 or (me.quarter + 4 - d) % 4 <= me.quarter))
    for c, goes, _ in dkv_copies:
        pl.when(goes)(c.start)
    mixed_rows(0)
    mixed_rows(1)
    feed_sums[0].drain()
    feed_sums[1].drain()
    shake(1, [me.by_x(1), me.by_x(3)])
    home_mixed = homeward(mix, o_mixed, sems(4))
    da_over.wait()
    ot_over.wait()

    def out_grad(n, carry):
        cols = lanes(n * 256, 256)
        wo[lanes(core * 256, 256), cols] = (
            dot_plain(ot[lanes(core * 256, 256), :], mf[:, cols]) + dot_plain(hp[0, 0:256, 0:512], h2p[:, cols])
        ).astype(BF16)
        return carry

    lax.fori_loop(0, 8, out_grad, 0)
    shake(3, xs_line + ys_line + zs_line)
    unshake(3, xs_line + ys_line + zs_line)
    out_sum.start()
    up_sum.sum_y()
    shake(4, zs_line)
    for c, _, comes in dkv_copies:
        pl.when(comes)(c.wait_recv)
    x1[...] = jnp.zeros(x1.shape, F32)
    for h in (0, 1):
        cols = slice(h * CHUNK, (h + 1) * CHUNK)
        total = dhf[:, lanes(chunk_of[h] * CHUNK, CHUNK)]
        for d in range(3):
            got_one = dkv_slot(dg, d * 2 + h)[...].astype(F32)
            if h == 1:
                got_one = jnp.where((me.quarter + 3 - d) % 4 <= me.quarter, got_one, 0.0)
            total = total + got_one
        for g in (0, 1):
            a, b = rope_rows(total[g * 64:g * 64 + 32], total[g * 64 + 32:g * 64 + 64], cosine[:, cols], -sine[:, cols])
            v = total[128 + g * 64:192 + g * 64]
            x1[pl.ds(heads[g], 32), cols] = a
            x1[pl.ds(heads[g] + 32, 32), cols] = b
            x1[pl.ds(256 + heads[g], 64), cols] = v
            dg[1, 256 + g * 64:288 + g * 64, cols] = a.astype(BF16)
            dg[1, 288 + g * 64:320 + g * 64, cols] = b.astype(BF16)
            dg[1, 384 + g * 64:448 + g * 64, cols] = v.astype(BF16)
    dkv_over.start()
    du[1, :, 0:512] = x1[...].T.astype(BF16)
    for c, goes, _ in dkv_copies:
        pl.when(goes)(c.wait_send)
    unstash.wait()

    def back_one(h):
        rows = rows_of(h)

        def step(n, carry):
            feats = lanes(n * 256, 256)
            orig = lanes(((n % 2) * 4 + n // 2) * 256, 256)
            total = dot_nt(du[0, rows, 0:512], wq[feats, :])
            total = total + dot_nt(du[1, rows, 0:256], w_key[orig, :]) + dot_nt(du[1, rows, 256:512], w_value[orig, :])
            dhf[:, feats] = total
            return carry

        lax.fori_loop(0, 8, step, 0)
        norm_back(h, cf, r1, row_one, 0)

    row_one = device_order_row(gain1)
    unshake(1, [me.by_x(1), me.by_x(3)])
    for c in home_mixed:
        c.start()
    one_sums = ring_sums()
    back_one(0)
    one_sums[0].start()
    dkv_over.wait()
    h1_over.wait()

    def kv_grads(n, carry):
        cols = lanes(n * 256, 256)
        mf[256:384, cols] = (
            dot_plain(dg[1, lanes(256 + core * 128, 128), 0:512], h1[:, cols]) + dot_plain(o_r[0:128, :], cfp[:, cols])
        ).astype(BF16)
        return carry

    lax.fori_loop(0, 8, kv_grads, 0)
    base = sems(25)
    kv_z = [
        send(mf.at[pl.ds(256, 128), lanes(((me.z + d) % 4) * 512, 512)], mf.at[pl.ds(384, 128), pl.ds((d - 1) * 512, 512)],
             acts, base + d, me.by_z(d)) for d in (1, 2, 3)
    ]
    for c in kv_z:
        c.start()
    back_one(1)
    one_sums[1].start()
    for k in range(2):
        small[k:k + 1, :] = gains[0:1, k * 1024:(k + 1) * 1024]
        small[2 + k:3 + k, :] = gains[1:2, k * 1024:(k + 1) * 1024]
    small[4:7, 0:512] = squares[0:3, :]

    def small_copies(n, peers, at):
        return [send(small, small_r.at[n, d], acts, at + d, p) for d, p in enumerate(peers)]

    def small_add(n, copies):
        for c in copies:
            c.wait()
        total = small[...]
        for d in range(len(copies)):
            total = total + small_r[n, d]
        small[...] = total

    small_z = small_copies(0, zs_line, sems(3))
    for c in small_z:
        c.start()
    one_sums[0].turn()
    for c in kv_z:
        c.wait()
    z_at = lanes(me.z * 512, 512)
    mf[256:384, z_at] = (
        mf[256:384, z_at].astype(F32) + mf[384:512, 0:512].astype(F32) + mf[384:512, 512:1024].astype(F32)
        + mf[384:512, 1024:1536].astype(F32)
    ).astype(BF16)
    kv_y = [
        send(mf.at[pl.ds(256, 128), lanes(me.z * 512 + ((me.y + d) % 4) * 128, 128)],
             mf.at[pl.ds(384, 128), pl.ds(1536 + (d - 1) * 128, 128)], acts, base + 3 + d, me.by_y(d)) for d in (1, 2, 3)
    ]
    for c in kv_y:
        c.start()
    small_add(0, small_z)
    small_y = small_copies(1, ys_line, sems(3))
    for c in small_y:
        c.start()
    dq_over.wait()

    def query_grad(n, carry):
        cols = lanes(n * 256, 256)
        h2[0:256, cols] = (
            dot_plain(qt[lanes(core * 256, 256), :], h1[:, cols]) + dot_plain(hp[0, 256:512, 0:512], cfp[:, cols])
        ).astype(BF16)
        return carry

    lax.fori_loop(0, 8, query_grad, 0)
    query_sum.start()
    one_sums[1].turn()
    unshake(4, zs_line)
    up_sum.send_z()
    for c in kv_y:
        c.wait()
    zy_at = lanes(me.z * 512 + me.y * 128, 128)
    mf[256:384, zy_at] = (
        mf[256:384, zy_at].astype(F32) + mf[384:512, 1536:1664].astype(F32) + mf[384:512, 1664:1792].astype(F32)
        + mf[384:512, 1792:1920].astype(F32)
    ).astype(BF16)
    pair = me.at(me.z, me.y, core, x + 1 - 2 * (x % 2))
    kv_pair = send(mf.at[pl.ds(256, 128), zy_at], mf.at[pl.ds(384, 128), pl.ds(1920, 128)], acts, base + 7, pair)
    kv_pair.start()
    small_add(1, small_y)
    small_x = small_copies(2, xs_line, sems(3))
    for c in small_x:
        c.start()
    for c in home_mixed:
        c.wait()

    def in_rows(h):
        rows = rows_of(h)
        mix[rows, :] = (dx1[rows, :] + one_sums[h].finish()).astype(BF16)

    in_rows(0)
    kv_pair.wait()
    mine = mf[pl.ds(pl.multiple_of(256 + (x % 2) * 64, 64), 64), zy_at].astype(F32)
    mine = mine + mf[pl.ds(pl.multiple_of(384 + (x % 2) * 64, 64), 64), 1920:2048].astype(F32)
    head_at = pl.ds(pl.multiple_of((2 * (x % 2) + x // 2) * 64, 64), 64)
    mf[head_at, zy_at] = mine.astype(BF16)
    kv_x = [send(mf.at[head_at, zy_at], mf.at[head_at, zy_at], acts, base + 7 + d, me.by_x(d)) for d in (1, 2, 3)]
    for c in kv_x:
        c.start()
    gate_sum.sum_z()
    shake(2, ys_line)
    small_add(2, small_x)
    small_c = small_copies(3, [partner], sems(1))
    for c in small_c:
        c.start()
    for c in kv_x:
        c.wait()
    block = mf.at[pl.ds(0, 256), zy_at]
    kv_y2 = [send(block, block, acts, base + 11 + d, me.by_y(d)) for d in (1, 2, 3)]
    for c in kv_y2:
        c.start()
    in_rows(1)
    home_in = homeward(mix, o_in, sems(4))
    for c in home_in:
        c.start()
    unshake(2, ys_line)
    gate_sum.send_y()
    for c in kv_y2:
        c.wait()
    block2 = mf.at[pl.ds(0, 256), z_at]
    kv_z2 = [send(block2, block2, acts, base + 15 + d, me.by_z(d)) for d in (1, 2, 3)]
    for c in kv_z2:
        c.start()
    small_add(3, small_c)
    small_out = pltpu.make_async_copy(small, o_small, lsem.at[8])
    small_out.start()
    down_sum.sum_z()
    shake(5, ys_line)
    out_sum.sum_z()
    query_sum.sum_z()
    shake(6, ys_line)
    up_sum.sum_z()
    unshake(5, ys_line)
    down_sum.send_y()
    unshake(6, ys_line)
    out_sum.send_y()
    query_sum.send_y()
    for c in kv_z2:
        c.wait()
    kv_last = send(mf.at[pl.ds(0, 256)], mf.at[pl.ds(256, 256)], acts, base + 20, partner)
    kv_last.start()
    flights = []

    def lay_out(home, first, k):
        for p, b in enumerate(ORIGINAL):
            spot = (k * 8 + p) % 4
            if len(flights) >= 4:
                flights[-4].wait()
            stage = x1.at[pl.ds((spot // 2) * 256, 256), pl.ds((spot % 2) * 256, 256)]
            x1[(spot // 2) * 256:(spot // 2 + 1) * 256, (spot % 2) * 256:(spot % 2 + 1) * 256] = (
                mf[first:first + 256, p * 256:(p + 1) * 256].astype(F32).T
            )
            copy = pltpu.make_async_copy(stage, home.at[pl.ds(b * 256, 256)], lsem.at[10 + spot])
            copy.start()
            flights.append(copy)

    lay_out(o_kv.at[core], 0, 0)
    gate_sum.sum_y()
    kv_last.wait()
    lay_out(o_kv.at[1 - core], 256, 1)
    down_sum.sum_y()
    out_sum.sum_y()
    query_sum.sum_y()
    for c in flights[-4:]:
        c.wait()
    for s in (gate_sum, up_sum, down_sum, out_sum, query_sum):
        s.finish()
    for c in home_in:
        c.wait()
    for h in (0, 1):
        one_sums[h].drain()
    small_out.wait()


ACTS = 270


def layer(tok, cot, wq, wo, wg, wu, wd, w_key, w_value, gain1, gain2, ids):
    ff = wg.shape[1]
    sds = jax.ShapeDtypeStruct
    outs = [
        sds((1024, 256), BF16), sds((1024, 256), BF16), sds((256, 128), BF16), sds((256, 128), BF16),
        sds((128, ff), BF16), sds((128, ff), BF16), sds((ff, 128), BF16), sds((2, 2048, 256), F32), sds((8, 1024), F32),
        sds((T, 2048), BF16),
    ]
    dma = pltpu.SemaphoreType.DMA
    vm = pl.BlockSpec(memory_space=pltpu.VMEM)
    wide = pltpu.VMEM((T, 2048), BF16)
    square = pltpu.VMEM((T, 512), BF16)
    inner = pltpu.VMEM((2, T, ff), BF16)
    row8 = pltpu.VMEM((8, CHUNK), F32)
    pair8 = pltpu.VMEM((2, 8, CHUNK), F32)
    return pl.pallas_call(
        layer_kernel, out_shape=outs, in_specs=[ANY] * 7 + [vm] * 5, out_specs=[ANY] * len(outs),
        scratch_shapes=[
            wide, wide, wide, wide, wide, wide,
            pltpu.VMEM((2048, 512), BF16), pltpu.VMEM((512, 2048), BF16),
            pltpu.VMEM((2, 2048, ff), BF16), pltpu.VMEM((2, 2048, ff), BF16), pltpu.VMEM((2, ff, 2048), BF16),
            square, square, square, pltpu.VMEM((8, 256, CHUNK), BF16),
            pltpu.VMEM((T, 512), F32), pltpu.VMEM((T, 512), F32),
            wide, pltpu.VMEM((2, 2, 256, 256), BF16), pltpu.VMEM((2, 2, 256, 512), BF16),
            pltpu.VMEM((512, CHUNK), F32), row8, row8, pair8, pair8,
            inner, inner, inner, pltpu.VMEM((3, T, ff), BF16), pltpu.VMEM((CHUNK, 2048), F32),
            pltpu.VMEM((T, 1), F32), pltpu.VMEM((T, 1), F32), square,
            pltpu.VMEM((2, 2048), F32), pltpu.VMEM((8, 512), F32), pltpu.VMEM((8, 1024), F32), pltpu.VMEM((4, 3, 8, 1024), F32),
            dma((ACTS,)), dma((ACTS,)), dma((5, 31)), dma((5, 31)), dma((14,)), pltpu.SemaphoreType.REGULAR((9,)),
        ],
        compiler_params=pltpu.CompilerParams(collective_id=0, has_side_effects=True, vmem_limit_bytes=64 << 20),
    )(tok, cot, wq, wo, wg, wu, wd, w_key, w_value, gain1, gain2, ids)


def from_device_order(v):
    return v.reshape((4, 2, 256) + v.shape[1:]).swapaxes(0, 1).reshape(v.shape)


def shards(tokens, segment_ids, norm_one, w_query, w_key, w_value, w_out, norm_two, w_gate, w_up, w_down, cotangent):
    mixed, input_grad, gq, go, gg, gu, gd, gkv, small, _ = layer(
        tokens, cotangent, w_query, w_out, w_gate, w_up, w_down, w_key, w_value,
        norm_one.reshape(1, 2048), norm_two.reshape(1, 2048), segment_ids.reshape(8, 16, 128),
    )
    key_total, value_total = gkv[0], gkv[1]
    rms = jnp.sqrt(jnp.sum(small[4:7, :512], 1) / (16384 * 2048))
    return (
        mixed, input_grad.astype(F32), gq.T.astype(F32), key_total, value_total, go.astype(F32), gg.astype(F32), gu.astype(F32),
        gd.astype(F32), from_device_order(small[0:2].reshape(2048)), from_device_order(small[2:4].reshape(2048)), rms,
    )


def solution(mesh):
    return jax.shard_map(
        shards,
        mesh=mesh,
        in_specs=(
            P("row", "col"), P(), P(), P("row", "col"), P(), P(), P("col", "row"), P(),
            P("row", "col"), P("row", "col"), P("col", "row"), P("row", "col"),
        ),
        out_specs=(
            P("row", "col"), P("row", "col"), P("row", "col"), P(), P(), P("col", "row"),
            P("row", "col"), P("row", "col"), P("col", "row"), P(), P(), P(),
        ),
        check_vma=False,
    )
```

```python
import functools
import math

import jax
import jax.numpy as jnp
from jax import lax
from jax.experimental import pallas as pl
from jax.experimental.pallas import tpu as pltpu
from jax.sharding import PartitionSpec as P

BF16 = jnp.bfloat16
F32 = jnp.float32
HEAD = 64
eps = 1e-05
MESH = pl.DeviceIdType.MESH
ANY = pl.BlockSpec(memory_space=pl.ANY)
CHUNK = 256
T = 512


class Place:
    def __init__(self):
        row = lax.axis_index("row")
        col = lax.axis_index("col")
        self.z = row // 4
        self.yh = (row // 2) % 2
        self.core = row % 2
        self.yl = col // 4
        self.x = col % 4
        self.y = self.yh * 2 + self.yl
        self.quarter = self.core * 2 + self.yl

    def at(self, z, y, core, x):
        return {"row": z * 4 + (y // 2) * 2 + core, "col": (y % 2) * 4 + x}

    def by_x(self, d):
        return self.at(self.z, self.y, self.core, (self.x + d) % 4)

    def by_z(self, d):
        return self.at((self.z + d) % 4, self.y, self.core, self.x)

    def by_y(self, d):
        return self.at(self.z, (self.y + d) % 4, self.core, self.x)

    def partner(self):
        return self.at(self.z, self.y, 1 - self.core, self.x)

    def by_quarter(self, d):
        q = (self.quarter + d) % 4
        return self.at(self.z, self.yh * 2 + q % 2, q // 2, self.x)


def greet(peers):
    barrier = pltpu.get_barrier_semaphore()
    for peer in peers:
        pl.semaphore_signal(barrier, inc=1, device_id=peer, device_id_type=MESH)
    pl.semaphore_wait(barrier, len(peers))


def send(src, dst, sems, k, peer):
    return pltpu.make_async_remote_copy(
        src_ref=src, dst_ref=dst, send_sem=sems[0].at[k], recv_sem=sems[1].at[k],
        device_id=peer, device_id_type=MESH,
    )


def each(count, act):
    def step(i, carry):
        act(i)
        return carry

    lax.fori_loop(0, count, step, 0)


def perm_row(z, y, core):
    yh = y // 2
    return ((z % 2) * 2 + yh) * 512 + (z // 2) * 256 + core * 128


def reshard_in(me, src, full, sems, base, lsem):
    def chunk(q):
        return src.at[pl.ds(pl.multiple_of(jnp.where(me.core == 0, q, 3 - q) * CHUNK, CHUNK), CHUNK)]

    half = pl.multiple_of(me.core * CHUNK, CHUNK)
    place = full.at[pl.ds(half, CHUNK), pl.ds(pl.multiple_of(me.x * 512 + me.yl * 256, 256), 256)]
    copies = []
    for d in (1, 2, 3):
        copies.append(send(chunk((me.quarter + d) % 4), place, sems, base + d, me.by_quarter(d)))
    local = pltpu.make_async_copy(chunk(me.quarter), place, lsem)
    return copies, local


class Spread:
    def __init__(self, me, src, slot, z_first, sems, lsem):
        self.me, self.src, self.slot, self.z_first, self.sems, self.lsem = me, src, slot, z_first, sems, lsem

    def local(self):
        me = self.me
        return pltpu.make_async_copy(self.src, self.slot(me.z, me.y, me.core), self.lsem)

    def first(self, i):
        me = self.me
        peer = me.by_z(i + 1) if self.z_first else me.by_y(i + 1)
        return send(self.src, self.slot(me.z, me.y, me.core), self.sems, i, peer)

    def line(self, k):
        me = self.me
        if self.z_first:
            return self.slot((me.z + 4 - k) % 4, me.y, me.core)
        return self.slot(me.z, (me.y + 4 - k) % 4, me.core)

    def second(self, k, i):
        me = self.me
        peer = me.by_y(i + 1) if self.z_first else me.by_z(i + 1)
        block = self.line(k)
        return send(block, block, self.sems, 3 + k * 3 + i, peer)

    def third(self, i):
        me = self.me
        if self.z_first:
            block = self.slot((me.z + 4 - i // 4) % 4, (me.y + 4 - i % 4) % 4, me.core)
        else:
            block = self.slot((me.z + 4 - i % 4) % 4, (me.y + 4 - i // 4) % 4, me.core)
        return send(block, block, self.sems, 15 + i, me.partner())

    def start(self):
        self.local().start()
        each(3, lambda i: self.first(i).start())

    def turn(self):
        self.local().wait()
        each(3, lambda i: self.second(0, i).start())
        self.third(0).start()

        def arrived(k):
            self.first(k).wait_recv()
            each(3, lambda i: self.second(k + 1, i).start())
            self.third((k + 1) * 4).start()

        each(3, arrived)

    def cross(self, k=None):
        def arrived(j):
            n, i = j // 3, j % 3
            self.second(n, i).wait_recv()
            self.third(n * 4 + i + 1).start()

        if k is None:
            each(12, arrived)
        else:
            each(3, lambda i: arrived(k * 3 + i))

    def finish(self):
        each(16, lambda i: self.third(i).wait_recv())
        each(3, lambda i: self.first(i).wait_send())
        each(12, lambda j: self.second(j // 3, j % 3).wait_send())
        each(16, lambda i: self.third(i).wait_send())


def weight_slots(q, o, g, u, d):
    def ds(start, size):
        return pl.ds(pl.multiple_of(start, 128), size)

    return (
        lambda z, y, c: q.at[ds(perm_row(z, y, c), 128), ds((y % 2) * 256, 256)],
        lambda z, y, c: o.at[ds((y % 2) * 256, 256), ds(perm_row(z, y, c), 128)],
        lambda z, y, c: g.at[y % 2, ds(perm_row(z, y, c), 128)],
        lambda z, y, c: u.at[y % 2, ds(perm_row(z, y, c), 128)],
        lambda z, y, c: d.at[y % 2, :, ds(perm_row(z, y, c), 128)],
    )


def dot_plain(left, right):
    return jnp.dot(left, right, preferred_element_type=F32)


def dot_tn(left, right):
    return lax.dot_general(left, right, (((0,), (0,)), ((), ())), preferred_element_type=F32)


def dot_nt(left, right):
    return lax.dot_general(left, right, (((1,), (1,)), ((), ())), preferred_element_type=F32)


def lanes(start, size):
    return pl.ds(pl.multiple_of(start, 128), size)


class Ring:
    def __init__(self, me, full, rows, sems, base):
        x = me.x
        right, left = me.by_x(1), me.by_x(3)
        xl, xr = (x + 3) % 4, (x + 1) % 4

        def at(b, off, size):
            return full.at[rows, lanes(b * 512 + off, size)]

        self.one = [
            send(at(x, 0, 512), at(x, 0, 512), sems, base + 0, right),
            send(at(x, 0, 512), at(x, 0, 512), sems, base + 1, left),
        ]
        self.two = [
            send(at(xl, 0, 256), at(xl, 0, 256), sems, base + 2, right),
            send(at(xr, 256, 256), at(xr, 256, 256), sems, base + 3, left),
        ]

    def start(self):
        for c in self.one:
            c.start()

    def turn(self):
        for a, b in zip(self.one, self.two):
            a.wait_recv()
            b.start()

    def finish(self):
        for a in self.one:
            a.wait_send()
        for b in self.two:
            b.wait()


class RingSum:
    def __init__(self, me, part, rows, hop, got, sems, base):
        x = me.x
        self.part, self.rows, self.hop, self.got, self.x = part, rows, hop, got, x
        right, left = me.by_x(1), me.by_x(3)
        far, xr, xl = (x + 2) % 4, (x + 1) % 4, (x + 3) % 4
        self.xr, self.xl = xr, xl

        def at(b, off):
            return part.at[rows, lanes(b * 512 + off, 256)]

        self.one = [
            send(at(far, 0), hop.at[0], sems, base + 0, right),
            send(at(far, 256), hop.at[1], sems, base + 1, left),
            send(at(xr, 256), got.at[0, :, pl.ds(256, 256)], sems, base + 2, right),
            send(at(xl, 0), got.at[1, :, pl.ds(0, 256)], sems, base + 3, left),
        ]
        self.two = [
            send(at(xr, 0), got.at[0, :, pl.ds(0, 256)], sems, base + 4, right),
            send(at(xl, 256), got.at[1, :, pl.ds(256, 256)], sems, base + 5, left),
        ]

    def start(self):
        for c in self.one:
            c.start()

    def turn(self):
        for k, (b, off) in enumerate(((self.xr, 0), (self.xl, 256))):
            self.one[k].wait_recv()
            cols = lanes(b * 512 + off, 256)
            total = self.part[self.rows, cols].astype(F32) + self.hop[k].astype(F32)
            self.part[self.rows, cols] = total.astype(BF16)
            self.two[k].start()

    def finish(self):
        for k in (2, 3):
            self.one[k].wait_recv()
        for c in self.two:
            c.wait_recv()
        own = self.part[self.rows, lanes(self.x * 512, 512)].astype(F32)
        return own + self.got[0].astype(F32) + self.got[1].astype(F32)

    def drain(self):
        for c in self.one + self.two:
            c.wait_send()


def rope_rows(a, b, cosine, sine):
    return a * cosine - b * sine, b * cosine + a * sine


def document_starts(ids, seq, place):
    ids = ids[seq]

    def below(number):
        hit = (ids < number).astype(F32)
        return jnp.sum(jnp.sum(hit, 1, keepdims=True), 0, keepdims=True)

    second, third = below(3 * seq + 1).astype(jnp.int32), below(3 * seq + 2).astype(jnp.int32)
    return jnp.where(place >= third, third, jnp.where(place >= second, second, 0))


ORIGINAL = [(p % 2) * 4 + p // 2 for p in range(8)]


def device_order_row(ref):
    return jnp.concatenate([ref[:, b * 256:(b + 1) * 256].astype(F32) for b in ORIGINAL], 1)


def rms_rows(src, gain, dst, rstd, first, count):
    def step(k, carry):
        rows = pl.ds(pl.multiple_of(first + k * 64, 64), 64)
        v = src[rows, :].astype(F32)
        r = lax.rsqrt(jnp.sum(v * v, 1, keepdims=True) * (1.0 / 2048.0) + eps)
        rstd[rows, :] = r
        dst[rows, :] = (v * r * gain).astype(BF16)
        return carry

    lax.fori_loop(0, count // 64, step, 0)


def column_squares(value):
    return jnp.sum(value * value, 0, keepdims=True)


class GradSum:
    def __init__(self, me, own, land, out, rows, halves, sems, base):
        self.me, self.own, self.land, self.out, self.rows, self.halves = me, own, land, out, rows, halves
        self.sems, self.base = sems, base

    def first(self, i):
        me = self.me
        return send(self.own((me.z + 1 + i // 2) % 4, i % 2), self.land(i), self.sems, self.base + i, me.by_z(1 + i // 2))

    def start(self):
        each(6, lambda i: self.first(i).start())

    def add(self, view, others):
        def step(k, carry):
            rows = pl.ds(pl.multiple_of(k * 64, 64), 64)
            total = view[rows, :].astype(F32)
            for other in others:
                total = total + other[rows, :].astype(F32)
            view[rows, :] = total.astype(BF16)
            return carry

        lax.fori_loop(0, self.rows // 64, step, 0)

    def sum_z(self):
        each(6, lambda i: self.first(i).wait_recv())
        for yh in (0, 1):
            self.add(self.own(self.me.z, yh), [self.land(d * 2 + yh) for d in range(3)])
        each(6, lambda i: self.first(i).wait_send())

    def second(self, yh):
        me = self.me
        to = yh * 2 + me.core
        step = (to + 4 - me.y) % 4
        slot = (step + 3) % 4
        copy = pltpu.make_async_remote_copy(
            src_ref=self.own(me.z, yh), dst_ref=self.land(slot), send_sem=self.sems[0].at[self.base + 6 + yh],
            recv_sem=self.sems[1].at[self.base + 6 + slot], device_id=me.at(me.z, to, me.core, me.x), device_id_type=MESH,
        )
        return step, copy

    def send_y(self):
        for yh in (0, 1):
            step, copy = self.second(yh)
            pl.when(step != 0)(copy.start)

    def last(self):
        me = self.me
        view = self.halves(self.own(me.z, me.yh), 1 - me.core)
        return send(view, self.out, self.sems, self.base + 9, me.partner())

    def keep(self):
        me = self.me
        return pltpu.make_async_copy(self.halves(self.own(me.z, me.yh), me.core), self.out, self.sems[0].at[self.base + 10])

    def sum_y(self):
        me = self.me

        def work():
            for slot in range(3):
                pltpu.make_async_remote_copy(
                    src_ref=self.land(slot), dst_ref=self.land(slot), send_sem=self.sems[0].at[self.base + 8],
                    recv_sem=self.sems[1].at[self.base + 6 + slot], device_id=me.partner(), device_id_type=MESH,
                ).wait_recv()
            self.add(self.own(me.z, me.yh), [self.land(slot) for slot in range(3)])
            self.last().start()
            self.keep().start()

        pl.when(me.yl == me.core)(work)

    def finish(self):
        me = self.me

        def sender():
            self.last().wait_send()
            self.keep().wait()

        pl.when(me.yl == me.core)(sender)
        pl.when(me.yl != me.core)(lambda: self.last().wait_recv())
        for yh in (0, 1):
            step, copy = self.second(yh)
            pl.when(step != 0)(copy.wait_send)


class GradSumY(GradSum):
    def __init__(self, me, own, land, extra, out, rows, halves, sems, base):
        super().__init__(me, own, land, out, rows, halves, sems, base)
        self.extra = extra

    def landing(self, step, k):
        return self.extra(k) if step == 3 else self.land((step - 1) * 4 + k)

    def first_y(self, yh, step, k):
        me = self.me
        return pltpu.make_async_remote_copy(
            src_ref=self.own(k, yh), dst_ref=self.landing(step, k), send_sem=self.sems[0].at[self.base + yh * 4 + k],
            recv_sem=self.sems[1].at[self.base + (step - 1) * 4 + k],
            device_id=me.at(me.z, yh * 2 + me.core, me.core, me.x), device_id_type=MESH,
        )

    def steps(self, act):
        me = self.me
        for yh in (0, 1):
            away = (yh * 2 + me.core + 4 - me.y) % 4
            for step in (1, 2, 3):
                pl.when(away == step)(functools.partial(act, yh, step))

    def start(self):
        self.steps(lambda yh, step: each(4, lambda k: self.first_y(yh, step, k).start()))

    def sum_y(self):
        me = self.me

        def work():
            for step in (1, 2, 3):
                each(4, lambda k: self.first_y(0, step, k).wait_recv())

            def one(k):
                self.add(self.own(k, me.yh), [self.landing(step, k) for step in (1, 2, 3)])

            each(4, one)

        pl.when(me.yl == me.core)(work)
        self.steps(lambda yh, step: each(4, lambda k: self.first_y(yh, step, k).wait_send()))

    def second_z(self, d):
        me = self.me
        return send(self.own((me.z + d) % 4, me.yh), self.land(d - 1), self.sems, self.base + 11 + d, me.by_z(d))

    def send_z(self):
        def work():
            for d in (1, 2, 3):
                self.second_z(d).start()

        pl.when(self.me.yl == self.me.core)(work)

    def last(self):
        me = self.me
        view = self.halves(self.own(me.z, me.yh), 1 - me.core)
        return send(view, self.out, self.sems, self.base + 15, me.partner())

    def keep(self):
        me = self.me
        return pltpu.make_async_copy(self.halves(self.own(me.z, me.yh), me.core), self.out, self.sems[0].at[self.base + 16])

    def sum_z(self):
        me = self.me

        def work():
            for d in (1, 2, 3):
                self.second_z(d).wait_recv()
            self.add(self.own(me.z, me.yh), [self.land(d) for d in range(3)])
            self.last().start()
            self.keep().start()

        pl.when(me.yl == me.core)(work)

    def finish(self):
        me = self.me

        def sender():
            for d in (1, 2, 3):
                self.second_z(d).wait_send()
            self.last().wait_send()
            self.keep().wait()

        pl.when(me.yl == me.core)(sender)
        pl.when(me.yl != me.core)(lambda: self.last().wait_recv())


def layer_kernel(
    tok, cot, wq_s, wo_s, wg_s, wu_s, wd_s, w_key, w_value, gain1, gain2, ids,
    o_mixed, o_in, o_q, o_out, o_gate, o_up, o_down, o_kv, o_small, xs,
    xf, cf, mf, h1, h2p, cfp, wq, wo, wg, wu, wd, qt, ot, o_r, kvt, x1, dx1, part, hop, got, acc, mx, sm, lse, delta,
    hid, dg, du, hp, dhf, r1, r2, mix, gains, squares, small, small_r,
    a_s, a_r, w_s, w_r, lsem, hs,
):
    me = Place()
    x, core = me.x, me.core
    h2, kv_tmp = xf, dx1
    acts = (a_s, a_r)
    count = [0]

    def sems(n):
        count[0] += n
        assert count[0] <= ACTS
        return count[0] - n

    def shake(k, peers):
        for peer in peers:
            pl.semaphore_signal(hs.at[k], inc=1, device_id=peer, device_id_type=MESH)

    def unshake(k, peers):
        pl.semaphore_wait(hs.at[k], len(peers))

    xs_line = [me.by_x(i) for i in (1, 2, 3)]
    ys_line = [me.by_y(i) for i in (1, 2, 3)]
    zs_line = [me.by_z(i) for i in (1, 2, 3)]
    four = [me.by_quarter(i) for i in (1, 2, 3)]
    partner = me.partner()
    greet(xs_line + ys_line + zs_line + four)
    slots = weight_slots(wq, wo, wg, wu, wd)
    first_z = (False, True, False, True, False)
    spreads = [
        Spread(me, src, slots[n], first_z[n], (w_s.at[n], w_r.at[n]), lsem.at[2 + n])
        for n, src in enumerate((wq_s, wo_s, wg_s, wu_s, wd_s))
    ]
    in_copies, in_local = reshard_in(me, tok, xf, acts, sems(4), lsem.at[0])
    cot_copies, cot_local = reshard_in(me, cot, cf, acts, sems(4), lsem.at[1])
    for c in in_copies + [in_local]:
        c.start()
    s_q, s_o, s_g, s_u, s_d = spreads
    s_q.start()
    seq = me.z * 2 + me.yh
    chunk_of = (me.quarter, 7 - me.quarter)
    lane = lax.broadcasted_iota(jnp.int32, (1, CHUNK), 1)
    places = [c * CHUNK + lane for c in chunk_of]
    starts = [document_starts(ids, seq, p) for p in places]
    pos = jnp.concatenate([p - s for p, s in zip(places, starts)], 1).astype(F32)
    turn = lax.broadcasted_iota(jnp.int32, (32, 1), 0).astype(F32)
    angle = jnp.exp(-math.log(10000.0) * turn / 32.0) * pos
    cosine, sine = jnp.cos(angle), jnp.sin(angle)
    gains[...] = jnp.zeros(gains.shape, F32)
    squares[...] = jnp.zeros(squares.shape, F32)
    small[...] = jnp.zeros(small.shape, F32)

    for c in in_copies:
        c.wait_recv()
    in_local.wait()
    ring_tok = Ring(me, xf, pl.ds(0, T), acts, sems(4))
    ring_tok.start()
    s_q.turn()
    s_g.start()
    for c in cot_copies + [cot_local]:
        c.start()
    s_d.start()
    s_o.start()
    s_u.start()
    ring_tok.turn()
    ring_cot = Ring(me, cf, pl.ds(0, T), acts, sems(4))
    s_q.cross()
    ring_tok.finish()
    s_g.turn()
    s_d.turn()
    for c in cot_copies:
        c.wait_recv()
    cot_local.wait()
    ring_cot.start()
    for c in in_copies + cot_copies:
        c.wait_send()
    stash = pltpu.make_async_copy(xf, xs, lsem.at[7])
    stash.start()

    rms_rows(xf, device_order_row(gain1), h1, r1, 0, T)
    s_q.finish()
    for n, w in enumerate((w_key, w_value)):
        total = None
        for p, b in enumerate(ORIGINAL):
            d = dot_plain(h1[:, p * 256:(p + 1) * 256], w[b * 256:(b + 1) * 256, :])
            total = d if total is None else total + d
        kv_tmp[n * 256:(n + 1) * 256, :] = total.T
    heads = [pl.multiple_of((2 * g + x // 2) * HEAD, HEAD) for g in (0, 1)]
    for g in (0, 1):
        head = heads[g]
        a, b = rope_rows(kv_tmp[pl.ds(head, 32), :], kv_tmp[pl.ds(head + 32, 32), :], cosine, sine)
        v = kv_tmp[pl.ds(256 + head, HEAD), :]
        for h in (0, 1):
            cols = slice(h * CHUNK, (h + 1) * CHUNK)
            kvt[chunk_of[h], g * 64:g * 64 + 32, :] = a[:, cols].astype(BF16)
            kvt[chunk_of[h], g * 64 + 32:g * 64 + 64, :] = b[:, cols].astype(BF16)
            kvt[chunk_of[h], 128 + g * 64:192 + g * 64, :] = v[:, cols].astype(BF16)
    kv_copies = []
    base = sems(8)
    for h in (0, 1):
        for d in (1, 2, 3):
            block = kvt.at[chunk_of[h]]
            copy = send(block, block, acts, base + h * 4 + d, me.by_quarter(d))
            kv_copies.append((copy, h == 0 or (me.quarter + d) % 4 <= me.quarter, h == 0 or me.quarter <= (me.quarter + 4 - d) % 4))
    for c, goes, _ in kv_copies:
        pl.when(goes)(c.start)
    for n in (0, 1):
        q = dot_plain(h1[...], wq[:, n * 256:(n + 1) * 256]).T
        for hd in range(4):
            at = hd * HEAD
            a, b = rope_rows(q[at:at + 32], q[at + 32:at + 64], cosine, sine)
            qt[n * 256 + at:n * 256 + at + 32, :] = (a * 0.125).astype(BF16)
            qt[n * 256 + at + 32:n * 256 + at + 64, :] = (b * 0.125).astype(BF16)
    ring_cot.turn()
    for c, goes, comes in kv_copies:
        pl.when(comes)(c.wait_recv)
        pl.when(goes)(c.wait_send)
    s_o.turn()

    def row_form(block):
        return block.astype(F32).T.astype(BF16)

    def allowed(h, j):
        at = lax.broadcasted_iota(jnp.int32, (CHUNK, CHUNK), 0) + j * CHUNK
        return (at >= starts[h]) & (at <= places[h])

    def attend_begin():
        mx[...] = jnp.full(mx.shape, -1e30, F32)
        sm[...] = jnp.zeros(sm.shape, F32)
        acc[...] = jnp.zeros(acc.shape, F32)

    def attend(h, low, high):
        cols = slice(h * CHUNK, (h + 1) * CHUNK)

        def step(j, carry):
            ok = allowed(h, j)
            keys = [row_form(kvt[j, g * 64:(g + 1) * 64, :]) for g in (0, 1)]
            for hd in range(8):
                g = hd // 4
                s = jnp.where(ok, dot_plain(keys[g], qt[hd * 64:(hd + 1) * 64, cols]), -1e30)
                old = mx[hd:hd + 1, :]
                new = jnp.maximum(old, jnp.max(s, 0, keepdims=True))
                p = jnp.exp(s - new)
                shrink = jnp.exp(old - new)
                mx[hd:hd + 1, :] = new
                sm[hd:hd + 1, :] = sm[hd:hd + 1, :] * shrink + jnp.sum(p, 0, keepdims=True)
                acc[hd * 64:(hd + 1) * 64, :] = acc[hd * 64:(hd + 1) * 64, :] * shrink + dot_plain(
                    kvt[j, 128 + g * 64:192 + g * 64, :], p.astype(BF16)
                )
            return carry

        lax.fori_loop(low, high, step, 0)

    def attend_end(h):
        cols = slice(h * CHUNK, (h + 1) * CHUNK)
        lse[h] = mx[...] + jnp.log(sm[...])
        for hd in range(8):
            rows = slice(hd * 64, (hd + 1) * 64)
            acc[rows, :] = acc[rows, :] / sm[hd:hd + 1, :]
        ot[:, cols] = acc[...].astype(BF16)
        o_r[cols, :] = acc[...].T.astype(BF16)

    def rows_of(h):
        return pl.ds(h * CHUNK, CHUNK)

    def project(h):
        rows = rows_of(h)

        def step(n, carry):
            cols = lanes(n * 256, 256)
            part[rows, cols] = dot_plain(o_r[rows, :], wo[:, cols]).astype(BF16)
            return carry

        lax.fori_loop(0, 8, step, 0)

    def ring_sums():
        return [RingSum(me, part, rows_of(h), hop.at[h], got.at[h], acts, sems(6)) for h in (0, 1)]

    def rings():
        return [Ring(me, mf, rows_of(h), acts, sems(4)) for h in (0, 1)]

    sums, ring = ring_sums(), rings()
    own = lanes(x * 512, 512)

    def stream(h):
        rows = rows_of(h)
        mine = xf[rows, own].astype(F32)
        total = mine + sums[h].finish()
        squares[0:1, :] += column_squares(mine)
        squares[1:2, :] += column_squares(total)
        x1[rows, :] = total
        mf[rows, own] = total.astype(BF16)

    attend_begin()
    attend(0, 0, chunk_of[0] + 1)
    attend_end(0)
    s_u.turn()
    s_o.cross()
    s_o.finish()
    project(0)
    sums[0].start()
    attend_begin()
    attend(1, 0, 3)
    sums[0].turn()
    attend(1, 3, chunk_of[1] + 1)
    attend_end(1)
    stream(0)
    ring[0].start()
    project(1)
    sums[1].start()
    ring[0].turn()
    sums[1].turn()
    stream(1)
    ring[1].start()
    ring_cot.finish()
    cot_over = send(cf, cfp, acts, sems(1), partner)
    cot_over.start()
    stash.wait()
    ring[0].finish()

    row_two = device_order_row(gain2)
    rms_rows(mf, row_two, h2, r2, 0, CHUNK)
    for s in spreads[2:]:
        s.cross()
    ring[1].turn()
    for s in spreads[2:]:
        s.finish()

    def feed_forward(h):
        rows = rows_of(h)

        def step(b, carry):
            for at, size in ((0, 256), (256, 256), (512, 192)):
                cols = slice(at, at + size)
                gate = dot_plain(h2[rows, :], wg[b, :, cols])
                up = dot_plain(h2[rows, :], wu[b, :, cols])
                d_hidden = dot_nt(cf[rows, :], wd[b, cols, :])
                sigma = 1.0 / (1.0 + jnp.exp(-gate))
                active = gate * sigma
                hid[b, rows, cols] = (active * up).astype(BF16)
                dg[b, rows, cols] = (d_hidden * up * sigma * (1.0 + gate * (1.0 - sigma))).astype(BF16)
                du[b, rows, cols] = (d_hidden * active).astype(BF16)
            return carry

        lax.fori_loop(0, 2, step, 0)

    def norm_back(h, u_ref, rstd, gain, k):
        def step(i, carry):
            at = pl.multiple_of(i * 64, 64)
            full = pl.ds(pl.multiple_of(h * CHUNK + i * 64, 64), 64)
            d = dhf[pl.ds(at, 64), :]
            u = u_ref[full, :].astype(F32)
            r = rstd[full, :]
            scaled = d * gain
            inner = jnp.sum(scaled * u, 1, keepdims=True)
            part[full, :] = (r * scaled - u * (r * r * r * (1.0 / 2048.0) * inner)).astype(BF16)
            gains[k:k + 1, :] += jnp.sum(d * u * r, 0, keepdims=True)
            return carry

        lax.fori_loop(0, CHUNK // 64, step, 0)

    def back_two(h):
        rows = rows_of(h)

        def step(n, carry):
            feats = lanes(n * 256, 256)
            total = dot_nt(dg[0, rows, :], wg[0, feats, :]) + dot_nt(dg[1, rows, :], wg[1, feats, :])
            total = total + dot_nt(du[0, rows, :], wu[0, feats, :]) + dot_nt(du[1, rows, :], wu[1, feats, :])
            dhf[:, feats] = total
            return carry

        lax.fori_loop(0, 8, step, 0)
        norm_back(h, mf, r2, row_two, 1)

    feed_forward(0)
    back_two_sums, ring_two = ring_sums(), rings()
    ring[1].finish()
    sums[0].drain()
    back_two(0)
    back_two_sums[0].start()
    rms_rows(mf, row_two, h2, r2, CHUNK, CHUNK)
    feed_forward(1)
    h2_over = send(h2, h2p, acts, sems(1), partner)
    h2_over.start()
    base = sems(3)
    hid_over = [send(ref.at[1 - core], hp.at[n], acts, base + n, partner) for n, ref in enumerate((hid, dg, du))]
    for c in hid_over:
        c.start()
    back_two_sums[0].turn()
    sums[1].drain()
    back_two(1)
    back_two_sums[1].start()

    def d_stream(h):
        rows = rows_of(h)
        total = cf[rows, own].astype(F32) + back_two_sums[h].finish()
        dx1[rows, :] = total
        mf[rows, own] = total.astype(BF16)

    d_stream(0)
    ring_two[0].start()
    ff = wg.shape[2]

    def row_slot(w):
        return lambda z, yh: w.at[core, lanes((z % 2) * 1024 + yh * 512 + (z // 2) * 256, 256)]

    def row_land(w):
        return lambda i: w.at[1 - core, lanes(i * 256, 256)]

    def row_half(v, c):
        return v.at[lanes(c * 128, 128)]

    gate_sum = GradSum(me, row_slot(wg), row_land(wg), o_gate, 256, row_half, acts, sems(11))
    up_sum = GradSumY(
        me, row_slot(wu), row_land(wu), lambda k: hp.at[1 + k // 2, lanes((k % 2) * 256, 256)], o_up, 256, row_half, acts, sems(17)
    )
    down_sum = GradSum(
        me, lambda z, yh: wd.at[core, :, lanes((z % 2) * 1024 + yh * 512 + (z // 2) * 256, 256)],
        lambda i: wd.at[1 - core, :, lanes(i * 256, 256)], o_down, ff, lambda v, c: v.at[:, lanes(c * 128, 128)], acts, sems(11),
    )
    out_sum = GradSum(
        me, lambda z, yh: wo.at[lanes(core * 256, 256), lanes((z % 2) * 1024 + yh * 512 + (z // 2) * 256, 256)],
        lambda i: wo.at[lanes((1 - core) * 256, 256), lanes(i * 256, 256)], o_out, 256,
        lambda v, c: v.at[:, lanes(c * 128, 128)], acts, sems(11),
    )
    query_sum = GradSum(
        me, lambda z, yh: h2.at[pl.ds(0, 256), lanes((z % 2) * 1024 + yh * 512 + (z // 2) * 256, 256)],
        lambda i: h2.at[pl.ds(256, 256), lanes(i * 256, 256)], o_q, 256,
        lambda v, c: v.at[:, lanes(c * 128, 128)], acts, sems(11),
    )
    h2_over.wait()
    for c in hid_over:
        c.wait()
    cot_over.wait()

    def feed(h):
        rows = rows_of(h)

        def step(n, carry):
            cols = lanes(n * 256, 256)
            part[rows, cols] = (dot_plain(hid[0, rows, :], wd[0, :, cols]) + dot_plain(hid[1, rows, :], wd[1, :, cols])).astype(BF16)
            return carry

        lax.fori_loop(0, 8, step, 0)

    def grads_in(low, high):
        def step(m, carry):
            feats = lanes(m * 256, 256)
            mine = h2[:, feats].T
            other = h2p[:, feats].T
            wg[core, feats, :] = (dot_plain(mine, dg[core]) + dot_plain(other, hp[1])).astype(BF16)
            wu[core, feats, :] = (dot_plain(mine, du[core]) + dot_plain(other, hp[2])).astype(BF16)
            return carry

        lax.fori_loop(low, high, step, 0)

    grads_in(0, 4)
    back_two_sums[1].turn()
    ring_two[0].turn()
    grads_in(4, 8)
    shake(7, zs_line + ys_line)
    d_stream(1)
    ring_two[1].start()
    unshake(7, zs_line + ys_line)
    up_sum.start()
    gate_sum.start()
    ring_two[0].finish()
    for h in (0, 1):
        back_two_sums[h].drain()
    feed_sums = ring_sums()
    feed(0)
    feed(1)
    ring_two[1].turn()
    feed_sums[0].start()

    for at, size in ((0, 256), (256, 256), (512, 192)):
        mine = hid[core, :, at:at + size].T
        other = hp[0, :, at:at + size].T

        def down(n, carry):
            cols = lanes(n * 512, 512)
            wd[core, at:at + size, cols] = (dot_plain(mine, cf[:, cols]) + dot_plain(other, cfp[:, cols])).astype(BF16)
            return carry

        lax.fori_loop(0, 4, down, 0)

    shake(0, zs_line + ys_line + four)
    unstash = pltpu.make_async_copy(xs, cf, lsem.at[7])
    unstash.start()

    def d_attended(h):
        cols = slice(h * CHUNK, (h + 1) * CHUNK)
        rows = rows_of(h)
        for k in (0, 1):
            feats = slice(k * 256, (k + 1) * 256)
            d = dot_nt(wo[feats, :], mf[rows, :])
            o_r[feats, cols] = d.astype(BF16)
            both = d.astype(BF16).astype(F32) * ot[feats, cols].astype(F32)
            for hd in range(4):
                delta[h, k * 4 + hd:k * 4 + hd + 1, :] = jnp.sum(both[hd * 64:(hd + 1) * 64], 0, keepdims=True)

    def attend_back(h, low, high):
        cols = slice(h * CHUNK, (h + 1) * CHUNK)

        def step(j, carry):
            ok = allowed(h, j)
            keys_at = lanes(j * CHUNK, CHUNK)
            for g in (0, 1):
                key_t = kvt[j, g * 64:(g + 1) * 64, :]
                key, value = row_form(key_t), row_form(kvt[j, 128 + g * 64:192 + g * 64, :])
                ps, ds = [], []
                for hd in range(4 * g, 4 * g + 4):
                    feats = slice(hd * 64, (hd + 1) * 64)
                    s = jnp.where(ok, dot_plain(key, qt[feats, cols]), -1e30)
                    p = jnp.exp(s - lse[h, hd:hd + 1, :])
                    dp = dot_plain(value, o_r[feats, cols])
                    d = (p * (dp - delta[h, hd:hd + 1, :])).astype(BF16)
                    acc[feats, :] += dot_plain(key_t, d)
                    ps.append(p.astype(BF16))
                    ds.append(d)
                q4 = jnp.concatenate([qt[hd * 64:(hd + 1) * 64, cols] for hd in range(4 * g, 4 * g + 4)], 1)
                do4 = jnp.concatenate([o_r[hd * 64:(hd + 1) * 64, cols] for hd in range(4 * g, 4 * g + 4)], 1)
                dhf[g * 64:(g + 1) * 64, keys_at] += dot_nt(q4, jnp.concatenate(ds, 1))
                dhf[128 + g * 64:192 + g * 64, keys_at] += dot_nt(do4, jnp.concatenate(ps, 1))
            return carry

        lax.fori_loop(low, high, step, 0)

    def attend_back_end(h):
        cols = slice(h * CHUNK, (h + 1) * CHUNK)
        for hd in range(8):
            at = hd * 64
            a, b = rope_rows(acc[at:at + 32, :] * 0.125, acc[at + 32:at + 64, :] * 0.125, cosine[:, cols], -sine[:, cols])
            acc[at:at + 32, :] = a
            acc[at + 32:at + 64, :] = b
        qt[:, cols] = acc[...].astype(BF16)
        du[0, rows_of(h), 0:512] = acc[...].T.astype(BF16)

    d_attended(0)
    dhf[...] = jnp.zeros(dhf.shape, F32)
    acc[...] = jnp.zeros(acc.shape, F32)
    unshake(0, zs_line + ys_line + four)
    down_sum.start()
    base = sems(5)
    h1_over = send(h1, cfp, acts, base, partner)
    ot_over = send(ot.at[lanes((1 - core) * 256, 256)], hp.at[0, pl.ds(0, 256), pl.ds(0, 512)], acts, base + 1, partner)
    da_over = send(mf, h2p, acts, base + 2, partner)
    dq_over = send(qt.at[lanes((1 - core) * 256, 256)], hp.at[0, pl.ds(256, 256), pl.ds(0, 512)], acts, base + 3, partner)
    dkv_over = send(dg.at[1, lanes(256 + (1 - core) * 128, 128), pl.ds(0, 512)], o_r.at[pl.ds(0, 128)], acts, base + 4, partner)
    h1_over.start()
    ot_over.start()
    attend_back(0, 0, chunk_of[0] + 1)
    attend_back_end(0)
    ring_two[1].finish()
    feed_sums[1].start()
    feed_sums[0].turn()
    da_over.start()
    d_attended(1)
    acc[...] = jnp.zeros(acc.shape, F32)

    def mixed_rows(h):
        rows = rows_of(h)
        total = x1[rows, :] + feed_sums[h].finish()
        squares[2:3, :] += column_squares(total)
        mix[rows, :] = total.astype(BF16)

    def homeward(src, home, at):
        def piece(q):
            half, block = q // 2, q % 2
            row = jnp.where(half == 0, me.quarter, 3 - me.quarter)
            return (
                src.at[lanes(half * 256, 256), lanes(block * 256, 256)],
                home.at[pl.ds(pl.multiple_of(row * CHUNK, CHUNK), CHUNK)],
            )

        copies = []
        for d in (1, 2, 3):
            s, t = piece((me.quarter + d) % 4)
            copies.append(send(s, t, acts, at + d, me.by_quarter(d)))
        s, t = piece(me.quarter)
        copies.append(pltpu.make_async_copy(s, t, acts[0].at[at]))
        return copies

    attend_back(1, 0, 3)
    feed_sums[1].turn()
    attend_back(1, 3, chunk_of[1] + 1)
    attend_back_end(1)
    dq_over.start()

    def dkv_slot(ref, k):
        return ref.at[k // 4, pl.ds(((k // 2) % 2) * 256, 256), pl.ds((k % 2) * 256, 256)]

    for j in range(8):
        dkv_slot(hid, j)[...] = dhf[:, j * CHUNK:(j + 1) * CHUNK].astype(BF16)
    base = sems(8)
    dkv_copies = []
    for d in (1, 2, 3):
        q = (me.quarter + d) % 4
        for h, k in ((0, q), (1, 7 - q)):
            src = hid.at[k // 4, lanes(((k // 2) % 2) * 256, 256), lanes((k % 2) * 256, 256)]
            copy = send(src, dkv_slot(dg, (d - 1) * 2 + h), acts, base + h * 4 + d, me.by_quarter(d))
            dkv_copies.append((copy, h == 0 or me.quarter <= q, h == 0 or (me.quarter + 4 - d) % 4 <= me.quarter))
    for c, goes, _ in dkv_copies:
        pl.when(goes)(c.start)
    mixed_rows(0)
    mixed_rows(1)
    feed_sums[0].drain()
    feed_sums[1].drain()
    shake(1, [me.by_x(1), me.by_x(3)])
    home_mixed = homeward(mix, o_mixed, sems(4))
    da_over.wait()
    ot_over.wait()

    def out_grad(n, carry):
        cols = lanes(n * 256, 256)
        wo[lanes(core * 256, 256), cols] = (
            dot_plain(ot[lanes(core * 256, 256), :], mf[:, cols]) + dot_plain(hp[0, 0:256, 0:512], h2p[:, cols])
        ).astype(BF16)
        return carry

    lax.fori_loop(0, 8, out_grad, 0)
    shake(3, xs_line + ys_line + zs_line)
    unshake(3, xs_line + ys_line + zs_line)
    up_sum.sum_y()
    shake(4, zs_line)
    for c, _, comes in dkv_copies:
        pl.when(comes)(c.wait_recv)
    x1[...] = jnp.zeros(x1.shape, F32)
    for h in (0, 1):
        cols = slice(h * CHUNK, (h + 1) * CHUNK)
        total = dhf[:, lanes(chunk_of[h] * CHUNK, CHUNK)]
        for d in range(3):
            got_one = dkv_slot(dg, d * 2 + h)[...].astype(F32)
            if h == 1:
                got_one = jnp.where((me.quarter + 3 - d) % 4 <= me.quarter, got_one, 0.0)
            total = total + got_one
        for g in (0, 1):
            a, b = rope_rows(total[g * 64:g * 64 + 32], total[g * 64 + 32:g * 64 + 64], cosine[:, cols], -sine[:, cols])
            v = total[128 + g * 64:192 + g * 64]
            x1[pl.ds(heads[g], 32), cols] = a
            x1[pl.ds(heads[g] + 32, 32), cols] = b
            x1[pl.ds(256 + heads[g], 64), cols] = v
            dg[1, 256 + g * 64:288 + g * 64, cols] = a.astype(BF16)
            dg[1, 288 + g * 64:320 + g * 64, cols] = b.astype(BF16)
            dg[1, 384 + g * 64:448 + g * 64, cols] = v.astype(BF16)
    dkv_over.start()
    du[1, :, 0:512] = x1[...].T.astype(BF16)
    for c, goes, _ in dkv_copies:
        pl.when(goes)(c.wait_send)
    unstash.wait()

    def back_one(h):
        rows = rows_of(h)

        def step(n, carry):
            feats = lanes(n * 256, 256)
            orig = lanes(((n % 2) * 4 + n // 2) * 256, 256)
            total = dot_nt(du[0, rows, 0:512], wq[feats, :])
            total = total + dot_nt(du[1, rows, 0:256], w_key[orig, :]) + dot_nt(du[1, rows, 256:512], w_value[orig, :])
            dhf[:, feats] = total
            return carry

        lax.fori_loop(0, 8, step, 0)
        norm_back(h, cf, r1, row_one, 0)

    row_one = device_order_row(gain1)
    unshake(1, [me.by_x(1), me.by_x(3)])
    for c in home_mixed:
        c.start()
    one_sums = ring_sums()
    back_one(0)
    one_sums[0].start()
    dkv_over.wait()
    h1_over.wait()

    def kv_grads(n, carry):
        cols = lanes(n * 256, 256)
        mf[256:384, cols] = (
            dot_plain(dg[1, lanes(256 + core * 128, 128), 0:512], h1[:, cols]) + dot_plain(o_r[0:128, :], cfp[:, cols])
        ).astype(BF16)
        return carry

    lax.fori_loop(0, 8, kv_grads, 0)
    base = sems(25)
    kv_z = [
        send(mf.at[pl.ds(256, 128), lanes(((me.z + d) % 4) * 512, 512)], mf.at[pl.ds(384, 128), pl.ds((d - 1) * 512, 512)],
             acts, base + d, me.by_z(d)) for d in (1, 2, 3)
    ]
    for c in kv_z:
        c.start()
    back_one(1)
    one_sums[1].start()
    for k in range(2):
        small[k:k + 1, :] = gains[0:1, k * 1024:(k + 1) * 1024]
        small[2 + k:3 + k, :] = gains[1:2, k * 1024:(k + 1) * 1024]
    small[4:7, 0:512] = squares[0:3, :]

    def small_copies(n, peers, at):
        return [send(small, small_r.at[n, d], acts, at + d, p) for d, p in enumerate(peers)]

    def small_add(n, copies):
        for c in copies:
            c.wait()
        total = small[...]
        for d in range(len(copies)):
            total = total + small_r[n, d]
        small[...] = total

    small_z = small_copies(0, zs_line, sems(3))
    for c in small_z:
        c.start()
    one_sums[0].turn()
    for c in kv_z:
        c.wait()
    z_at = lanes(me.z * 512, 512)
    mf[256:384, z_at] = (
        mf[256:384, z_at].astype(F32) + mf[384:512, 0:512].astype(F32) + mf[384:512, 512:1024].astype(F32)
        + mf[384:512, 1024:1536].astype(F32)
    ).astype(BF16)
    kv_y = [
        send(mf.at[pl.ds(256, 128), lanes(me.z * 512 + ((me.y + d) % 4) * 128, 128)],
             mf.at[pl.ds(384, 128), pl.ds(1536 + (d - 1) * 128, 128)], acts, base + 3 + d, me.by_y(d)) for d in (1, 2, 3)
    ]
    for c in kv_y:
        c.start()
    small_add(0, small_z)
    small_y = small_copies(1, ys_line, sems(3))
    for c in small_y:
        c.start()
    dq_over.wait()

    def query_grad(n, carry):
        cols = lanes(n * 256, 256)
        h2[0:256, cols] = (
            dot_plain(qt[lanes(core * 256, 256), :], h1[:, cols]) + dot_plain(hp[0, 256:512, 0:512], cfp[:, cols])
        ).astype(BF16)
        return carry

    lax.fori_loop(0, 8, query_grad, 0)
    query_sum.start()
    out_sum.start()
    one_sums[1].turn()
    unshake(4, zs_line)
    up_sum.send_z()
    for c in kv_y:
        c.wait()
    zy_at = lanes(me.z * 512 + me.y * 128, 128)
    mf[256:384, zy_at] = (
        mf[256:384, zy_at].astype(F32) + mf[384:512, 1536:1664].astype(F32) + mf[384:512, 1664:1792].astype(F32)
        + mf[384:512, 1792:1920].astype(F32)
    ).astype(BF16)
    pair = me.at(me.z, me.y, core, x + 1 - 2 * (x % 2))
    kv_pair = send(mf.at[pl.ds(256, 128), zy_at], mf.at[pl.ds(384, 128), pl.ds(1920, 128)], acts, base + 7, pair)
    kv_pair.start()
    small_add(1, small_y)
    small_x = small_copies(2, xs_line, sems(3))
    for c in small_x:
        c.start()
    for c in home_mixed:
        c.wait()

    def in_rows(h):
        rows = rows_of(h)
        mix[rows, :] = (dx1[rows, :] + one_sums[h].finish()).astype(BF16)

    in_rows(0)
    kv_pair.wait()
    mine = mf[pl.ds(pl.multiple_of(256 + (x % 2) * 64, 64), 64), zy_at].astype(F32)
    mine = mine + mf[pl.ds(pl.multiple_of(384 + (x % 2) * 64, 64), 64), 1920:2048].astype(F32)
    head_at = pl.ds(pl.multiple_of((2 * (x % 2) + x // 2) * 64, 64), 64)
    mf[head_at, zy_at] = mine.astype(BF16)
    kv_x = [send(mf.at[head_at, zy_at], mf.at[head_at, zy_at], acts, base + 7 + d, me.by_x(d)) for d in (1, 2, 3)]
    for c in kv_x:
        c.start()
    gate_sum.sum_z()
    shake(2, ys_line)
    small_add(2, small_x)
    small_c = small_copies(3, [partner], sems(1))
    for c in small_c:
        c.start()
    for c in kv_x:
        c.wait()
    block = mf.at[pl.ds(0, 256), zy_at]
    kv_y2 = [send(block, block, acts, base + 11 + d, me.by_y(d)) for d in (1, 2, 3)]
    for c in kv_y2:
        c.start()
    in_rows(1)
    home_in = homeward(mix, o_in, sems(4))
    for c in home_in:
        c.start()
    unshake(2, ys_line)
    gate_sum.send_y()
    for c in kv_y2:
        c.wait()
    block2 = mf.at[pl.ds(0, 256), z_at]
    kv_z2 = [send(block2, block2, acts, base + 15 + d, me.by_z(d)) for d in (1, 2, 3)]
    for c in kv_z2:
        c.start()
    small_add(3, small_c)
    small_out = pltpu.make_async_copy(small, o_small, lsem.at[8])
    small_out.start()
    down_sum.sum_z()
    shake(5, ys_line)
    out_sum.sum_z()
    query_sum.sum_z()
    shake(6, ys_line)
    up_sum.sum_z()
    unshake(5, ys_line)
    down_sum.send_y()
    unshake(6, ys_line)
    out_sum.send_y()
    query_sum.send_y()
    for c in kv_z2:
        c.wait()
    kv_last = send(mf.at[pl.ds(0, 256)], mf.at[pl.ds(256, 256)], acts, base + 20, partner)
    kv_last.start()
    flights = []

    def lay_out(home, first, k):
        for p, b in enumerate(ORIGINAL):
            spot = (k * 8 + p) % 4
            if len(flights) >= 4:
                flights[-4].wait()
            stage = x1.at[pl.ds((spot // 2) * 256, 256), pl.ds((spot % 2) * 256, 256)]
            x1[(spot // 2) * 256:(spot // 2 + 1) * 256, (spot % 2) * 256:(spot % 2 + 1) * 256] = (
                mf[first:first + 256, p * 256:(p + 1) * 256].astype(F32).T
            )
            copy = pltpu.make_async_copy(stage, home.at[pl.ds(b * 256, 256)], lsem.at[10 + spot])
            copy.start()
            flights.append(copy)

    lay_out(o_kv.at[core], 0, 0)
    gate_sum.sum_y()
    kv_last.wait()
    lay_out(o_kv.at[1 - core], 256, 1)
    down_sum.sum_y()
    out_sum.sum_y()
    query_sum.sum_y()
    for c in flights[-4:]:
        c.wait()
    for s in (gate_sum, up_sum, down_sum, out_sum, query_sum):
        s.finish()
    for c in home_in:
        c.wait()
    for h in (0, 1):
        one_sums[h].drain()
    small_out.wait()


ACTS = 270


def layer(tok, cot, wq, wo, wg, wu, wd, w_key, w_value, gain1, gain2, ids):
    ff = wg.shape[1]
    sds = jax.ShapeDtypeStruct
    outs = [
        sds((1024, 256), BF16), sds((1024, 256), BF16), sds((256, 128), BF16), sds((256, 128), BF16),
        sds((128, ff), BF16), sds((128, ff), BF16), sds((ff, 128), BF16), sds((2, 2048, 256), F32), sds((8, 1024), F32),
        sds((T, 2048), BF16),
    ]
    dma = pltpu.SemaphoreType.DMA
    vm = pl.BlockSpec(memory_space=pltpu.VMEM)
    wide = pltpu.VMEM((T, 2048), BF16)
    square = pltpu.VMEM((T, 512), BF16)
    inner = pltpu.VMEM((2, T, ff), BF16)
    row8 = pltpu.VMEM((8, CHUNK), F32)
    pair8 = pltpu.VMEM((2, 8, CHUNK), F32)
    return pl.pallas_call(
        layer_kernel, out_shape=outs, in_specs=[ANY] * 7 + [vm] * 5, out_specs=[ANY] * len(outs),
        scratch_shapes=[
            wide, wide, wide, wide, wide, wide,
            pltpu.VMEM((2048, 512), BF16), pltpu.VMEM((512, 2048), BF16),
            pltpu.VMEM((2, 2048, ff), BF16), pltpu.VMEM((2, 2048, ff), BF16), pltpu.VMEM((2, ff, 2048), BF16),
            square, square, square, pltpu.VMEM((8, 256, CHUNK), BF16),
            pltpu.VMEM((T, 512), F32), pltpu.VMEM((T, 512), F32),
            wide, pltpu.VMEM((2, 2, 256, 256), BF16), pltpu.VMEM((2, 2, 256, 512), BF16),
            pltpu.VMEM((512, CHUNK), F32), row8, row8, pair8, pair8,
            inner, inner, inner, pltpu.VMEM((3, T, ff), BF16), pltpu.VMEM((CHUNK, 2048), F32),
            pltpu.VMEM((T, 1), F32), pltpu.VMEM((T, 1), F32), square,
            pltpu.VMEM((2, 2048), F32), pltpu.VMEM((8, 512), F32), pltpu.VMEM((8, 1024), F32), pltpu.VMEM((4, 3, 8, 1024), F32),
            dma((ACTS,)), dma((ACTS,)), dma((5, 31)), dma((5, 31)), dma((14,)), pltpu.SemaphoreType.REGULAR((9,)),
        ],
        compiler_params=pltpu.CompilerParams(collective_id=0, has_side_effects=True, vmem_limit_bytes=64 << 20),
    )(tok, cot, wq, wo, wg, wu, wd, w_key, w_value, gain1, gain2, ids)


def from_device_order(v):
    return v.reshape((4, 2, 256) + v.shape[1:]).swapaxes(0, 1).reshape(v.shape)


def shards(tokens, segment_ids, norm_one, w_query, w_key, w_value, w_out, norm_two, w_gate, w_up, w_down, cotangent):
    mixed, input_grad, gq, go, gg, gu, gd, gkv, small, _ = layer(
        tokens, cotangent, w_query, w_out, w_gate, w_up, w_down, w_key, w_value,
        norm_one.reshape(1, 2048), norm_two.reshape(1, 2048), segment_ids.reshape(8, 16, 128),
    )
    key_total, value_total = gkv[0], gkv[1]
    rms = jnp.sqrt(jnp.sum(small[4:7, :512], 1) / (16384 * 2048))
    return (
        mixed, input_grad.astype(F32), gq.T.astype(F32), key_total, value_total, go.astype(F32), gg.astype(F32), gu.astype(F32),
        gd.astype(F32), from_device_order(small[0:2].reshape(2048)), from_device_order(small[2:4].reshape(2048)), rms,
    )


def solution(mesh):
    return jax.shard_map(
        shards,
        mesh=mesh,
        in_specs=(
            P("row", "col"), P(), P(), P("row", "col"), P(), P(), P("col", "row"), P(),
            P("row", "col"), P("row", "col"), P("col", "row"), P("row", "col"),
        ),
        out_specs=(
            P("row", "col"), P("row", "col"), P("row", "col"), P(), P(), P("col", "row"),
            P("row", "col"), P("row", "col"), P("col", "row"), P(), P(), P(),
        ),
        check_vma=False,
    )
```
